32 devices in a mesh: dp: 16 (over z, y, core), shard: 2 (over x).
Axes of the slice: x: 2, y: 2, z: 4, core: 2. Of those that a mesh axis runs over, the one named last changes fastest.
Arguments:
- hidden: bfloat16 [32, 4096, 256], P('shard', 'dp'), may hold values from -6 to 6
- cotangent: bfloat16 [32, 4096, 256], P('shard', 'dp'), may hold values from -6 to 6
- assign: int32 [32], replicated, may hold values from 0 to 15, as said below
- live_blocks: int32 [32], replicated, may hold values from 16 to 64, as said below
- tail_live: int32 [32, 64], replicated, may hold values from 0 to 1, as said below
- random_blocks: int32 [32, 4, 64, 3], P(('dp', 'shard')), may hold values from 2 to 63, as said below
- w_qkv: bfloat16 [256, 768], P('shard'), may hold values from -0.375 to 0.375
- w_out: bfloat16 [256, 256], P('shard'), may hold values from -3 to 3
- w_up: bfloat16 [256, 1024], P('shard'), may hold values from -0.375 to 0.375
- w_down: bfloat16 [1024, 256], P('shard'), may hold values from -0.1875 to 0.1875
- up_bias: bfloat16 [1024], P('shard'), may hold values from -2 to 2
- vectors: bfloat16 [8, 256], P('shard')
- state_qkv: float32 [3, 256, 768], P(None, 'shard')
- state_out: float32 [3, 256, 256], P(None, 'shard')
- state_up: float32 [3, 256, 1024], P(None, 'shard')
- state_down: float32 [3, 1024, 256], P(None, 'shard')
- state_ubias: float32 [3, 1024], P(None, 'shard')
- state_vec: float32 [3, 8, 256], P(None, 'shard')
Outputs:
- layer_out: bfloat16 [32, 4096, 256], P('shard', 'dp')
- input_grad: bfloat16 [32, 4096, 256], P('shard', 'dp')
- grad_qkv: float32 [256, 768], P('shard')
- grad_out: float32 [256, 256], P('shard')
- grad_up: float32 [256, 1024], P('shard')
- grad_down: float32 [1024, 256], P('shard')
- grad_ubias: float32 [1024], P('shard')
- grad_vec: float32 [8, 256], P('shard')
- new_masters: float32 [2, 394752], P('shard')
- new_firsts: float32 [2, 394752], P('shard')
- new_seconds: float32 [2, 394752], P('shard')
The draws below stay inside these ranges and needn't reach their ends.
Inputs may be any that keep to these rules, and one draw needn't show every extreme that they name: `assign`: among the slots g with (g) % 2 equal to one value, every number 0 to 15 appears once. `live_blocks`: among each shard row's 16 sequences one has 64 live blocks. `tail_live`: position 0 of each row is 1. `random_blocks`: for query block i the 3 entries of one slot and head are distinct, and none is 0, 1, i - 1, i or i + 1.
All inputs are finite; a program needn't handle non-finite values.
Results may differ from the reference program's by a relative error of at most 0.014.
Values may be sent and summed in bfloat16 or wider, within the bound.
No kernel may reach another device: no remote copies, remote signals or barrier semaphores. Data moves between devices by JAX's collectives and lax.ppermute only.
A program may use at most 256 MiB of HBM per device.

```python
import math
import jax
import jax.numpy as jnp
from jax import lax

D = 256
H = 4
HD = 64
FF = 1024
BLOCK = 64
RAND = 3
STEP = 1
LEN = 4096
SEQ_DEV = 1
NB = 64
SHARDS = 2
ROW_SEQS = 16
SEQS = 32
MIN_BLOCKS = 16


def draw_assign(key, part):
    row_list = []
    for group_index in range(SHARDS):
        row_list.append(jax.random.permutation(jax.random.fold_in(key, group_index), ROW_SEQS).astype(jnp.int32))
    assigned = jnp.stack(row_list).reshape(SHARDS, ROW_SEQS // SEQ_DEV, SEQ_DEV)
    return jnp.transpose(assigned, (1, 0, 2)).reshape(SEQS).astype(jnp.int32)


def draw_live_blocks(key, part):
    counts = jax.random.randint(jax.random.fold_in(key, 1), (SHARDS, ROW_SEQS), MIN_BLOCKS, NB + 1)
    longest = jax.random.randint(jax.random.fold_in(key, 2), (SHARDS, 1), 0, ROW_SEQS)
    counts = jnp.where(jnp.arange(ROW_SEQS)[None, :] == longest, NB, counts)
    return counts.reshape(SEQS).astype(jnp.int32)


def draw_tail_live(key, part):
    flags = jax.random.randint(key, (SEQS, BLOCK), 0, 2)
    return flags.at[:, 0].set(1).astype(jnp.int32)


def draw_random_blocks(key, part):
    ranks = jax.random.randint(key, (SEQS, H, NB, NB), 0, 1 << 20)
    row_ids = jnp.arange(NB)[:, None]
    candidate = jnp.arange(NB)[None, :]
    banned = (candidate < 2) | (jnp.abs(candidate - row_ids) <= 1)
    ranked = jnp.where(banned[None, None], -1, ranks * NB + candidate)
    return lax.top_k(ranked, RAND)[1].astype(jnp.int32)


def draw_vectors(key, part):
    noise = jax.random.normal(key, (8, D), jnp.float32)
    gain_rows = ((jnp.arange(8) == 3) | (jnp.arange(8) == 6))[:, None]
    return jnp.where(gain_rows, 1.0 + 0.1 * noise, 0.15 * noise).astype(jnp.bfloat16)


def make_state(key, shape, spread, factor):
    grad_scale = factor * math.sqrt(0.6 * SEQS * LEN)
    master = spread * jax.random.normal(jax.random.fold_in(key, 11), shape, jnp.float32)
    moment = grad_scale * jax.random.normal(jax.random.fold_in(key, 12), shape, jnp.float32)
    second = grad_scale * grad_scale * jnp.exp(jax.random.uniform(jax.random.fold_in(key, 13), shape, jnp.float32, -1.2, 1.2))
    return jnp.stack([master, moment, second]).astype(jnp.float32)


def draw_state_qkv(key, part):
    return make_state(key, (D, 3 * D), D ** (-0.5), 0.3)


def draw_state_out(key, part):
    return make_state(key, (D, D), max(1, D // 64) ** (-0.5), 0.1)


def draw_state_up(key, part):
    return make_state(key, (D, FF), D ** (-0.5), 0.2)


def draw_state_down(key, part):
    return make_state(key, (FF, D), FF ** (-0.5), 0.3)


def draw_state_ubias(key, part):
    return make_state(key, (FF,), 0.3, 0.2)


def draw_state_vec(key, part):
    stacked = make_state(key, (8, D), 0.15, 0.7)
    gain_rows = ((jnp.arange(8) == 3) | (jnp.arange(8) == 6))[:, None]
    master = jnp.where(gain_rows, 1.0 + stacked[0], stacked[0])
    return jnp.stack([master, stacked[1], stacked[2]]).astype(jnp.float32)


def block_levels(rng, shape, cuts, least, largest):
    gain, own = 1.0, jax.random.fold_in(rng, 6)
    for axis_at, parts in cuts:
        draws = jnp.exp(jax.random.uniform(jax.random.fold_in(own, axis_at), (parts,), jnp.float32, least / len(cuts), largest / len(cuts)))
        gain = gain * jnp.repeat(draws, shape[axis_at] // parts).reshape([-1 if axis == axis_at else 1 for axis in range(len(shape))])
    return gain


def normal_values(rng, dims, width, reach, shards=(), kind=jnp.bfloat16):
    entries = width * jax.random.normal(rng, dims, jnp.float32)
    if shards:
        entries = entries * block_levels(rng, dims, shards, -0.22, 0.18)
    return jnp.clip(entries, -reach, reach).astype(kind)


def setup_inputs(seed: int = 0) -> dict:
    splits = jax.random.split(jax.random.key(seed), 19)
    return {
        "hidden": normal_values(splits[0], (SEQS, LEN, D), 1.0, 6.0, ((0, 2), (1, 16))),
        "cotangent": normal_values(splits[1], (SEQS, LEN, D), 1.0, 6.0, ((0, 2), (1, 16))),
        "assign": draw_assign(jax.random.fold_in(splits[18], 71), 0),
        "live_blocks": draw_live_blocks(jax.random.fold_in(splits[18], 71), 0),
        "tail_live": draw_tail_live(jax.random.fold_in(splits[18], 71), 0),
        "random_blocks": draw_random_blocks(jax.random.fold_in(splits[18], 71), 0),
        "w_qkv": normal_values(splits[6], (D, 3 * D), D ** -0.5, 0.375, ((0, 2),)),
        "w_out": normal_values(splits[7], (D, D), (max(1, D // 64)) ** -0.5, 3.0, ((0, 2),)),
        "w_up": normal_values(splits[8], (D, FF), D ** -0.5, 0.375, ((0, 2),)),
        "w_down": normal_values(splits[9], (FF, D), FF ** -0.5, 0.1875, ((0, 2),)),
        "up_bias": normal_values(splits[10], (FF,), 0.3, 2.0, ((0, 2),)),
        "vectors": draw_vectors(jax.random.fold_in(splits[18], 71), 0),
        "state_qkv": draw_state_qkv(jax.random.fold_in(splits[18], 71), 0),
        "state_out": draw_state_out(jax.random.fold_in(splits[18], 71), 0),
        "state_up": draw_state_up(jax.random.fold_in(splits[18], 71), 0),
        "state_down": draw_state_down(jax.random.fold_in(splits[18], 71), 0),
        "state_ubias": draw_state_ubias(jax.random.fold_in(splits[18], 71), 0),
        "state_vec": draw_state_vec(jax.random.fold_in(splits[18], 71), 0),
    }


QUERY_SCALE = 0.125
NORM_EPSILON = 1e-12
LEARNING_RATE = 0.02
WEIGHT_DECAY = 0.01
ADAM_EPSILON = 1e-08
FIRST_BETA = 0.5
SECOND_BETA = 0.5
MASK_VALUE = -1e+30
ROOT_HALF = 0.7071067811865476

@jax.custom_vjp
def low(v):
    return lax.optimization_barrier(v.astype(jnp.bfloat16)).astype(jnp.float32)

@jax.custom_vjp
def low_back(v):
    return v

def low_keep(v):
    return (low(v), None)

def low_pass(kept, grad):
    return (grad,)

def back_keep(v):
    return (v, None)

def back_low(kept, grad):
    return (low(grad),)
low.defvjp(low_keep, low_pass)
low_back.defvjp(back_keep, back_low)

def matmul_high(left, right):
    return jnp.dot(left, right, precision=lax.Precision.HIGHEST, preferred_element_type=jnp.float32)

def gelu_exact(values):
    return 0.5 * values * (1.0 + jax.scipy.special.erf(values * ROOT_HALF))

def normalize(summed):
    center = summed - lax.optimization_barrier(jnp.mean(summed, axis=-1, keepdims=True))
    factor = lax.rsqrt(lax.optimization_barrier(jnp.mean(center * center, axis=-1, keepdims=True)) + NORM_EPSILON)
    return center * factor

def token_mask(live_count, tail_flags):
    block_ids = jnp.arange(NB, dtype=jnp.int32)[:, None]
    tail_open = (tail_flags == 1)[None, :]
    return (block_ids < live_count - 1) | (block_ids == live_count - 1) & tail_open

def tile_tables(first_block, tile_span, random_row, live_grid):
    block_ids = first_block + jnp.arange(tile_span, dtype=jnp.int32)
    nearby = jnp.stack([jnp.maximum(block_ids - 1, 0), block_ids, jnp.minimum(block_ids + 1, NB - 1), jnp.zeros_like(block_ids), jnp.ones_like(block_ids)], axis=1)
    drawn_ids = jnp.transpose(lax.dynamic_slice_in_dim(random_row, first_block, tile_span, 1), (1, 0, 2))
    key_index = jnp.concatenate([jnp.broadcast_to(nearby[:, None, :], (tile_span, H, 5)), drawn_ids], axis=2)
    always = jnp.ones_like(block_ids) > 0
    allowed = jnp.stack([block_ids >= 3, block_ids >= 2, (block_ids >= 1) & (block_ids + 1 < NB), always, always], axis=1)
    allowed = jnp.concatenate([allowed, jnp.broadcast_to(always[:, None], (tile_span, drawn_ids.shape[2]))], axis=1)
    key_live = live_grid[key_index]
    key_mask = allowed[:, None, None, :, None] & key_live[:, :, None, :, :]
    return (key_index, key_mask)

def soft_weights(scores, axes):
    row_peak = lax.optimization_barrier(jnp.max(scores, axis=axes, keepdims=True))
    raised = jnp.exp(scores - row_peak)
    return raised / lax.optimization_barrier(jnp.sum(raised, axis=axes, keepdims=True))

def attention(query_rows, key_rows, value_rows, live_grid, random_row):
    query_blocks = query_rows.reshape(NB // 8, 8, BLOCK, H, HD)
    key_heads = jnp.transpose(key_rows.reshape(NB, BLOCK, H, HD), (2, 0, 1, 3))
    value_heads = jnp.transpose(value_rows.reshape(NB, BLOCK, H, HD), (2, 0, 1, 3))
    head_pick = jnp.arange(H, dtype=jnp.int32)[None, :, None]

    @jax.checkpoint
    def tile_context(first_block, query_tile, key_heads, value_heads):
        key_index, key_mask = tile_tables(first_block, 8, random_row, live_grid)
        scores = jnp.einsum('tqhd,thskd->thqsk', query_tile, key_heads[head_pick, key_index], precision=lax.Precision.HIGHEST) * QUERY_SCALE
        scores = jnp.where(key_mask, low_back(scores), MASK_VALUE)
        prob_low = low(soft_weights(scores, (3, 4)))
        return jnp.einsum('thqsk,thskd->tqhd', prob_low, value_heads[head_pick, key_index], precision=lax.Precision.HIGHEST)
    firsts = jnp.arange(NB // 8, dtype=jnp.int32) * 8
    contexts = lax.map(lambda paired: tile_context(paired[0], paired[1], key_heads, value_heads), (firsts, query_blocks))
    glob_rows = 2 * BLOCK
    glob_query = query_rows[:glob_rows].reshape(glob_rows, H, HD)
    scores = jnp.einsum('qhd,khd->hqk', glob_query, key_rows.reshape(LEN, H, HD), precision=lax.Precision.HIGHEST) * QUERY_SCALE
    key_open = live_grid.reshape(LEN)[None, None, :]
    scores = jnp.where(key_open, low_back(scores), MASK_VALUE)
    prob_low = low(soft_weights(scores, (2,)))
    glob_context = jnp.einsum('hqk,khd->qhd', prob_low, value_rows.reshape(LEN, H, HD), precision=lax.Precision.HIGHEST).reshape(glob_rows, D)
    return jnp.concatenate([glob_context, contexts.reshape(LEN, D)[glob_rows:]], axis=0)

def layer(tokens, w_qkv, w_out, w_up, w_down, up_bias, vectors, live_grid, random_row):
    shift_qkv = jnp.concatenate([vectors[0], jnp.zeros_like(vectors[0]), vectors[1]])
    qkv = low(low_back(matmul_high(tokens, w_qkv) + shift_qkv))
    context = attention(qkv[:, :D], qkv[:, D:2 * D], qkv[:, 2 * D:], live_grid, random_row)
    context = low(low_back(context))
    attended = low_back(matmul_high(context, w_out) + vectors[2])
    first_out = normalize(tokens + attended) * vectors[3] + vectors[4]
    hidden_pre = low_back(matmul_high(low(first_out), w_up) + up_bias)
    activated = low(gelu_exact(hidden_pre))
    branch = low_back(matmul_high(activated, w_down) + vectors[5])
    live_rows = live_grid.reshape(LEN, 1).astype(jnp.float32)
    return (normalize(first_out + branch) * vectors[6] + vectors[7]) * live_rows

def adam_update(grad, state, decay, correct_one, correct_two):
    first_new = FIRST_BETA * state[1] + (1.0 - FIRST_BETA) * grad
    second_new = SECOND_BETA * state[2] + (1.0 - SECOND_BETA) * grad * grad
    direction = first_new / correct_one / (jnp.sqrt(second_new / correct_two) + ADAM_EPSILON)
    master_new = state[0] - LEARNING_RATE * (direction + decay * state[0])
    return (master_new, first_new, second_new)

def lay_out(pieces):
    return jnp.concatenate([piece.reshape(SHARDS, -1) for piece in pieces], axis=1)

def reference(hidden, cotangent, assign, live_blocks, tail_live, random_blocks, w_qkv, w_out, w_up, w_down, up_bias, vectors, state_qkv, state_out, state_up, state_down, state_ubias, state_vec):
    weights = tuple((weight_arg.astype(jnp.float32) for weight_arg in (w_qkv, w_out, w_up, w_down, up_bias, vectors)))
    slot_ids = jnp.arange(SEQS, dtype=jnp.int32)
    sequence_of_slot = slot_ids // SEQ_DEV % SHARDS * ROW_SEQS + assign

    def one_slot(totals, slot_id):
        seq_id = sequence_of_slot[slot_id]
        tokens = lax.dynamic_index_in_dim(hidden, seq_id, 0, keepdims=False).astype(jnp.float32)
        cot_rows = lax.dynamic_index_in_dim(cotangent, seq_id, 0, keepdims=False).astype(jnp.float32)
        live_grid = token_mask(live_blocks[seq_id], tail_live[seq_id])
        random_row = lax.dynamic_index_in_dim(random_blocks, slot_id, 0, keepdims=False)

        def apply_layer(token_arg, *param_args):
            return layer(token_arg, *param_args, live_grid, random_row)
        result, pullback = jax.vjp(apply_layer, tokens, *weights)
        grads = pullback(cot_rows)
        totals = tuple((left + right for left, right in zip(totals, grads[1:])))
        return (totals, (result.astype(jnp.bfloat16), grads[0].astype(jnp.bfloat16)))
    empty_grads = tuple((jnp.zeros_like(weight_arg) for weight_arg in weights))
    totals, (outs_slot, grads_slot) = lax.scan(one_slot, empty_grads, slot_ids)
    inverse = jnp.zeros((SEQS,), jnp.int32).at[sequence_of_slot].set(slot_ids)
    layer_out = outs_slot[inverse]
    input_grad = grads_slot[inverse]
    correct_one = 1.0 - FIRST_BETA ** STEP
    correct_two = 1.0 - SECOND_BETA ** STEP
    states = (state_qkv, state_out, state_up, state_down, state_ubias, state_vec)
    decays = (WEIGHT_DECAY, WEIGHT_DECAY, WEIGHT_DECAY, WEIGHT_DECAY, 0.0, 0.0)
    updated = [adam_update(grad, state, decay, correct_one, correct_two) for grad, state, decay in zip(totals, states, decays)]
    new_masters = lay_out([entry[0] for entry in updated])
    new_firsts = lay_out([entry[1] for entry in updated])
    new_seconds = lay_out([entry[2] for entry in updated])
    return (layer_out, input_grad, totals[0], totals[1], totals[2], totals[3], totals[4], totals[5], new_masters, new_firsts, new_seconds)
```

```python
import functools

import jax
import jax.numpy as jnp
from jax import lax
from jax.experimental import pallas as pl
from jax.experimental.pallas import tpu as pltpu
from jax.sharding import PartitionSpec as P

STEP = 1
QUERY_SCALE = 0.125
NORM_EPSILON = 1e-12
LEARNING_RATE = 0.02
WEIGHT_DECAY = 0.01
ADAM_EPSILON = 1e-08
FIRST_BETA = 0.5
SECOND_BETA = 0.5
MASK_VALUE = -1e30
NORMAL_PEAK = 0.3989422804014327

LOW = jnp.bfloat16
F32 = jnp.float32
VMEM_LIMIT = 60 * 1024 * 1024

BLOCK = 64
HALF = 128


def dot_nn(a, b):
    return lax.dot_general(a, b, (((1,), (0,)), ((), ())), preferred_element_type=F32)


def dot_nt(a, b):
    return lax.dot_general(a, b, (((1,), (1,)), ((), ())), preferred_element_type=F32)


def dot_tn(a, b):
    return lax.dot_general(a, b, (((0,), (0,)), ((), ())), preferred_element_type=F32)


def first_half(rows):
    return lax.broadcasted_iota(jnp.int32, (rows, HALF), 1) < BLOCK


def spread_heads(rows, picks):
    return jnp.concatenate([rows, rows, rows, rows], axis=0) * picks


def pick_heads(wide):
    low = first_half(BLOCK)
    left = jnp.where(low, wide[0:64, 0:HALF], wide[64:128, 0:HALF])
    right = jnp.where(low, wide[128:192, HALF:], wide[192:256, HALF:])
    return jnp.concatenate([left, right], axis=1)


def head_picks():
    row = lax.broadcasted_iota(jnp.int32, (256, 256), 0) // BLOCK
    col = lax.broadcasted_iota(jnp.int32, (256, 256), 1) // BLOCK
    return jnp.where(row == col, 1.0, 0.0).astype(LOW)


def gather_slot(ref, chosen, tile):
    a, b = chosen[2 * tile], chosen[2 * tile + 1]
    cols = pl.ds(tile * HALF, HALF)
    left = ref[pl.ds(pl.multiple_of(a * BLOCK, BLOCK), BLOCK), cols]
    right = ref[pl.ds(pl.multiple_of(b * BLOCK, BLOCK), BLOCK), cols]
    return jnp.where(first_half(BLOCK), left, right)


class Unit:
    def __init__(self, i, live, drawn, blocks):
        last = live - 1

        def state(b):
            return (b >= last).astype(jnp.int32) + (b > last).astype(jnp.int32)

        after = jnp.minimum(i + 1, blocks - 1)
        self.near = [i - 1, i, after]
        self.near_state = [
            jnp.where(i >= 3, state(i - 1), 2),
            state(i),
            jnp.where(i + 1 < blocks, state(after), 2),
        ]
        self.fixed_state = [state(0 * i), state(0 * i + 1)]
        self.chosen = [
            [drawn[(h * blocks + i) * 3 + s] for h in range(4)] for s in range(3)
        ]
        self.chosen_state = [[state(b) for b in row] for row in self.chosen]

    def gather(self, ref, out):
        for n, b in enumerate(self.near):
            out[pl.ds(128 + 64 * n, 64), :] = ref[pl.ds(pl.multiple_of(b * BLOCK, BLOCK), BLOCK), :]
        for s in range(3):
            for t in range(2):
                out[pl.ds(320 + 64 * s, 64), pl.ds(t * HALF, HALF)] = gather_slot(
                    ref, self.chosen[s], t
                )

    def bias(self, table, slots):
        rows = []
        for n in slots:
            if n < 5:
                one = table[(self.fixed_state + self.near_state)[n]]
                rows.append(jnp.concatenate([one, one], axis=1))
            else:
                st = self.chosen_state[n - 5]
                low = first_half(BLOCK)
                rows.append(
                    jnp.concatenate(
                        [
                            jnp.where(low, table[st[0]], table[st[1]]),
                            jnp.where(low, table[st[2]], table[st[3]]),
                        ],
                        axis=1,
                    )
                )
        return jnp.concatenate(rows, axis=0)


def chunk_bias(table, live, first, count):
    last = live - 1
    rows = []
    for n in range(count):
        b = first + n
        st = (b >= last).astype(jnp.int32) + (b > last).astype(jnp.int32)
        one = table[st]
        rows.append(jnp.concatenate([one, one], axis=1))
    return jnp.concatenate(rows, axis=0)


def forward_kernel(scal, drawn, table, x, w, shift, q_o, k_o, v_o, ctx_o, lse_o, picks, kg, vg, sg):
    length = x.shape[0]
    blocks = length // BLOCK
    live = scal[0]
    picks[...] = head_picks()

    def project(c, _):
        rows = pl.ds(pl.multiple_of(c * 512, 512), 512)
        out = (dot_nn(x[rows, :], w[...]) + shift[...]).astype(LOW)
        q_o[rows, :] = out[:, 0:256]
        k_o[rows, :] = out[:, 256:512]
        v_o[rows, :] = out[:, 512:768]
        return 0

    lax.fori_loop(0, length // 512, project, 0)
    for u in range(2):
        kg[u, 0:128, :] = k_o[0:128, :]
        vg[u, 0:128, :] = v_o[0:128, :]

    def sparse(i, u):
        unit = Unit(i, live, drawn, blocks)
        rows = pl.ds(pl.multiple_of(i * BLOCK, BLOCK), BLOCK)
        bd = spread_heads(q_o[rows, :] * jnp.asarray(QUERY_SCALE, LOW), picks[...])
        unit.gather(k_o, kg.at[u])
        unit.gather(v_o, vg.at[u])
        s = dot_nt(kg[u], bd) + unit.bias(table, range(8))
        m = jnp.max(s, axis=0, keepdims=True)
        e = jnp.exp(s - m)
        total = jnp.sum(e, axis=0, keepdims=True)
        p = (e * (1.0 / total)).astype(LOW)
        o = dot_tn(p, vg[u])
        ctx_o[rows, :] = pick_heads(o).astype(LOW)
        lse_o[pl.ds(i, 1), :] = m + jnp.log(total)

    def pair(j, _):
        sparse(2 + 2 * j, 0)
        sparse(3 + 2 * j, 1)
        return 0

    lax.fori_loop(0, blocks // 2 - 1, pair, 0)

    for g in range(2):
        bd = spread_heads(q_o[g * 64 : g * 64 + 64, :] * jnp.asarray(QUERY_SCALE, LOW), picks[...])

        def score(c, m):
            rows = pl.ds(pl.multiple_of(c * 512, 512), 512)
            s = dot_nt(k_o[rows, :], bd) + chunk_bias(table, live, c * 8, 8)
            sg[rows, :] = s
            return jnp.maximum(m, jnp.max(s, axis=0, keepdims=True))

        m = lax.fori_loop(0, length // 512, score, jnp.full((1, 256), MASK_VALUE, F32))

        def raise_(c, total):
            rows = pl.ds(pl.multiple_of(c * 512, 512), 512)
            e = jnp.exp(sg[rows, :] - m)
            sg[rows, :] = e
            return total + jnp.sum(e, axis=0, keepdims=True)

        total = lax.fori_loop(0, length // 512, raise_, jnp.zeros((1, 256), F32))
        scale = 1.0 / total

        def mix(c, o):
            rows = pl.ds(pl.multiple_of(c * 512, 512), 512)
            p = (sg[rows, :] * scale).astype(LOW)
            return o + dot_tn(p, v_o[rows, :])

        o = lax.fori_loop(0, length // 512, mix, jnp.zeros((256, 256), F32))
        ctx_o[g * 64 : g * 64 + 64, :] = pick_heads(o).astype(LOW)
        lse_o[g : g + 1, :] = m + jnp.log(total)


def vmem():
    return pl.BlockSpec(memory_space=pltpu.VMEM)


def smem():
    return pl.BlockSpec(memory_space=pltpu.SMEM)


def forward_attention(scal, drawn, table, x, w, shift):
    length = x.shape[0]
    blocks = length // BLOCK
    rows = jax.ShapeDtypeStruct((length, 256), LOW)
    return pl.pallas_call(
        forward_kernel,
        out_shape=(rows, rows, rows, rows, jax.ShapeDtypeStruct((blocks, 256), F32)),
        in_specs=[smem(), smem(), vmem(), vmem(), vmem(), vmem()],
        out_specs=[vmem()] * 5,
        scratch_shapes=[
            pltpu.VMEM((256, 256), LOW),
            pltpu.VMEM((2, 512, 256), LOW),
            pltpu.VMEM((2, 512, 256), LOW),
            pltpu.VMEM((length, 256), F32),
        ],
        compiler_params=pltpu.CompilerParams(vmem_limit_bytes=VMEM_LIMIT),
        cost_estimate=pl.CostEstimate(flops=16_000_000_000, bytes_accessed=12_000_000, transcendentals=10_000_000),
        name="attend_forward",
    )(scal, drawn, table, x, w, shift)


def normalize(summed):
    center = summed - jnp.mean(summed, axis=-1, keepdims=True)
    factor = lax.rsqrt(jnp.mean(center * center, axis=-1, keepdims=True) + NORM_EPSILON)
    return (center * factor, factor)


def normalize_back(grad_normed, normed, factor):
    return factor * (
        grad_normed
        - jnp.mean(grad_normed, axis=-1, keepdims=True)
        - normed * jnp.mean(grad_normed * normed, axis=-1, keepdims=True)
    )


ERF_P = 0.3275911 * 0.7071067811865476
ERF_A = (0.254829592, -0.284496736, 1.421413741, -1.453152027, 1.061405429)


def gelu_parts(v):
    bell = jnp.exp(-0.5 * v * v)
    t = 1.0 / (1.0 + ERF_P * jnp.abs(v))
    a1, a2, a3, a4, a5 = (0.5 * a for a in ERF_A)
    tail = ((((a5 * t + a4) * t + a3) * t + a2) * t + a1) * t * bell
    cumulative = jnp.where(v < 0.0, tail, 1.0 - tail)
    return v * cumulative, cumulative + v * (NORMAL_PEAK * bell)


def middle_kernel(
    scal, table, x, cot, ctx, w_out, w_up, w_down, up_shift, vec,
    out_o, gz1_o, gctx_o, delta_o, gdown_o, gup_o, gout_o, gub_o, gvec_o, act, slope,
):
    step = pl.program_id(0)
    rows = x.shape[0]
    last = scal[0] - 1

    @pl.when(step == 0)
    def _():
        for ref in (gdown_o, gup_o, gout_o, gub_o, gvec_o):
            ref[...] = jnp.zeros_like(ref)

    marks = []
    for n in range(rows // BLOCK):
        b = step * (rows // BLOCK) + n
        st = (b >= last).astype(jnp.int32) + (b > last).astype(jnp.int32)
        one = table[st]
        marks.append(jnp.concatenate([one, one], axis=1))
    open_ = jnp.concatenate(marks, axis=0) == 0.0

    def row(n):
        return vec[n : n + 1, :]

    ctx_v = ctx[...]
    attended = dot_nn(ctx_v, w_out[...]) + row(2)
    normed_one, factor_one = normalize(x[...].astype(F32) + attended)
    first_out = normed_one * row(3) + row(4)
    first_low = first_out.astype(LOW)
    branch = row(5)
    for c in range(0, 1024, 256):
        pre = dot_nn(first_low, w_up[:, c : c + 256]) + up_shift[:, c : c + 256]
        a, s = gelu_parts(pre)
        act[:, c : c + 256] = a.astype(LOW)
        slope[:, c : c + 256] = s
    branch = dot_nn(act[...], w_down[...]) + row(5)
    normed_two, factor_two = normalize(first_out + branch)
    out_o[...] = jnp.where(open_, normed_two * row(6) + row(7), 0.0).astype(LOW)
    grad_y = jnp.where(open_, cot[...].astype(F32), 0.0)
    grad_z2 = normalize_back(grad_y * row(6), normed_two, factor_two)
    grad_branch = grad_z2.astype(LOW)
    gdown_o[...] += dot_tn(act[...], grad_branch)
    back = jnp.zeros((rows, 256), F32)
    for c in range(0, 1024, 256):
        grad_act = dot_nt(grad_branch, w_down[c : c + 256, :])
        grad_pre = (grad_act * slope[:, c : c + 256]).astype(LOW)
        act[:, c : c + 256] = grad_pre
        gub_o[:, c : c + 256] += jnp.sum(grad_pre.astype(F32), axis=0, keepdims=True)
    gup_o[...] += dot_tn(first_low, act[...])
    grad_first = grad_z2 + dot_nt(act[...], w_up[...])
    grad_z1 = normalize_back(grad_first * row(3), normed_one, factor_one)
    gz1_o[...] = grad_z1
    grad_attended = grad_z1.astype(LOW)
    gout_o[...] += dot_tn(ctx_v, grad_attended)
    grad_context = dot_nt(grad_attended, w_out[...]).astype(LOW)
    gctx_o[...] = grad_context

    def add(n, values):
        gvec_o[n : n + 1, :] += jnp.sum(values, axis=0, keepdims=True)

    add(2, grad_attended.astype(F32))
    add(3, grad_first * normed_one)
    add(4, grad_first)
    add(5, grad_branch.astype(F32))
    add(6, grad_y * normed_two)
    add(7, grad_y)
    both = ctx_v.astype(F32) * grad_context.astype(F32)
    upper = both.astype(LOW)
    lower = (both - upper.astype(F32)).astype(LOW)
    group = lax.broadcasted_iota(jnp.int32, (8, 256), 1) // BLOCK
    ones = jnp.where(group == lax.broadcasted_iota(jnp.int32, (8, 256), 0), 1.0, 0.0).astype(LOW)
    sums = dot_nt(ones, upper) + dot_nt(ones, lower)
    for n in range(rows // BLOCK):
        part = sums[0:4, n * BLOCK : (n + 1) * BLOCK]
        delta_o[n : n + 1, :] = jnp.concatenate([part[h : h + 1, :] for h in range(4)], axis=1)


def middle(scal, table, x, cot, ctx, w_out, w_up, w_down, up_shift, vec):
    length = x.shape[0]
    rows = 512
    wide = pl.BlockSpec((rows, 256), lambda i, s: (i, 0))

    def whole(*shape):
        return pl.BlockSpec(shape, lambda i, s: (0,) * len(shape))

    shape = jax.ShapeDtypeStruct
    return pl.pallas_call(
        middle_kernel,
        grid_spec=pltpu.PrefetchScalarGridSpec(
            num_scalar_prefetch=1,
            grid=(length // rows,),
            in_specs=[
                whole(3, 64, 128), wide, wide, wide, whole(256, 256), whole(256, 1024), whole(1024, 256),
                whole(1, 1024), whole(8, 256),
            ],
            out_specs=[
                wide, wide, wide, pl.BlockSpec((rows // BLOCK, 256), lambda i, s: (i, 0)),
                whole(1024, 256), whole(256, 1024), whole(256, 256), whole(1, 1024), whole(8, 256),
            ],
            scratch_shapes=[pltpu.VMEM((rows, 1024), LOW), pltpu.VMEM((rows, 1024), F32)],
        ),
        out_shape=(
            shape((length, 256), LOW), shape((length, 256), F32), shape((length, 256), LOW),
            shape((length // BLOCK, 256), F32), shape((1024, 256), F32), shape((256, 1024), F32),
            shape((256, 256), F32), shape((1, 1024), F32), shape((8, 256), F32),
        ),
        compiler_params=pltpu.CompilerParams(vmem_limit_bytes=VMEM_LIMIT),
        cost_estimate=pl.CostEstimate(flops=16_000_000_000, bytes_accessed=20_000_000, transcendentals=10_000_000),
        name="middle",
    )(scal, table, x, cot, ctx, w_out, w_up, w_down, up_shift, vec)


def backward_kernel(
    scal, drawn, table, q, k, v, gctx, lse, delta, gz1, x, w,
    gin_o, gw_o, gs_o, picks, kg, vg, dq, dk, dv,
):
    length = x.shape[0]
    blocks = length // BLOCK
    live = scal[0]
    picks[...] = head_picks()
    dk[...] = jnp.zeros_like(dk)
    dv[...] = jnp.zeros_like(dv)
    for u in range(2):
        kg[u, 0:128, :] = k[0:128, :]
        vg[u, 0:128, :] = v[0:128, :]

    def terms(kh, vh, bias, bdq, bdo, lse_row, delta_row):
        p = jnp.exp(dot_nt(kh, bdq) + bias - lse_row)
        dvh = dot_nn(p.astype(LOW), bdo)
        ds = (p * (dot_nt(vh, bdo) - delta_row)).astype(LOW)
        return dvh, dot_nn(ds, bdq), dot_tn(ds, kh)

    def spread(i):
        rows = pl.ds(pl.multiple_of(i * BLOCK, BLOCK), BLOCK)
        bdq = spread_heads(q[rows, :] * jnp.asarray(QUERY_SCALE, LOW), picks[...])
        bdo = spread_heads(gctx[rows, :], picks[...])
        return rows, bdq, bdo

    def sparse(i, u):
        unit = Unit(i, live, drawn, blocks)
        rows, bdq, bdo = spread(i)
        unit.gather(k, kg.at[u])
        unit.gather(v, vg.at[u])
        lse_row, delta_row = lse[pl.ds(i, 1), :], delta[pl.ds(i, 1), :]
        low = first_half(BLOCK)
        grad_q = None
        for half in range(2):
            part = slice(half * 256, half * 256 + 256)
            dvh, dkh, dqh = terms(
                kg[u, part, :], vg[u, part, :], unit.bias(table, range(4 * half, 4 * half + 4)), bdq, bdo, lse_row, delta_row
            )
            grad_q = dqh if grad_q is None else grad_q + dqh
            for acc, terms_ in ((dk, dkh), (dv, dvh)):
                if half == 0:
                    acc[0:128, :] += terms_[0:128, :]
                for n in range(4):
                    slot = 4 * half + n
                    one = terms_[n * 64 : n * 64 + 64, :]
                    if slot < 2:
                        continue
                    if slot < 5:
                        at = pl.ds(pl.multiple_of(unit.near[slot - 2] * BLOCK, BLOCK), BLOCK)
                        acc[at, :] += one
                    else:
                        for h in range(4):
                            t = h // 2
                            at = pl.ds(pl.multiple_of(unit.chosen[slot - 5][h] * BLOCK, BLOCK), BLOCK)
                            cols = pl.ds(t * HALF, HALF)
                            mine = low if h % 2 == 0 else jnp.logical_not(low)
                            acc[at, cols] += jnp.where(mine, one[:, t * HALF : t * HALF + HALF], 0.0)
        dq[rows, :] = (pick_heads(grad_q) * QUERY_SCALE).astype(LOW)

    def pair(j, _):
        sparse(2 + 2 * j, 0)
        sparse(3 + 2 * j, 1)
        return 0

    lax.fori_loop(0, blocks // 2 - 1, pair, 0)

    for g in range(2):
        _, bdq, bdo = spread(g)
        lse_row, delta_row = lse[g : g + 1, :], delta[g : g + 1, :]

        def chunk(c, grad_q):
            at = pl.ds(pl.multiple_of(c * 256, 256), 256)
            dvh, dkh, dqh = terms(
                k[at, :], v[at, :], chunk_bias(table, live, c * 4, 4), bdq, bdo, lse_row, delta_row
            )
            dk[at, :] += dkh
            dv[at, :] += dvh
            return grad_q + dqh

        grad_q = lax.fori_loop(0, length // 256, chunk, jnp.zeros((256, 256), F32))
        dq[g * 64 : g * 64 + 64, :] = (pick_heads(grad_q) * QUERY_SCALE).astype(LOW)

    gw_o[...] = jnp.zeros_like(gw_o)

    def finish(c, shifts):
        rows = pl.ds(pl.multiple_of(c * 512, 512), 512)
        dqkv = jnp.concatenate([dq[rows, :], dk[rows, :].astype(LOW), dv[rows, :].astype(LOW)], axis=1)
        gin_o[rows, :] = (gz1[rows, :] + dot_nt(dqkv, w[...])).astype(LOW)
        gw_o[...] += dot_tn(x[rows, :], dqkv)
        return shifts + jnp.sum(dqkv.astype(F32), axis=0, keepdims=True)

    gs_o[...] = lax.fori_loop(0, length // 512, finish, jnp.zeros((1, 768), F32))


def backward_attention(scal, drawn, table, q, k, v, gctx, lse, delta, gz1, x, w):
    length = x.shape[0]
    shape = jax.ShapeDtypeStruct
    return pl.pallas_call(
        backward_kernel,
        out_shape=(shape((length, 256), LOW), shape((256, 768), F32), shape((1, 768), F32)),
        in_specs=[smem(), smem()] + [vmem()] * 10,
        out_specs=[vmem()] * 3,
        scratch_shapes=[
            pltpu.VMEM((256, 256), LOW),
            pltpu.VMEM((2, 512, 256), LOW),
            pltpu.VMEM((2, 512, 256), LOW),
            pltpu.VMEM((length, 256), LOW),
            pltpu.VMEM((length, 256), F32),
            pltpu.VMEM((length, 256), F32),
        ],
        compiler_params=pltpu.CompilerParams(vmem_limit_bytes=VMEM_LIMIT),
        cost_estimate=pl.CostEstimate(flops=40_000_000_000, bytes_accessed=20_000_000, transcendentals=10_000_000),
        name="attend_backward",
    )(scal, drawn, table, q, k, v, gctx, lse, delta, gz1, x, w)


def bias_table(tail):
    column = jnp.stack([jnp.zeros_like(tail, F32), jnp.where(tail == 1, 0.0, MASK_VALUE), jnp.full(tail.shape, MASK_VALUE, F32)])
    return jnp.broadcast_to(column[:, :, None], (3, BLOCK, HALF))


def reorder_kernel(scatter, order, src, dst, sems):
    count = src.shape[0]
    copies = []
    for j in range(count):
        one = order[j]
        if scatter:
            copies.append(pltpu.make_async_copy(src.at[j], dst.at[one], sems.at[j]))
        else:
            copies.append(pltpu.make_async_copy(src.at[one], dst.at[j], sems.at[j]))
        copies[-1].start()
    for copy in copies:
        copy.wait()


def reorder(order, src, scatter):
    return pl.pallas_call(
        functools.partial(reorder_kernel, scatter),
        out_shape=jax.ShapeDtypeStruct(src.shape, src.dtype),
        in_specs=[smem(), pl.BlockSpec(memory_space=pl.ANY)],
        out_specs=pl.BlockSpec(memory_space=pl.ANY),
        scratch_shapes=[pltpu.SemaphoreType.DMA((src.shape[0],))],
        cost_estimate=pl.CostEstimate(flops=0, bytes_accessed=2 * src.size * 2, transcendentals=0),
        name="reorder",
    )(order, src)


def exchange_weights(shard_index, parts):
    w_qkv, w_out, w_up, w_down, up_bias, vectors = parts
    rows = w_qkv.shape[0]
    down = w_down.reshape(4, rows, -1)
    pack = jnp.concatenate([w_qkv, w_out, w_up] + [down[n] for n in range(4)], axis=1)
    small = jnp.concatenate([up_bias.reshape(-1, 256), vectors], axis=0)
    swap = [(0, 1), (1, 0)]
    other, other_small = lax.ppermute(pack, "shard", swap), lax.ppermute(small, "shard", swap)
    first = shard_index == 0

    def join(own, got):
        return jnp.stack([jnp.where(first, own, got), jnp.where(first, got, own)])

    both, both_small = join(pack, other), join(small, other_small)

    def cols(lo, hi):
        return both[:, :, lo:hi].reshape(2 * rows, hi - lo)

    full_down = jnp.transpose(both[:, :, 2048:].reshape(2, rows, 4, 256), (0, 2, 1, 3)).reshape(-1, 256)
    full_bias = both_small[:, :2].reshape(-1)
    full_vec = both_small[:, 2:].reshape(8, 256)
    return cols(0, 768), cols(768, 1024), cols(1024, 2048), full_down, full_bias, full_vec


def sum_over_devices(pack):
    shards, rows, columns = pack.shape
    count = lax.axis_size("dp")
    pieces = jnp.transpose(pack.reshape(shards, count, rows // count, columns), (1, 0, 2, 3))
    pieces = pieces.reshape(count * shards, rows // count, columns)
    got = lax.all_to_all(pieces, ("dp", "shard"), split_axis=0, concat_axis=0, tiled=True)
    mine = jnp.sum(got.astype(F32), axis=0)
    return lax.all_gather(mine, "dp", axis=0, tiled=True)


def adam_update(grad, state, decay):
    correct_one = 1.0 - FIRST_BETA**STEP
    correct_two = 1.0 - SECOND_BETA**STEP
    first_new = FIRST_BETA * state[1] + (1.0 - FIRST_BETA) * grad
    second_new = SECOND_BETA * state[2] + (1.0 - SECOND_BETA) * grad * grad
    direction = first_new / correct_one / (jnp.sqrt(second_new / correct_two) + ADAM_EPSILON)
    master_new = state[0] - LEARNING_RATE * (direction + decay * state[0])
    return (master_new, first_new, second_new)


def on_device(
    hidden, cotangent, assign, live_blocks, tail_live, random_blocks, w_qkv, w_out, w_up, w_down, up_bias, vectors,
    state_qkv, state_out, state_up, state_down, state_ubias, state_vec,
):
    shard_count = lax.axis_size("shard")
    shard_index = lax.axis_index("shard")
    data_index = lax.axis_index("dp")
    row_seqs, rows_here, width = hidden.shape
    length = row_seqs * rows_here
    order = lax.dynamic_index_in_dim(assign.reshape(row_seqs, shard_count), shard_index, 1, keepdims=False)
    own = shard_index * row_seqs + lax.dynamic_index_in_dim(order, data_index, 0, keepdims=False)
    live = lax.dynamic_slice_in_dim(live_blocks, own, 1)
    tail = lax.dynamic_index_in_dim(tail_live, own, 0, keepdims=False)

    def to_slot(rows):
        return lax.all_to_all(rows, "dp", split_axis=0, concat_axis=0, tiled=True)

    x = to_slot(reorder(order, hidden, False)).reshape(length, width)
    cot = to_slot(reorder(order, cotangent, False)).reshape(length, width)
    w_qkv, w_out, w_up, w_down, up_bias, vectors = exchange_weights(
        shard_index, (w_qkv, w_out, w_up, w_down, up_bias, vectors)
    )
    vec = vectors.astype(F32)
    shift = jnp.concatenate([vec[0], jnp.zeros_like(vec[0]), vec[1]])[None]
    table = bias_table(tail)
    drawn = random_blocks.reshape(-1)
    q, k, v, ctx, lse = forward_attention(live, drawn, table, x, w_qkv, shift)
    out, gz1, gctx, delta, gdown, gup, gout, gub, gvec = middle(
        live, table, x, cot, ctx, w_out, w_up, w_down, up_bias.astype(F32)[None], vec
    )

    def from_slot(rows):
        back = lax.all_to_all(
            rows.reshape(row_seqs, rows_here, width), "dp", split_axis=0, concat_axis=0, tiled=True
        )
        return reorder(order, back, True)

    layer_out = from_slot(out)
    half = gup.shape[0] // 2

    def extra(*pieces):
        block = jnp.concatenate([piece.reshape(shard_count, -1, HALF) for piece in pieces], axis=1)
        return jnp.pad(block, ((0, 0), (0, half - block.shape[1]), (0, 0)))

    down = jnp.transpose(gdown.reshape(2, 4, half, 256), (0, 2, 1, 3)).reshape(2, half, 1024)
    early = jnp.concatenate(
        [gup.reshape(2, half, 1024), gout.reshape(2, half, 256), down, extra(gub, gvec)], axis=2
    ).astype(LOW)
    early = sum_over_devices(early)
    gin, gw, gs = backward_attention(live, drawn, table, q, k, v, gctx, lse, delta, gz1, x, w_qkv)
    input_grad = from_slot(gin)
    ends = jnp.concatenate([gs[:, :256], gs[:, 512:], jnp.zeros((6, 256), F32)])
    late = jnp.concatenate([gw.reshape(2, half, 768), extra(ends)], axis=2).astype(LOW)
    late = sum_over_devices(late)
    grad_qkv = late[:, :768]
    grad_up = early[:, :1024]
    grad_out = early[:, 1024:1280]
    grad_down = jnp.concatenate([early[:, 1280 + 256 * n : 1536 + 256 * n] for n in range(4)], axis=0)
    grad_ubias = early[0:4, 2304:].reshape(-1)
    grad_vec = early[4:12, 2304:].reshape(4, 256) + late[0:8, 768:].reshape(4, 256)
    grads = (grad_qkv, grad_out, grad_up, grad_down, grad_ubias, grad_vec)
    states = (state_qkv, state_out, state_up, state_down, state_ubias, state_vec)
    decays = (WEIGHT_DECAY, WEIGHT_DECAY, WEIGHT_DECAY, WEIGHT_DECAY, 0.0, 0.0)
    updated = [adam_update(*group) for group in zip(grads, states, decays)]
    rows = [jnp.concatenate([entry[n].reshape(1, -1) for entry in updated], axis=1) for n in range(3)]
    return (layer_out, input_grad) + grads + tuple(rows)


def solution(mesh):
    placed = (
        P("shard", "dp", None), P("shard", "dp", None), P(), P(), P(), P(("dp", "shard"), None, None, None),
        P("shard", None), P("shard", None), P("shard", None), P("shard", None), P("shard"), P("shard", None),
        P(None, "shard", None), P(None, "shard", None), P(None, "shard", None), P(None, "shard", None),
        P(None, "shard"), P(None, "shard", None),
    )
    return jax.shard_map(
        on_device,
        mesh=mesh,
        in_specs=placed,
        out_specs=(
            P("shard", "dp", None), P("shard", "dp", None), P("shard", None), P("shard", None), P("shard", None),
            P("shard", None), P("shard"), P("shard", None), P("shard", None), P("shard", None), P("shard", None),
        ),
        check_vma=False,
    )
```

```python
import functools

import jax
import jax.numpy as jnp
from jax import lax
from jax.experimental import pallas as pl
from jax.experimental.pallas import tpu as pltpu
from jax.sharding import PartitionSpec as P

STEP = 1
QUERY_SCALE = 0.125
NORM_EPSILON = 1e-12
LEARNING_RATE = 0.02
WEIGHT_DECAY = 0.01
ADAM_EPSILON = 1e-08
FIRST_BETA = 0.5
SECOND_BETA = 0.5
MASK_VALUE = -1e30
NORMAL_PEAK = 0.3989422804014327

LOW = jnp.bfloat16
F32 = jnp.float32
VMEM_LIMIT = 60 * 1024 * 1024

BLOCK = 64
HALF = 128


def dot_nn(a, b):
    return lax.dot_general(a, b, (((1,), (0,)), ((), ())), preferred_element_type=F32)


def dot_nt(a, b):
    return lax.dot_general(a, b, (((1,), (1,)), ((), ())), preferred_element_type=F32)


def dot_tn(a, b):
    return lax.dot_general(a, b, (((0,), (0,)), ((), ())), preferred_element_type=F32)


def first_half(rows):
    return lax.broadcasted_iota(jnp.int32, (rows, HALF), 1) < BLOCK


def spread_heads(rows, picks):
    return jnp.concatenate([rows, rows, rows, rows], axis=0) * picks


def pick_heads(wide):
    low = first_half(BLOCK)
    left = jnp.where(low, wide[0:64, 0:HALF], wide[64:128, 0:HALF])
    right = jnp.where(low, wide[128:192, HALF:], wide[192:256, HALF:])
    return jnp.concatenate([left, right], axis=1)


def head_picks():
    row = lax.broadcasted_iota(jnp.int32, (256, 256), 0) // BLOCK
    col = lax.broadcasted_iota(jnp.int32, (256, 256), 1) // BLOCK
    return jnp.where(row == col, 1.0, 0.0).astype(LOW)


def gather_slot(ref, chosen, tile):
    a, b = chosen[2 * tile], chosen[2 * tile + 1]
    cols = pl.ds(tile * HALF, HALF)
    left = ref[pl.ds(pl.multiple_of(a * BLOCK, BLOCK), BLOCK), cols]
    right = ref[pl.ds(pl.multiple_of(b * BLOCK, BLOCK), BLOCK), cols]
    return jnp.where(first_half(BLOCK), left, right)


class Unit:
    def __init__(self, i, live, drawn, blocks):
        last = live - 1

        def state(b):
            return (b >= last).astype(jnp.int32) + (b > last).astype(jnp.int32)

        after = jnp.minimum(i + 1, blocks - 1)
        self.near = [i - 1, i, after]
        self.near_state = [
            jnp.where(i >= 3, state(i - 1), 2),
            state(i),
            jnp.where(i + 1 < blocks, state(after), 2),
        ]
        self.fixed_state = [state(0 * i), state(0 * i + 1)]
        self.chosen = [
            [drawn[(h * blocks + i) * 3 + s] for h in range(4)] for s in range(3)
        ]
        self.chosen_state = [[state(b) for b in row] for row in self.chosen]

    def gather(self, ref, out):
        for n, b in enumerate(self.near):
            out[pl.ds(128 + 64 * n, 64), :] = ref[pl.ds(pl.multiple_of(b * BLOCK, BLOCK), BLOCK), :]
        for s in range(3):
            for t in range(2):
                out[pl.ds(320 + 64 * s, 64), pl.ds(t * HALF, HALF)] = gather_slot(
                    ref, self.chosen[s], t
                )

    def bias(self, table, slots):
        rows = []
        for n in slots:
            if n < 5:
                one = table[(self.fixed_state + self.near_state)[n]]
                rows.append(jnp.concatenate([one, one], axis=1))
            else:
                st = self.chosen_state[n - 5]
                low = first_half(BLOCK)
                rows.append(
                    jnp.concatenate(
                        [
                            jnp.where(low, table[st[0]], table[st[1]]),
                            jnp.where(low, table[st[2]], table[st[3]]),
                        ],
                        axis=1,
                    )
                )
        return jnp.concatenate(rows, axis=0)


def chunk_bias(table, live, first, count):
    last = live - 1
    rows = []
    for n in range(count):
        b = first + n
        st = (b >= last).astype(jnp.int32) + (b > last).astype(jnp.int32)
        one = table[st]
        rows.append(jnp.concatenate([one, one], axis=1))
    return jnp.concatenate(rows, axis=0)


def forward_kernel(scal, drawn, table, x, w, shift, q_o, k_o, v_o, ctx_o, lse_o, picks, kg, vg, sg):
    length = x.shape[0]
    blocks = length // BLOCK
    live = scal[0]
    picks[...] = head_picks()

    def project(c, _):
        rows = pl.ds(pl.multiple_of(c * 512, 512), 512)
        out = (dot_nn(x[rows, :], w[...]) + shift[...]).astype(LOW)
        q_o[rows, :] = out[:, 0:256]
        k_o[rows, :] = out[:, 256:512]
        v_o[rows, :] = out[:, 512:768]
        return 0

    lax.fori_loop(0, length // 512, project, 0)
    for u in range(2):
        kg[u, 0:128, :] = k_o[0:128, :]
        vg[u, 0:128, :] = v_o[0:128, :]

    def sparse(i, u):
        unit = Unit(i, live, drawn, blocks)
        rows = pl.ds(pl.multiple_of(i * BLOCK, BLOCK), BLOCK)
        bd = spread_heads(q_o[rows, :] * jnp.asarray(QUERY_SCALE, LOW), picks[...])
        unit.gather(k_o, kg.at[u])
        unit.gather(v_o, vg.at[u])
        s = dot_nt(kg[u], bd) + unit.bias(table, range(8))
        m = jnp.max(s, axis=0, keepdims=True)
        e = jnp.exp(s - m)
        total = jnp.sum(e, axis=0, keepdims=True)
        p = (e * (1.0 / total)).astype(LOW)
        o = dot_tn(p, vg[u])
        ctx_o[rows, :] = pick_heads(o).astype(LOW)
        lse_o[pl.ds(i, 1), :] = m + jnp.log(total)

    def pair(j, _):
        sparse(2 + 2 * j, 0)
        sparse(3 + 2 * j, 1)
        return 0

    lax.fori_loop(0, blocks // 2 - 1, pair, 0)

    for g in range(2):
        bd = spread_heads(q_o[g * 64 : g * 64 + 64, :] * jnp.asarray(QUERY_SCALE, LOW), picks[...])

        def score(c, m):
            rows = pl.ds(pl.multiple_of(c * 512, 512), 512)
            s = dot_nt(k_o[rows, :], bd) + chunk_bias(table, live, c * 8, 8)
            sg[rows, :] = s
            return jnp.maximum(m, jnp.max(s, axis=0, keepdims=True))

        m = lax.fori_loop(0, length // 512, score, jnp.full((1, 256), MASK_VALUE, F32))

        def raise_(c, total):
            rows = pl.ds(pl.multiple_of(c * 512, 512), 512)
            e = jnp.exp(sg[rows, :] - m)
            sg[rows, :] = e
            return total + jnp.sum(e, axis=0, keepdims=True)

        total = lax.fori_loop(0, length // 512, raise_, jnp.zeros((1, 256), F32))
        scale = 1.0 / total

        def mix(c, o):
            rows = pl.ds(pl.multiple_of(c * 512, 512), 512)
            p = (sg[rows, :] * scale).astype(LOW)
            return o + dot_tn(p, v_o[rows, :])

        o = lax.fori_loop(0, length // 512, mix, jnp.zeros((256, 256), F32))
        ctx_o[g * 64 : g * 64 + 64, :] = pick_heads(o).astype(LOW)
        lse_o[g : g + 1, :] = m + jnp.log(total)


def vmem():
    return pl.BlockSpec(memory_space=pltpu.VMEM)


def smem():
    return pl.BlockSpec(memory_space=pltpu.SMEM)


def forward_attention(scal, drawn, table, x, w, shift):
    length = x.shape[0]
    blocks = length // BLOCK
    rows = jax.ShapeDtypeStruct((length, 256), LOW)
    return pl.pallas_call(
        forward_kernel,
        out_shape=(rows, rows, rows, rows, jax.ShapeDtypeStruct((blocks, 256), F32)),
        in_specs=[smem(), smem(), vmem(), vmem(), vmem(), vmem()],
        out_specs=[vmem()] * 5,
        scratch_shapes=[
            pltpu.VMEM((256, 256), LOW),
            pltpu.VMEM((2, 512, 256), LOW),
            pltpu.VMEM((2, 512, 256), LOW),
            pltpu.VMEM((length, 256), F32),
        ],
        compiler_params=pltpu.CompilerParams(vmem_limit_bytes=VMEM_LIMIT),
        cost_estimate=pl.CostEstimate(flops=16_000_000_000, bytes_accessed=12_000_000, transcendentals=10_000_000),
        name="attend_forward",
    )(scal, drawn, table, x, w, shift)


def normalize(summed):
    center = summed - jnp.mean(summed, axis=-1, keepdims=True)
    factor = lax.rsqrt(jnp.mean(center * center, axis=-1, keepdims=True) + NORM_EPSILON)
    return (center * factor, factor)


def normalize_back(grad_normed, normed, factor):
    return factor * (
        grad_normed
        - jnp.mean(grad_normed, axis=-1, keepdims=True)
        - normed * jnp.mean(grad_normed * normed, axis=-1, keepdims=True)
    )


ERF_P = 0.3275911 * 0.7071067811865476
ERF_A = (0.254829592, -0.284496736, 1.421413741, -1.453152027, 1.061405429)


def gelu_parts(v):
    bell = jnp.exp(-0.5 * v * v)
    t = 1.0 / (1.0 + ERF_P * jnp.abs(v))
    a1, a2, a3, a4, a5 = (0.5 * a for a in ERF_A)
    tail = ((((a5 * t + a4) * t + a3) * t + a2) * t + a1) * t * bell
    cumulative = jnp.where(v < 0.0, tail, 1.0 - tail)
    return v * cumulative, cumulative + v * (NORMAL_PEAK * bell)


def middle_kernel(
    scal, table, x, cot, ctx, w_out, w_up, w_down, up_shift, vec,
    out_o, gz1_o, gctx_o, delta_o, pack0, pack1, pack2, pack3, gdown_o, gup_o, gout_o, gub_o, gvec_o, act, slope,
):
    step = pl.program_id(0)
    rows = x.shape[0]
    last = scal[0] - 1

    @pl.when(step == 0)
    def _():
        for ref in (gdown_o, gup_o, gout_o, gub_o, gvec_o):
            ref[...] = jnp.zeros_like(ref)

    marks = []
    for n in range(rows // BLOCK):
        b = step * (rows // BLOCK) + n
        st = (b >= last).astype(jnp.int32) + (b > last).astype(jnp.int32)
        one = table[st]
        marks.append(jnp.concatenate([one, one], axis=1))
    open_ = jnp.concatenate(marks, axis=0) == 0.0

    def row(n):
        return vec[n : n + 1, :]

    ctx_v = ctx[...]
    attended = dot_nn(ctx_v, w_out[...]) + row(2)
    normed_one, factor_one = normalize(x[...].astype(F32) + attended)
    first_out = normed_one * row(3) + row(4)
    first_low = first_out.astype(LOW)
    branch = row(5)
    for c in range(0, 1024, 256):
        pre = dot_nn(first_low, w_up[:, c : c + 256]) + up_shift[:, c : c + 256]
        a, s = gelu_parts(pre)
        act[:, c : c + 256] = a.astype(LOW)
        slope[:, c : c + 256] = s
    branch = dot_nn(act[...], w_down[...]) + row(5)
    normed_two, factor_two = normalize(first_out + branch)
    out_o[...] = jnp.where(open_, normed_two * row(6) + row(7), 0.0).astype(LOW)
    grad_y = jnp.where(open_, cot[...].astype(F32), 0.0)
    grad_z2 = normalize_back(grad_y * row(6), normed_two, factor_two)
    grad_branch = grad_z2.astype(LOW)
    gdown_o[...] += dot_tn(act[...], grad_branch)
    back = jnp.zeros((rows, 256), F32)
    for c in range(0, 1024, 256):
        grad_act = dot_nt(grad_branch, w_down[c : c + 256, :])
        grad_pre = (grad_act * slope[:, c : c + 256]).astype(LOW)
        act[:, c : c + 256] = grad_pre
        gub_o[:, c : c + 256] += jnp.sum(grad_pre.astype(F32), axis=0, keepdims=True)
    gup_o[...] += dot_tn(first_low, act[...])
    grad_first = grad_z2 + dot_nt(act[...], w_up[...])
    grad_z1 = normalize_back(grad_first * row(3), normed_one, factor_one)
    gz1_o[...] = grad_z1
    grad_attended = grad_z1.astype(LOW)
    gout_o[...] += dot_tn(ctx_v, grad_attended)
    grad_context = dot_nt(grad_attended, w_out[...]).astype(LOW)
    gctx_o[...] = grad_context

    def add(n, values):
        gvec_o[n : n + 1, :] += jnp.sum(values, axis=0, keepdims=True)

    add(2, grad_attended.astype(F32))
    add(3, grad_first * normed_one)
    add(4, grad_first)
    add(5, grad_branch.astype(F32))
    add(6, grad_y * normed_two)
    add(7, grad_y)
    both = ctx_v.astype(F32) * grad_context.astype(F32)
    upper = both.astype(LOW)
    lower = (both - upper.astype(F32)).astype(LOW)
    group = lax.broadcasted_iota(jnp.int32, (8, 256), 1) // BLOCK
    ones = jnp.where(group == lax.broadcasted_iota(jnp.int32, (8, 256), 0), 1.0, 0.0).astype(LOW)
    sums = dot_nt(ones, upper) + dot_nt(ones, lower)
    for n in range(rows // BLOCK):
        part = sums[0:4, n * BLOCK : (n + 1) * BLOCK]
        delta_o[n : n + 1, :] = jnp.concatenate([part[h : h + 1, :] for h in range(4)], axis=1)

    @pl.when(step == pl.num_programs(0) - 1)
    def _():
        for r, pack in enumerate((pack0, pack1, pack2, pack3)):
            piece = scal[1] ^ r
            shard, core = piece // 2, piece % 2
            here = pl.ds(pl.multiple_of(piece * 64, 64), 64)
            pack[:, 0:1024] = gup_o[here, :].astype(LOW)
            pack[:, 1024:1280] = gout_o[here, :].astype(LOW)
            for g in range(4):
                at = pl.ds(pl.multiple_of(shard * 512 + g * 128 + core * 64, 64), 64)
                pack[:, 1280 + 256 * g : 1536 + 256 * g] = gdown_o[at, :].astype(LOW)
            lines = [gub_o[:, pl.ds(pl.multiple_of(shard * 512 + 128 * n, 128), 128)] for n in range(4)]
            first = shard == 0
            for n in range(4):
                line = jnp.where(first, gvec_o[n : n + 1, :], gvec_o[4 + n : 5 + n, :])
                lines += [line[:, 0:128], line[:, 128:256]]
            put_extra(pack, 2304, lines, core)


def put_extra(pack, at, lines, core):
    some = jnp.concatenate(lines + [jnp.zeros((16 - len(lines), HALF), F32)], axis=0)
    pack[0:16, at : at + HALF] = jnp.where(core == 0, some, 0.0).astype(LOW)
    pack[16:64, at : at + HALF] = jnp.zeros((48, HALF), LOW)


def middle(scal, table, x, cot, ctx, w_out, w_up, w_down, up_shift, vec):
    length = x.shape[0]
    rows = 512
    wide = pl.BlockSpec((rows, 256), lambda i, s: (i, 0))

    def whole(*shape):
        return pl.BlockSpec(shape, lambda i, s: (0,) * len(shape))

    shape = jax.ShapeDtypeStruct
    return pl.pallas_call(
        middle_kernel,
        grid_spec=pltpu.PrefetchScalarGridSpec(
            num_scalar_prefetch=1,
            grid=(length // rows,),
            in_specs=[
                whole(3, 64, 128), wide, wide, wide, whole(256, 256), whole(256, 1024), whole(1024, 256),
                whole(1, 1024), whole(8, 256),
            ],
            out_specs=[
                wide, wide, wide, pl.BlockSpec((rows // BLOCK, 256), lambda i, s: (i, 0)),
                whole(64, 2432), whole(64, 2432), whole(64, 2432), whole(64, 2432),
            ],
            scratch_shapes=[
                pltpu.VMEM((1024, 256), F32), pltpu.VMEM((256, 1024), F32), pltpu.VMEM((256, 256), F32),
                pltpu.VMEM((1, 1024), F32), pltpu.VMEM((8, 256), F32),
                pltpu.VMEM((rows, 1024), LOW), pltpu.VMEM((rows, 1024), F32),
            ],
        ),
        out_shape=(
            shape((length, 256), LOW), shape((length, 256), F32), shape((length, 256), LOW),
            shape((length // BLOCK, 256), F32),
        ) + (shape((64, 2432), LOW),) * 4,
        compiler_params=pltpu.CompilerParams(vmem_limit_bytes=VMEM_LIMIT),
        cost_estimate=pl.CostEstimate(flops=16_000_000_000, bytes_accessed=20_000_000, transcendentals=10_000_000),
        name="middle",
    )(scal, table, x, cot, ctx, w_out, w_up, w_down, up_shift, vec)


def backward_kernel(
    scal, drawn, table, q, k, v, gctx, lse, delta, gz1, x, w,
    gin_o, pack0, pack1, pack2, pack3, picks, kg, vg, dq, dk, dv, gw_o,
):
    length = x.shape[0]
    blocks = length // BLOCK
    live = scal[0]
    picks[...] = head_picks()
    dk[...] = jnp.zeros_like(dk)
    dv[...] = jnp.zeros_like(dv)
    for u in range(2):
        kg[u, 0:128, :] = k[0:128, :]
        vg[u, 0:128, :] = v[0:128, :]

    def terms(kh, vh, bias, bdq, bdo, lse_row, delta_row):
        p = jnp.exp(dot_nt(kh, bdq) + bias - lse_row)
        dvh = dot_nn(p.astype(LOW), bdo)
        ds = (p * (dot_nt(vh, bdo) - delta_row)).astype(LOW)
        return dvh, dot_nn(ds, bdq), dot_tn(ds, kh)

    def spread(i):
        rows = pl.ds(pl.multiple_of(i * BLOCK, BLOCK), BLOCK)
        bdq = spread_heads(q[rows, :] * jnp.asarray(QUERY_SCALE, LOW), picks[...])
        bdo = spread_heads(gctx[rows, :], picks[...])
        return rows, bdq, bdo

    def sparse(i, u):
        unit = Unit(i, live, drawn, blocks)
        rows, bdq, bdo = spread(i)
        unit.gather(k, kg.at[u])
        unit.gather(v, vg.at[u])
        lse_row, delta_row = lse[pl.ds(i, 1), :], delta[pl.ds(i, 1), :]
        low = first_half(BLOCK)
        grad_q = None
        for half in range(2):
            part = slice(half * 256, half * 256 + 256)
            dvh, dkh, dqh = terms(
                kg[u, part, :], vg[u, part, :], unit.bias(table, range(4 * half, 4 * half + 4)), bdq, bdo, lse_row, delta_row
            )
            grad_q = dqh if grad_q is None else grad_q + dqh
            for acc, terms_ in ((dk, dkh), (dv, dvh)):
                if half == 0:
                    acc[0:128, :] += terms_[0:128, :]
                for n in range(4):
                    slot = 4 * half + n
                    one = terms_[n * 64 : n * 64 + 64, :]
                    if slot < 2:
                        continue
                    if slot < 5:
                        at = pl.ds(pl.multiple_of(unit.near[slot - 2] * BLOCK, BLOCK), BLOCK)
                        acc[at, :] += one
                    else:
                        for h in range(4):
                            t = h // 2
                            at = pl.ds(pl.multiple_of(unit.chosen[slot - 5][h] * BLOCK, BLOCK), BLOCK)
                            cols = pl.ds(t * HALF, HALF)
                            mine = low if h % 2 == 0 else jnp.logical_not(low)
                            acc[at, cols] += jnp.where(mine, one[:, t * HALF : t * HALF + HALF], 0.0)
        dq[rows, :] = (pick_heads(grad_q) * QUERY_SCALE).astype(LOW)

    def pair(j, _):
        sparse(2 + 2 * j, 0)
        sparse(3 + 2 * j, 1)
        return 0

    lax.fori_loop(0, blocks // 2 - 1, pair, 0)

    for g in range(2):
        _, bdq, bdo = spread(g)
        lse_row, delta_row = lse[g : g + 1, :], delta[g : g + 1, :]

        def chunk(c, grad_q):
            at = pl.ds(pl.multiple_of(c * 256, 256), 256)
            dvh, dkh, dqh = terms(
                k[at, :], v[at, :], chunk_bias(table, live, c * 4, 4), bdq, bdo, lse_row, delta_row
            )
            dk[at, :] += dkh
            dv[at, :] += dvh
            return grad_q + dqh

        grad_q = lax.fori_loop(0, length // 256, chunk, jnp.zeros((256, 256), F32))
        dq[g * 64 : g * 64 + 64, :] = (pick_heads(grad_q) * QUERY_SCALE).astype(LOW)

    gw_o[...] = jnp.zeros_like(gw_o)

    def finish(c, shifts):
        rows = pl.ds(pl.multiple_of(c * 512, 512), 512)
        dqkv = jnp.concatenate([dq[rows, :], dk[rows, :].astype(LOW), dv[rows, :].astype(LOW)], axis=1)
        gin_o[rows, :] = (gz1[rows, :] + dot_nt(dqkv, w[...])).astype(LOW)
        gw_o[...] += dot_tn(x[rows, :], dqkv)
        return shifts + jnp.sum(dqkv.astype(F32), axis=0, keepdims=True)

    shifts = lax.fori_loop(0, length // 512, finish, jnp.zeros((1, 768), F32))
    for r, pack in enumerate((pack0, pack1, pack2, pack3)):
        piece = scal[1] ^ r
        core = piece % 2
        pack[:, 0:768] = gw_o[pl.ds(pl.multiple_of(piece * 64, 64), 64), :].astype(LOW)
        mine = jnp.where(piece // 2 == 0, shifts, 0.0)
        lines = [jnp.zeros((4, HALF), F32)] + [mine[:, a : a + HALF] for a in (0, 128, 512, 640)]
        lines += [jnp.zeros((8, HALF), F32)]
        pack[:, 768:896] = jnp.zeros((64, HALF), LOW)
        pack[0:16, 768:896] = jnp.where(core == 0, jnp.concatenate(lines, axis=0), 0.0).astype(LOW)


def backward_attention(scal, drawn, table, q, k, v, gctx, lse, delta, gz1, x, w):
    length = x.shape[0]
    shape = jax.ShapeDtypeStruct
    return pl.pallas_call(
        backward_kernel,
        out_shape=(shape((length, 256), LOW),) + (shape((64, 896), LOW),) * 4,
        in_specs=[smem(), smem()] + [vmem()] * 10,
        out_specs=[vmem()] * 5,
        scratch_shapes=[
            pltpu.VMEM((256, 256), LOW),
            pltpu.VMEM((2, 512, 256), LOW),
            pltpu.VMEM((2, 512, 256), LOW),
            pltpu.VMEM((length, 256), LOW),
            pltpu.VMEM((length, 256), F32),
            pltpu.VMEM((length, 256), F32),
            pltpu.VMEM((256, 768), F32),
        ],
        compiler_params=pltpu.CompilerParams(vmem_limit_bytes=VMEM_LIMIT),
        cost_estimate=pl.CostEstimate(flops=40_000_000_000, bytes_accessed=20_000_000, transcendentals=10_000_000),
        name="attend_backward",
    )(scal, drawn, table, q, k, v, gctx, lse, delta, gz1, x, w)


def bias_table(tail):
    column = jnp.stack([jnp.zeros_like(tail, F32), jnp.where(tail == 1, 0.0, MASK_VALUE), jnp.full(tail.shape, MASK_VALUE, F32)])
    return jnp.broadcast_to(column[:, :, None], (3, BLOCK, HALF))


def reorder_kernel(scatter, order, src, *rest):
    *_, dst, held, arrived, left = rest
    count = src.shape[0]
    loads, stores = [], []
    for j in range(count):
        one = order[j]
        loads.append(pltpu.make_async_copy(src.at[j if scatter else one], held.at[j], arrived.at[j]))
        stores.append(pltpu.make_async_copy(held.at[j], dst.at[one if scatter else j], left.at[j]))
        loads[-1].start()
    for load, store in zip(loads, stores):
        load.wait()
        store.start()
    for store in stores:
        store.wait()


def reorder(order, src, scatter, after=()):
    return pl.pallas_call(
        functools.partial(reorder_kernel, scatter),
        out_shape=jax.ShapeDtypeStruct(src.shape, src.dtype),
        in_specs=[smem()] + [pl.BlockSpec(memory_space=pl.ANY)] * (1 + len(after)),
        out_specs=pl.BlockSpec(memory_space=pl.ANY),
        scratch_shapes=[
            pltpu.VMEM(src.shape, src.dtype),
            pltpu.SemaphoreType.DMA((src.shape[0],)),
            pltpu.SemaphoreType.DMA((src.shape[0],)),
        ],
        cost_estimate=pl.CostEstimate(flops=0, bytes_accessed=4 * src.size, transcendentals=0),
        name="reorder",
    )(order, src, *after)


def hold(values, after):
    count = len(values)
    anywhere = pl.BlockSpec(memory_space=pl.ANY)
    return pl.pallas_call(
        lambda *refs: None,
        out_shape=tuple(jax.ShapeDtypeStruct(v.shape, v.dtype) for v in values),
        in_specs=[anywhere] * (count + len(after)),
        out_specs=(anywhere,) * count,
        input_output_aliases={n: n for n in range(count)},
        name="hold",
    )(*values, *after)


def pack_weights(parts):
    w_qkv, w_out, w_up, w_down, up_bias, vectors = parts
    rows = w_qkv.shape[0]
    down = w_down.reshape(4, rows, -1)
    pack = jnp.concatenate([w_qkv, w_out, w_up] + [down[n] for n in range(4)], axis=1)
    small = jnp.concatenate([up_bias.reshape(-1, 256), vectors], axis=0)
    return pack, small


def exchange_weights(shard_index, pack, small):
    rows = pack.shape[0]
    swap = [(0, 1), (1, 0)]
    other, other_small = lax.ppermute(pack, "shard", swap), lax.ppermute(small, "shard", swap)
    first = shard_index == 0

    def join(own, got):
        return jnp.stack([jnp.where(first, own, got), jnp.where(first, got, own)])

    both, both_small = join(pack, other), join(small, other_small)

    def cols(lo, hi):
        return both[:, :, lo:hi].reshape(2 * rows, hi - lo)

    full_down = jnp.transpose(both[:, :, 2048:].reshape(2, rows, 4, 256), (0, 2, 1, 3)).reshape(-1, 256)
    full_bias = both_small[:, :2].reshape(-1)
    full_vec = both_small[:, 2:].reshape(8, 256)
    return cols(0, 768), cols(768, 1024), cols(1024, 2048), full_down, full_bias, full_vec


def trade(pieces):
    count = lax.axis_size("dp")
    held = [pieces[0]]
    for n in (1, 2, 3):
        pairs = [(d * 2 + s, (d ^ (n % 2)) * 2 + (s ^ (n // 2))) for d in range(count) for s in range(2)]
        held.append(lax.ppermute(pieces[n], ("dp", "shard"), pairs))
    return held


def total(pieces):
    return sum(piece.astype(F32) for piece in pieces)


def sum_rest(part, data_index):
    count = lax.axis_size("dp")
    groups = count // 4
    half = part.shape[0] // 2
    bit = (data_index // 2) % 2
    flip = [(d, d ^ 2) for d in range(count)]
    keep = lax.dynamic_slice_in_dim(part, bit * half, half, 0)
    give = lax.dynamic_slice_in_dim(part, (1 - bit) * half, half, 0)
    part = keep + lax.ppermute(give.astype(LOW), "dp", flip).astype(F32)
    at = data_index // 4
    small = half // groups
    hops = [[(d, (d + 4 * k) % count) for d in range(count)] for k in range(1, groups)]

    def piece(k):
        return lax.dynamic_slice_in_dim(part, lax.rem(at + k, groups) * small, small, 0)

    mine = piece(0)
    got = [lax.ppermute(piece(k + 1).astype(LOW), "dp", hop) for k, hop in enumerate(hops)]
    for one in got:
        mine = mine + one.astype(F32)
    mine = mine.astype(LOW)
    near = jnp.stack([mine] + [lax.ppermute(mine, "dp", hop) for hop in hops])
    core = [(d, d ^ 1) for d in range(count)]
    across = lax.ppermute(near, "dp", flip)
    near_core, across_core = lax.ppermute(near, "dp", core), lax.ppermute(across, "dp", core)
    return jnp.stack([near, across, near_core, across_core]).astype(F32)


def adam_update(grad, state, decay):
    correct_one = 1.0 - FIRST_BETA**STEP
    correct_two = 1.0 - SECOND_BETA**STEP
    first_new = FIRST_BETA * state[1] + (1.0 - FIRST_BETA) * grad
    second_new = SECOND_BETA * state[2] + (1.0 - SECOND_BETA) * grad * grad
    direction = first_new / correct_one / (jnp.sqrt(second_new / correct_two) + ADAM_EPSILON)
    master_new = state[0] - LEARNING_RATE * (direction + decay * state[0])
    return (master_new, first_new, second_new)


def update_kernel(
    where, parts, s_qkv, s_out, s_up, s_down, s_bias, s_vec,
    g_qkv, g_out, g_up, g_down, g_bias, g_vec, o_master, o_first, o_second, grads,
):
    groups, small = parts.shape[1:3]
    index = where[0]
    for core in range(2):
        for side in range(2):
            base = ((index % 2) ^ core) * 64 + (((index // 2) % 2) ^ side) * 32
            for k in range(groups):
                at = base + lax.rem(index // 4 + groups - k, groups) * small
                grads[pl.ds(pl.multiple_of(at, small), small), :] = parts[2 * core + side, k]
    outs = (o_master, o_first, o_second)

    def place(base, grad, state, decay):
        rows, columns = grad.shape
        wide = columns // HALF
        for out, value in zip(outs, adam_update(grad, state, decay)):
            for c in range(wide):
                at = pl.ds(base + c, rows, stride=wide) if wide > 1 else pl.ds(base, rows)
                out[at, :] = value[:, c * HALF : (c + 1) * HALF]

    qkv, outer, up = grads[:, 2304:3072], grads[:, 1024:1280], grads[:, 0:1024]
    g_qkv[...] = qkv
    g_out[...] = outer
    g_up[...] = up
    place(0, qkv, s_qkv, WEIGHT_DECAY)
    place(768, outer, s_out, WEIGHT_DECAY)
    place(1024, up, s_up, WEIGHT_DECAY)
    for n in range(4):
        rows = slice(128 * n, 128 * n + 128)
        down = grads[:, 1280 + 256 * n : 1536 + 256 * n]
        g_down[rows, :] = down
        place(2048 + 256 * n, down, s_down[:, rows, :], WEIGHT_DECAY)
    extra = grads[0:16, 3072:3200]
    g_bias[...] = extra[0:4]
    place(3072, extra[0:4], s_bias, 0.0)
    vec = jnp.concatenate(
        [jnp.concatenate([extra[4 + 2 * n : 5 + 2 * n], extra[5 + 2 * n : 6 + 2 * n]], axis=1) for n in range(4)], axis=0
    )
    g_vec[...] = vec
    place(3076, vec, s_vec, 0.0)


def update(data_index, parts, states):
    shape = lambda *dims: jax.ShapeDtypeStruct(dims, F32)
    s_qkv, s_out, s_up, s_down, s_bias, s_vec = states
    flat = shape(3084, HALF)
    *grads, master, first, second = pl.pallas_call(
        update_kernel,
        out_shape=(
            shape(128, 768), shape(128, 256), shape(128, 1024), shape(512, 256), shape(4, HALF), shape(4, 256),
            flat, flat, flat,
        ),
        in_specs=[smem()] + [vmem()] * 7,
        out_specs=[vmem()] * 9,
        scratch_shapes=[pltpu.VMEM((128, 3200), F32)],
        compiler_params=pltpu.CompilerParams(vmem_limit_bytes=VMEM_LIMIT),
        cost_estimate=pl.CostEstimate(flops=10_000_000, bytes_accessed=14_000_000, transcendentals=400_000),
        name="update",
    )(data_index.reshape(1), parts, s_qkv, s_out, s_up, s_down, s_bias.reshape(3, 4, HALF), s_vec)
    grads[4] = grads[4].reshape(-1)
    return tuple(grads) + tuple(row.reshape(1, -1) for row in (master, first, second))


def on_device(
    hidden, cotangent, assign, live_blocks, tail_live, random_blocks, w_qkv, w_out, w_up, w_down, up_bias, vectors,
    state_qkv, state_out, state_up, state_down, state_ubias, state_vec,
):
    shard_count = lax.axis_size("shard")
    shard_index = lax.axis_index("shard")
    data_index = lax.axis_index("dp")
    row_seqs, rows_here, width = hidden.shape
    length = row_seqs * rows_here
    pack, small = pack_weights((w_qkv, w_out, w_up, w_down, up_bias, vectors))
    pack, small, assign = lax.optimization_barrier((pack, small, assign))
    order = lax.dynamic_index_in_dim(assign.reshape(row_seqs, shard_count), shard_index, 1, keepdims=False)

    def to_slot(rows):
        return lax.all_to_all(rows, "dp", split_axis=0, concat_axis=0, tiled=True).reshape(length, width)

    x = to_slot(reorder(order, hidden, False))
    own = shard_index * row_seqs + lax.dynamic_index_in_dim(order, data_index, 0, keepdims=False)
    live = lax.dynamic_index_in_dim(live_blocks, own, 0, keepdims=False)
    scal = jnp.stack([live, 2 * shard_index + data_index % 2])
    tail = lax.dynamic_index_in_dim(tail_live, own, 0, keepdims=False)
    w_qkv, w_out, w_up, w_down, up_bias, vectors = exchange_weights(shard_index, pack, small)
    vec = vectors.astype(F32)
    shift = jnp.concatenate([vec[0], jnp.zeros_like(vec[0]), vec[1]])[None]
    up_shift = up_bias.astype(F32)[None]
    table = bias_table(tail)
    drawn = random_blocks.reshape(-1)
    ready = (w_qkv, w_out, w_up, w_down, up_shift, vec, shift, table)
    cot = to_slot(reorder(order, cotangent, False, ready))
    q, k, v, ctx, lse = forward_attention(scal, drawn, table, x, w_qkv, shift)
    out, gz1, gctx, delta, *early = middle(
        scal, table, x, cot, ctx, w_out, w_up, w_down, up_shift, vec
    )

    def from_slot(rows):
        return lax.all_to_all(
            rows.reshape(row_seqs, rows_here, width), "dp", split_axis=0, concat_axis=0, tiled=True
        )

    back_out = from_slot(out)
    early = trade(early)
    gin, *late = backward_attention(scal, drawn, table, q, k, v, gctx, lse, delta, gz1, x, w_qkv)
    gin, *late = hold((gin, *late), (back_out, *early[1:]))
    back_gin = from_slot(gin)

    def sum_all(early, late):
        early, late = total(early), total(trade(late))
        sums = jnp.concatenate([early[:, :2304], late[:, :768], early[:, 2304:] + late[:, 768:]], axis=1)
        return sum_rest(sums, data_index)

    made = jax.eval_shape(sum_all, early, late)
    parts = lax.cond(live_blocks[0] > 0, sum_all, lambda *unused: jnp.zeros(made.shape, made.dtype), early, late)
    layer_out = reorder(order, back_out, True)
    updated = update(data_index, parts, (state_qkv, state_out, state_up, state_down, state_ubias, state_vec))
    input_grad = reorder(order, back_gin, True)
    return (layer_out, input_grad) + updated


def solution(mesh):
    placed = (
        P("shard", "dp", None), P("shard", "dp", None), P(), P(), P(), P(("dp", "shard"), None, None, None),
        P("shard", None), P("shard", None), P("shard", None), P("shard", None), P("shard"), P("shard", None),
        P(None, "shard", None), P(None, "shard", None), P(None, "shard", None), P(None, "shard", None),
        P(None, "shard"), P(None, "shard", None),
    )
    return jax.shard_map(
        on_device,
        mesh=mesh,
        in_specs=placed,
        out_specs=(
            P("shard", "dp", None), P("shard", "dp", None), P("shard", None), P("shard", None), P("shard", None),
            P("shard", None), P("shard"), P("shard", None), P("shard", None), P("shard", None), P("shard", None),
        ),
        check_vma=False,
    )
```

```python
import functools

import jax
import jax.numpy as jnp
from jax import lax
from jax.experimental import pallas as pl
from jax.experimental.pallas import tpu as pltpu
from jax.sharding import PartitionSpec as P

STEP = 1
QUERY_SCALE = 0.125
NORM_EPSILON = 1e-12
LEARNING_RATE = 0.02
WEIGHT_DECAY = 0.01
ADAM_EPSILON = 1e-08
FIRST_BETA = 0.5
SECOND_BETA = 0.5
MASK_VALUE = -1e30
NORMAL_PEAK = 0.3989422804014327

LOW = jnp.bfloat16
F32 = jnp.float32
VMEM_LIMIT = 60 * 1024 * 1024

BLOCK = 64
HALF = 128
GROUP = 31
AHEAD_ROWS = 1024
BEHIND_ROWS = 512
BACK = 10


def dot_nn(a, b):
    return lax.dot_general(a, b, (((1,), (0,)), ((), ())), preferred_element_type=F32)


def dot_nt(a, b):
    return lax.dot_general(a, b, (((1,), (1,)), ((), ())), preferred_element_type=F32)


def dot_tn(a, b):
    return lax.dot_general(a, b, (((0,), (0,)), ((), ())), preferred_element_type=F32)


def first_half(rows):
    return lax.broadcasted_iota(jnp.int32, (rows, HALF), 1) < BLOCK


def spread_heads(rows, picks):
    return jnp.concatenate([rows, rows, rows, rows], axis=0) * picks


def pick_heads(wide):
    low = first_half(BLOCK)
    left = jnp.where(low, wide[0:64, 0:HALF], wide[64:128, 0:HALF])
    right = jnp.where(low, wide[128:192, HALF:], wide[192:256, HALF:])
    return jnp.concatenate([left, right], axis=1)


def head_picks():
    row = lax.broadcasted_iota(jnp.int32, (256, 256), 0) // BLOCK
    col = lax.broadcasted_iota(jnp.int32, (256, 256), 1) // BLOCK
    return jnp.where(row == col, 1.0, 0.0).astype(LOW)


def gather_slot(ref, chosen, tile):
    a, b = chosen[2 * tile], chosen[2 * tile + 1]
    cols = pl.ds(tile * HALF, HALF)
    left = ref[pl.ds(pl.multiple_of(a * BLOCK, BLOCK), BLOCK), cols]
    right = ref[pl.ds(pl.multiple_of(b * BLOCK, BLOCK), BLOCK), cols]
    return jnp.where(first_half(BLOCK), left, right)


def turn_pairs(ref, turned):
    pairs = turned.shape[0] // 2

    def one(j, _):
        pair = ref[:, pl.ds(pl.multiple_of(j * HALF, HALF), HALF)]
        turned[j] = pair
        turned[pairs + j] = jnp.concatenate([pair[:, BLOCK:], pair[:, :BLOCK]], axis=1)
        return 0

    lax.fori_loop(0, pairs, one, 0, unroll=8)


def pick_turned(wide):
    low = first_half(BLOCK)
    left, right = wide[0:HALF, 0:HALF].T, wide[HALF:, HALF:].T
    return jnp.concatenate(
        [jnp.where(low, part[0:BLOCK], part[BLOCK:]) for part in (left, right)], axis=1
    )


class Unit:
    def __init__(self, i, live, drawn, blocks):
        last = live - 1

        def state(b):
            return (b >= last).astype(jnp.int32) + (b > last).astype(jnp.int32)

        after = jnp.minimum(i + 1, blocks - 1)
        self.near = [i - 1, i, after]
        self.near_state = [
            jnp.where(i >= 3, state(i - 1), 2),
            state(i),
            jnp.where(i + 1 < blocks, state(after), 2),
        ]
        self.fixed_state = [state(0 * i), state(0 * i + 1)]
        self.chosen = [
            [drawn[(h * blocks + i) * 3 + s] for h in range(4)] for s in range(3)
        ]
        self.chosen_state = [[state(b) for b in row] for row in self.chosen]

    def bias(self, table, slots):
        rows = []
        for n in slots:
            if n < 5:
                one = table[(self.fixed_state + self.near_state)[n]]
                rows.append(jnp.concatenate([one, one], axis=1))
            else:
                st = self.chosen_state[n - 5]
                low = first_half(BLOCK)
                rows.append(
                    jnp.concatenate(
                        [
                            jnp.where(low, table[st[0]], table[st[1]]),
                            jnp.where(low, table[st[2]], table[st[3]]),
                        ],
                        axis=1,
                    )
                )
        return jnp.concatenate(rows, axis=0)


def chunk_bias(table, live, first, count):
    last = live - 1
    rows = []
    for n in range(count):
        b = first + n
        st = (b >= last).astype(jnp.int32) + (b > last).astype(jnp.int32)
        one = table[st]
        rows.append(jnp.concatenate([one, one], axis=1))
    return jnp.concatenate(rows, axis=0)


def slot_rows(unit, ref):
    near = [ref[pl.ds(pl.multiple_of(b * BLOCK, BLOCK), BLOCK), :] for b in unit.near]
    rand = [jnp.concatenate([gather_slot(ref, unit.chosen[s], t) for t in range(2)], axis=1) for s in range(3)]
    return jnp.concatenate([ref[0:128, :]] + near + rand, axis=0)


def slot_turned(unit, first, turned):
    low = lax.broadcasted_iota(jnp.int32, (BLOCK, HALF), 1) < BLOCK
    every = [[b] * 4 for b in unit.near] + unit.chosen
    pairs = turned.shape[0] // 2
    tiles = [first]
    for n in range(3):
        parts = []
        for h in range(4):
            rows = pl.ds(h * BLOCK, BLOCK)
            a, b = every[2 * n][h], every[2 * n + 1][h]
            left = turned[(a & 1) * pairs + (a >> 1), rows, :]
            right = turned[(1 - (b & 1)) * pairs + (b >> 1), rows, :]
            parts.append(jnp.where(low, left, right))
        tiles.append(jnp.concatenate(parts, axis=0))
    return jnp.concatenate(tiles, axis=1)


def forward_kernel(
    scal, drawn, table, x, w, w_kt, w_vt, shift, shift_vt,
    q_o, k_o, v_o, kt_o, ctx_o, lse_o, picks, q_v, k_v, v_v, kt_v, vt, turned, sg, og, sems,
):
    length = x.shape[0]
    blocks = length // BLOCK
    live = scal[0]
    picks[...] = head_picks()

    def project(c, _):
        rows = pl.ds(pl.multiple_of(c * 512, 512), 512)
        xc = x[rows, :]
        out = (dot_nn(xc, w[...]) + shift[...]).astype(LOW)
        q_v[rows, :] = out[:, 0:256]
        k_v[rows, :] = out[:, 256:512]
        v_v[rows, :] = out[:, 512:768]
        kt_v[:, rows] = dot_nt(w_kt[...], xc).astype(LOW)
        vt[:, rows] = (dot_nt(w_vt[...], xc) + shift_vt[:, 0:1]).astype(LOW)
        return 0

    lax.fori_loop(0, length // 512, project, 0)
    copies = [
        pltpu.make_async_copy(here, there, sems.at[n])
        for n, (here, there) in enumerate(((q_v, q_o), (k_v, k_o), (v_v, v_o), (kt_v, kt_o)))
    ]
    for copy in copies:
        copy.start()
    turn_pairs(vt, turned)

    def group(j, _):
        idx = [2 + GROUP * j + u for u in range(GROUP)]
        units = [Unit(i, live, drawn, blocks) for i in idx]
        rows = [pl.ds(pl.multiple_of(i * BLOCK, BLOCK), BLOCK) for i in idx]
        bd = [spread_heads(q_v[r, :] * jnp.asarray(QUERY_SCALE, LOW), picks[...]) for r in rows]
        every = range(GROUP)
        s = [dot_nt(slot_rows(units[u], k_v), bd[u]) + units[u].bias(table, range(8)) for u in every]
        m = [jnp.max(s[u], axis=0, keepdims=True) for u in every]
        e = [jnp.exp(s[u] - m[u]) for u in every]
        total = [jnp.sum(e[u], axis=0, keepdims=True) for u in every]
        o = [
            dot_nn(slot_turned(units[u], vt[:, 0:128], turned), e[u].astype(LOW)) * (1.0 / total[u]) for u in every
        ]
        for u in every:
            ctx_o[rows[u], :] = pick_turned(o[u]).astype(LOW)
            lse_o[pl.ds(idx[u], 1), :] = m[u] + jnp.log(total[u])
        return 0

    lax.fori_loop(0, (blocks - 2) // GROUP, group, 0)

    bds = [
        spread_heads(q_v[g * 64 : g * 64 + 64, :] * jnp.asarray(QUERY_SCALE, LOW), picks[...]) for g in range(2)
    ]

    def score(c, peaks):
        rows = pl.ds(pl.multiple_of(c * 512, 512), 512)
        bias = chunk_bias(table, live, c * 8, 8)
        out = []
        for g in range(2):
            s = dot_nt(k_v[rows, :], bds[g]) + bias
            sg[g, rows, :] = s
            out.append(jnp.maximum(peaks[g], jnp.max(s, axis=0, keepdims=True)))
        return tuple(out)

    peaks = lax.fori_loop(0, length // 512, score, (jnp.full((1, 256), MASK_VALUE, F32),) * 2)

    og[...] = jnp.zeros_like(og)

    def mix(c, totals):
        rows = pl.ds(pl.multiple_of(c * 512, 512), 512)
        out = []
        for g in range(2):
            e = jnp.exp(sg[g, rows, :] - peaks[g])
            out.append(totals[g] + jnp.sum(e, axis=0, keepdims=True))
            og[g] += dot_nn(vt[:, rows], e.astype(LOW))
        return tuple(out)

    totals = lax.fori_loop(0, length // 512, mix, (jnp.zeros((1, 256), F32),) * 2)
    for g in range(2):
        ctx_o[g * 64 : g * 64 + 64, :] = pick_turned(og[g] * (1.0 / totals[g])).astype(LOW)
        lse_o[g : g + 1, :] = peaks[g] + jnp.log(totals[g])
    for copy in copies:
        copy.wait()


def vmem():
    return pl.BlockSpec(memory_space=pltpu.VMEM)


def smem():
    return pl.BlockSpec(memory_space=pltpu.SMEM)


def forward_attention(scal, drawn, table, x, w, w_kt, w_vt, shift, shift_vt):
    length = x.shape[0]
    blocks = length // BLOCK
    rows = jax.ShapeDtypeStruct((length, 256), LOW)
    return pl.pallas_call(
        forward_kernel,
        out_shape=(
            rows, rows, rows, jax.ShapeDtypeStruct((256, length), LOW), rows, jax.ShapeDtypeStruct((blocks, 256), F32),
        ),
        in_specs=[smem(), smem()] + [vmem()] * 7,
        out_specs=[pl.BlockSpec(memory_space=pl.ANY)] * 4 + [vmem()] * 2,
        scratch_shapes=[
            pltpu.VMEM((256, 256), LOW),
            pltpu.VMEM((length, 256), LOW),
            pltpu.VMEM((length, 256), LOW),
            pltpu.VMEM((length, 256), LOW),
            pltpu.VMEM((256, length), LOW),
            pltpu.VMEM((256, length), LOW),
            pltpu.VMEM((blocks, 256, HALF), LOW),
            pltpu.VMEM((2, length, 256), F32),
            pltpu.VMEM((2, 256, 256), F32),
            pltpu.SemaphoreType.DMA((4,)),
        ],
        compiler_params=pltpu.CompilerParams(vmem_limit_bytes=VMEM_LIMIT),
        cost_estimate=pl.CostEstimate(flops=16_000_000_000, bytes_accessed=12_000_000, transcendentals=10_000_000),
        name="attend_forward",
    )(scal, drawn, table, x, w, w_kt, w_vt, shift, shift_vt)


def normalize(summed):
    center = summed - jnp.mean(summed, axis=-1, keepdims=True)
    factor = lax.rsqrt(jnp.mean(center * center, axis=-1, keepdims=True) + NORM_EPSILON)
    return (center * factor, factor)


def normalize_back(grad_normed, normed, factor):
    return factor * (
        grad_normed
        - jnp.mean(grad_normed, axis=-1, keepdims=True)
        - normed * jnp.mean(grad_normed * normed, axis=-1, keepdims=True)
    )


ROOT_HALF = 0.7071067811865476


def gelu_parts(v):
    cumulative = 0.5 * (1.0 + lax.erf(v * ROOT_HALF))
    return v * cumulative, cumulative + v * (NORMAL_PEAK * jnp.exp(-0.5 * v * v))


def open_rows(table, scal, rows):
    last = scal[0] - 1
    marks = []
    for n in range(rows // BLOCK):
        b = pl.program_id(0) * (rows // BLOCK) + n
        one = table[(b >= last).astype(jnp.int32) + (b > last).astype(jnp.int32)]
        marks.append(jnp.concatenate([one, one], axis=1))
    return jnp.concatenate(marks, axis=0) == 0.0


def ahead_kernel(scal, table, x, ctx, w_out, w_up, w_down, up_shift, vec, out_o, one_o, two_o, stat_o, act_o, slope_o):
    rows = x.shape[0]

    def row(n):
        return vec[n : n + 1, :]

    attended = dot_nn(ctx[...], w_out[...]) + row(2)
    normed_one, factor_one = normalize(x[...].astype(F32) + attended)
    one_o[...] = normed_one
    first_out = normed_one * row(3) + row(4)
    first_low = first_out.astype(LOW)
    for c in range(0, 1024, 256):
        pre = dot_nn(first_low, w_up[:, c : c + 256]) + up_shift[:, c : c + 256]
        a, s = gelu_parts(pre)
        act_o[:, c : c + 256] = a.astype(LOW)
        slope_o[:, c : c + 256] = s.astype(LOW)
    branch = dot_nn(act_o[...], w_down[...]) + row(5)
    normed_two, factor_two = normalize(first_out + branch)
    two_o[...] = normed_two
    stat_o[...] = jnp.where(first_half(rows), factor_one, factor_two)
    out_o[...] = jnp.where(open_rows(table, scal, rows), normed_two * row(6) + row(7), 0.0).astype(LOW)


def ahead(scal, table, x, ctx, w_out, w_up, w_down, up_shift, vec):
    length = x.shape[0]
    rows = AHEAD_ROWS

    def wide(columns):
        return pl.BlockSpec((rows, columns), lambda i, s: (i, 0))

    def whole(*shape):
        return pl.BlockSpec(shape, lambda i, s: (0,) * len(shape))

    shape = jax.ShapeDtypeStruct
    return pl.pallas_call(
        ahead_kernel,
        grid_spec=pltpu.PrefetchScalarGridSpec(
            num_scalar_prefetch=1,
            grid=(length // rows,),
            in_specs=[
                whole(3, 64, 128), wide(256), wide(256), whole(256, 256), whole(256, 1024), whole(1024, 256),
                whole(1, 1024), whole(8, 256),
            ],
            out_specs=[wide(256), wide(256), wide(256), wide(HALF), wide(1024), wide(1024)],
        ),
        out_shape=(
            shape((length, 256), LOW), shape((length, 256), F32), shape((length, 256), F32),
            shape((length, HALF), F32), shape((length, 1024), LOW), shape((length, 1024), LOW),
        ),
        compiler_params=pltpu.CompilerParams(vmem_limit_bytes=VMEM_LIMIT),
        cost_estimate=pl.CostEstimate(flops=5_000_000_000, bytes_accessed=34_000_000, transcendentals=10_000_000),
        name="ahead",
    )(scal, table, x, ctx, w_out, w_up, w_down, up_shift, vec)


def behind_kernel(
    scal, table, cot, ctx, one, two, stat, act, slope, w_out, w_up, w_down, vec,
    gz1_o, gctx_o, delta_o, pack0, pack1, pack2, pack3, gdown_o, gup_o, gout_o, gub_o, gvec_o, pre,
):
    step = pl.program_id(0)
    rows = cot.shape[0]

    @pl.when(step == 0)
    def _():
        for ref in (gdown_o, gup_o, gout_o, gub_o, gvec_o):
            ref[...] = jnp.zeros_like(ref)

    def row(n):
        return vec[n : n + 1, :]

    normed_one, normed_two = one[...], two[...]
    factor_one, factor_two = stat[:, 0:1], stat[:, BLOCK : BLOCK + 1]
    first_low = (normed_one * row(3) + row(4)).astype(LOW)
    grad_y = jnp.where(open_rows(table, scal, rows), cot[...].astype(F32), 0.0)
    grad_z2 = normalize_back(grad_y * row(6), normed_two, factor_two)
    grad_branch = grad_z2.astype(LOW)
    for c in range(0, 1024, 256):
        grad_act = dot_nt(grad_branch, w_down[c : c + 256, :])
        grad_pre = (grad_act * slope[:, c : c + 256].astype(F32)).astype(LOW)
        pre[:, c : c + 256] = grad_pre
        gub_o[:, c : c + 256] += jnp.sum(grad_pre.astype(F32), axis=0, keepdims=True)
    gdown_o[...] += dot_tn(act[...], grad_branch)
    grad_first = grad_z2 + dot_nt(pre[...], w_up[...])
    gup_o[...] += dot_tn(first_low, pre[...])
    grad_z1 = normalize_back(grad_first * row(3), normed_one, factor_one)
    gz1_o[...] = grad_z1
    grad_attended = grad_z1.astype(LOW)
    ctx_v = ctx[...]
    gout_o[...] += dot_tn(ctx_v, grad_attended)
    grad_context = dot_nt(grad_attended, w_out[...]).astype(LOW)
    gctx_o[...] = grad_context

    def add(n, values):
        gvec_o[n : n + 1, :] += jnp.sum(values, axis=0, keepdims=True)

    add(2, grad_attended.astype(F32))
    add(3, grad_first * normed_one)
    add(4, grad_first)
    add(5, grad_branch.astype(F32))
    add(6, grad_y * normed_two)
    add(7, grad_y)
    both = ctx_v.astype(F32) * grad_context.astype(F32)
    upper = both.astype(LOW)
    lower = (both - upper.astype(F32)).astype(LOW)
    group = lax.broadcasted_iota(jnp.int32, (8, 256), 1) // BLOCK
    ones = jnp.where(group == lax.broadcasted_iota(jnp.int32, (8, 256), 0), 1.0, 0.0).astype(LOW)
    sums = dot_nt(ones, upper) + dot_nt(ones, lower)
    for n in range(rows // BLOCK):
        part = sums[0:4, n * BLOCK : (n + 1) * BLOCK]
        delta_o[n : n + 1, :] = jnp.concatenate([part[h : h + 1, :] for h in range(4)], axis=1)

    @pl.when(step == pl.num_programs(0) - 1)
    def _():
        for r, pack in enumerate((pack0, pack1, pack2, pack3)):
            piece = scal[1] ^ r
            shard, core = piece // 2, piece % 2
            here = pl.ds(pl.multiple_of(piece * 64, 64), 64)
            pack[:, 0:1024] = gup_o[here, :].astype(LOW)
            pack[:, 1024:1280] = gout_o[here, :].astype(LOW)
            for g in range(4):
                at = pl.ds(pl.multiple_of(shard * 512 + g * 128 + core * 64, 64), 64)
                pack[:, 1280 + 256 * g : 1536 + 256 * g] = gdown_o[at, :].astype(LOW)
            lines = [gub_o[:, pl.ds(pl.multiple_of(shard * 512 + 128 * n, 128), 128)] for n in range(4)]
            first = shard == 0
            for n in range(4):
                line = jnp.where(first, gvec_o[n : n + 1, :], gvec_o[4 + n : 5 + n, :])
                lines += [line[:, 0:128], line[:, 128:256]]
            put_extra(pack, 2304, lines, core)


def put_extra(pack, at, lines, core):
    some = jnp.concatenate(lines + [jnp.zeros((16 - len(lines), HALF), F32)], axis=0)
    pack[0:16, at : at + HALF] = jnp.where(core == 0, some, 0.0).astype(LOW)
    pack[16:64, at : at + HALF] = jnp.zeros((48, HALF), LOW)


def behind(scal, table, cot, ctx, one, two, stat, act, slope, w_out, w_up, w_down, vec):
    length = cot.shape[0]
    rows = BEHIND_ROWS

    def wide(columns):
        return pl.BlockSpec((rows, columns), lambda i, s: (i, 0))

    def whole(*shape):
        return pl.BlockSpec(shape, lambda i, s: (0,) * len(shape))

    shape = jax.ShapeDtypeStruct
    return pl.pallas_call(
        behind_kernel,
        grid_spec=pltpu.PrefetchScalarGridSpec(
            num_scalar_prefetch=1,
            grid=(length // rows,),
            in_specs=[
                whole(3, 64, 128), wide(256), wide(256), wide(256), wide(256), wide(HALF), wide(1024), wide(1024),
                whole(256, 256), whole(256, 1024), whole(1024, 256), whole(8, 256),
            ],
            out_specs=[
                wide(256), wide(256), pl.BlockSpec((rows // BLOCK, 256), lambda i, s: (i, 0)),
                whole(64, 2432), whole(64, 2432), whole(64, 2432), whole(64, 2432),
            ],
            scratch_shapes=[
                pltpu.VMEM((1024, 256), F32), pltpu.VMEM((256, 1024), F32), pltpu.VMEM((256, 256), F32),
                pltpu.VMEM((1, 1024), F32), pltpu.VMEM((8, 256), F32), pltpu.VMEM((rows, 1024), LOW),
            ],
        ),
        out_shape=(
            shape((length, 256), F32), shape((length, 256), LOW), shape((length // BLOCK, 256), F32),
        ) + (shape((64, 2432), LOW),) * 4,
        compiler_params=pltpu.CompilerParams(vmem_limit_bytes=VMEM_LIMIT),
        cost_estimate=pl.CostEstimate(flops=10_000_000_000, bytes_accessed=40_000_000, transcendentals=0),
        name="behind",
    )(scal, table, cot, ctx, one, two, stat, act, slope, w_out, w_up, w_down, vec)


def backward_kernel(
    scal, drawn, table, q, k, v, kt, gctx, lse, delta, gz1, x, w,
    gin_o, pack0, pack1, pack2, pack3, picks, turned, dqg, dq, dk, dv, gw_o, gz1_v, x_v, gin_v, sems,
):
    length = x.shape[0]
    blocks = length // BLOCK
    live = scal[0]
    picks[...] = head_picks()
    dk[...] = jnp.zeros_like(dk)
    dv[...] = jnp.zeros_like(dv)
    loads = [pltpu.make_async_copy(gz1, gz1_v, sems.at[0]), pltpu.make_async_copy(x, x_v, sems.at[1])]
    for load in loads:
        load.start()
    turn_pairs(kt, turned)

    def spread(i):
        rows = pl.ds(pl.multiple_of(i * BLOCK, BLOCK), BLOCK)
        bdq = spread_heads(q[rows, :] * jnp.asarray(QUERY_SCALE, LOW), picks[...])
        bdo = spread_heads(gctx[rows, :], picks[...])
        return rows, bdq, bdo

    def group(idx):
        units = [Unit(i, live, drawn, blocks) for i in idx]
        spreads = [spread(i) for i in idx]
        every = range(len(idx))
        s = [dot_nt(slot_rows(units[u], k), spreads[u][1]) for u in every]
        g = [dot_nt(slot_rows(units[u], v), spreads[u][2]) for u in every]
        p = [jnp.exp(s[u] + units[u].bias(table, range(8)) - lse[pl.ds(idx[u], 1), :]) for u in every]
        ds = [(p[u] * (g[u] - delta[pl.ds(idx[u], 1), :])).astype(LOW) for u in every]
        dvs = [dot_nn(p[u].astype(LOW), spreads[u][2]) for u in every]
        dks = [dot_nn(ds[u], spreads[u][1]) for u in every]
        dqs = [dot_nn(slot_turned(units[u], kt[:, 0:128], turned), ds[u]) for u in every]
        low = first_half(BLOCK)
        for u in every:
            for acc, terms_ in ((dk, dks[u]), (dv, dvs[u])):
                acc[0:128, :] += terms_[0:128, :]
                for n in range(2, 8):
                    one = terms_[n * 64 : n * 64 + 64, :]
                    if n < 5:
                        at = pl.ds(pl.multiple_of(units[u].near[n - 2] * BLOCK, BLOCK), BLOCK)
                        acc[at, :] += one
                    else:
                        for h in range(4):
                            t = h // 2
                            at = pl.ds(pl.multiple_of(units[u].chosen[n - 5][h] * BLOCK, BLOCK), BLOCK)
                            cols = pl.ds(t * HALF, HALF)
                            mine = low if h % 2 == 0 else jnp.logical_not(low)
                            acc[at, cols] += jnp.where(mine, one[:, t * HALF : t * HALF + HALF], 0.0)
            dq[spreads[u][0], :] = (pick_turned(dqs[u]) * QUERY_SCALE).astype(LOW)

    def several(j, _):
        group([2 + BACK * j + u for u in range(BACK)])
        return 0

    lax.fori_loop(0, (blocks - 2) // BACK, several, 0)
    if (blocks - 2) % BACK:
        group([live * 0 + i for i in range(blocks - (blocks - 2) % BACK, blocks)])

    spreads = [spread(g)[1:] for g in range(2)]
    dqg[...] = jnp.zeros_like(dqg)

    def chunk(c, _):
        at = pl.ds(pl.multiple_of(c * 512, 512), 512)
        bias = chunk_bias(table, live, c * 8, 8)
        kh, vh, th = k[at, :], v[at, :], kt[:, at]
        two = range(2)
        s = [dot_nt(kh, spreads[g][0]) for g in two]
        t = [dot_nt(vh, spreads[g][1]) for g in two]
        p = [jnp.exp(s[g] + bias - lse[g : g + 1, :]) for g in two]
        ds = [(p[g] * (t[g] - delta[g : g + 1, :])).astype(LOW) for g in two]
        dvs = [dot_nn(p[g].astype(LOW), spreads[g][1]) for g in two]
        dks = [dot_nn(ds[g], spreads[g][0]) for g in two]
        for g in two:
            dqg[g] += dot_nn(th, ds[g])
        dv[at, :] += dvs[0] + dvs[1]
        dk[at, :] += dks[0] + dks[1]
        return 0

    lax.fori_loop(0, length // 512, chunk, 0, unroll=2)
    for g in range(2):
        dq[g * 64 : g * 64 + 64, :] = (pick_turned(dqg[g]) * QUERY_SCALE).astype(LOW)

    gw_o[...] = jnp.zeros_like(gw_o)
    for load in loads:
        load.wait()

    def finish(c, shifts):
        rows = pl.ds(pl.multiple_of(c * 512, 512), 512)
        dqkv = jnp.concatenate([dq[rows, :], dk[rows, :].astype(LOW), dv[rows, :].astype(LOW)], axis=1)
        gin_v[rows, :] = (gz1_v[rows, :] + dot_nt(dqkv, w[...])).astype(LOW)
        gw_o[...] += dot_tn(x_v[rows, :], dqkv)
        return shifts + jnp.sum(dqkv.astype(F32), axis=0, keepdims=True)

    shifts = lax.fori_loop(0, length // 512, finish, jnp.zeros((1, 768), F32))
    store = pltpu.make_async_copy(gin_v, gin_o, sems.at[2])
    store.start()
    for r, pack in enumerate((pack0, pack1, pack2, pack3)):
        piece = scal[1] ^ r
        core = piece % 2
        pack[:, 0:768] = gw_o[pl.ds(pl.multiple_of(piece * 64, 64), 64), :].astype(LOW)
        mine = jnp.where(piece // 2 == 0, shifts, 0.0)
        lines = [jnp.zeros((4, HALF), F32)] + [mine[:, a : a + HALF] for a in (0, 128, 512, 640)]
        lines += [jnp.zeros((8, HALF), F32)]
        pack[:, 768:896] = jnp.zeros((64, HALF), LOW)
        pack[0:16, 768:896] = jnp.where(core == 0, jnp.concatenate(lines, axis=0), 0.0).astype(LOW)
    store.wait()


def backward_attention(scal, drawn, table, q, k, v, kt, gctx, lse, delta, gz1, x, w):
    length = x.shape[0]
    shape = jax.ShapeDtypeStruct
    return pl.pallas_call(
        backward_kernel,
        out_shape=(shape((length, 256), LOW),) + (shape((64, 896), LOW),) * 4,
        in_specs=[smem(), smem()] + [vmem()] * 8 + [pl.BlockSpec(memory_space=pl.ANY)] * 2 + [vmem()],
        out_specs=[pl.BlockSpec(memory_space=pl.ANY)] + [vmem()] * 4,
        scratch_shapes=[
            pltpu.VMEM((256, 256), LOW),
            pltpu.VMEM((length // BLOCK, 256, HALF), LOW),
            pltpu.VMEM((2, 256, 256), F32),
            pltpu.VMEM((length, 256), LOW),
            pltpu.VMEM((length, 256), F32),
            pltpu.VMEM((length, 256), F32),
            pltpu.VMEM((256, 768), F32),
            pltpu.VMEM((length, 256), F32),
            pltpu.VMEM((length, 256), LOW),
            pltpu.VMEM((length, 256), LOW),
            pltpu.SemaphoreType.DMA((3,)),
        ],
        compiler_params=pltpu.CompilerParams(vmem_limit_bytes=VMEM_LIMIT),
        cost_estimate=pl.CostEstimate(flops=40_000_000_000, bytes_accessed=20_000_000, transcendentals=10_000_000),
        name="attend_backward",
    )(scal, drawn, table, q, k, v, kt, gctx, lse, delta, gz1, x, w)


def bias_table(tail):
    column = jnp.stack([jnp.zeros_like(tail, F32), jnp.where(tail == 1, 0.0, MASK_VALUE), jnp.full(tail.shape, MASK_VALUE, F32)])
    return jnp.broadcast_to(column[:, :, None], (3, BLOCK, HALF))


def reorder_kernel(scatter, where, assign, src, *rest):
    *_, dst, held, arrived, left = rest
    count = src.shape[0]
    shards = assign.shape[0] // count
    loads, stores = [], []
    for j in range(count):
        one = assign[shards * j + where[0]]
        loads.append(pltpu.make_async_copy(src.at[j if scatter else one], held.at[j], arrived.at[j]))
        stores.append(pltpu.make_async_copy(held.at[j], dst.at[one if scatter else j], left.at[j]))
        loads[-1].start()
    for load, store in zip(loads, stores):
        load.wait()
        store.start()
    for store in stores:
        store.wait()


def reorder(shard, assign, src, scatter, after=()):
    return pl.pallas_call(
        functools.partial(reorder_kernel, scatter),
        out_shape=jax.ShapeDtypeStruct(src.shape, src.dtype),
        in_specs=[smem(), smem()] + [pl.BlockSpec(memory_space=pl.ANY)] * (1 + len(after)),
        out_specs=pl.BlockSpec(memory_space=pl.ANY),
        scratch_shapes=[
            pltpu.VMEM(src.shape, src.dtype),
            pltpu.SemaphoreType.DMA((src.shape[0],)),
            pltpu.SemaphoreType.DMA((src.shape[0],)),
        ],
        compiler_params=pltpu.CompilerParams(vmem_limit_bytes=8 * 1024 * 1024),
        cost_estimate=pl.CostEstimate(flops=0, bytes_accessed=4 * src.size, transcendentals=0),
        name="reorder",
    )(shard, assign, src, *after)


def hold(values, after):
    count = len(values)
    anywhere = pl.BlockSpec(memory_space=pl.ANY)
    return pl.pallas_call(
        lambda *refs: None,
        out_shape=tuple(jax.ShapeDtypeStruct(v.shape, v.dtype) for v in values),
        in_specs=[anywhere] * (count + len(after)),
        out_specs=(anywhere,) * count,
        input_output_aliases={n: n for n in range(count)},
        name="hold",
    )(*values, *after)


def pack_kernel(w_qkv, w_out, w_up, w_down, up_bias, vectors, after, out):
    rows = w_qkv.shape[0]
    out[0:rows, 0:768] = w_qkv[...]
    out[0:rows, 768:1024] = w_out[...]
    out[0:rows, 1024:2048] = w_up[...]
    for n in range(4):
        out[0:rows, 2048 + 256 * n : 2304 + 256 * n] = w_down[rows * n : rows * (n + 1), :]
    lines = [up_bias[...].astype(F32)] + [vectors[n : n + 1, :].astype(F32) for n in range(4)]
    line = jnp.concatenate(lines + [jnp.zeros((1, 3072 - 1536), F32)], axis=1)
    out[rows : rows + 16, :] = jnp.broadcast_to(line, (16, 3072)).astype(LOW)


def pack_weights(parts, after):
    w_qkv, w_out, w_up, w_down, up_bias, vectors = parts
    return pl.pallas_call(
        pack_kernel,
        out_shape=jax.ShapeDtypeStruct((w_qkv.shape[0] + 16, 3072), LOW),
        in_specs=[vmem()] * 6 + [pl.BlockSpec(memory_space=pl.ANY)],
        out_specs=vmem(),
        compiler_params=pltpu.CompilerParams(vmem_limit_bytes=8 * 1024 * 1024),
        name="pack_weights",
    )(w_qkv, w_out, w_up, w_down, up_bias.reshape(1, -1), vectors, after)


def unpack_kernel(shard, own, got, w_qkv, w_out, w_up, w_down, w_kt, w_vt, up_shift, vec, shift, shift_vt):
    rows = own.shape[0] - 16
    first = shard[0] == 0

    def half(n, at, cols):
        mine, other = own[at, cols], got[at, cols]
        return jnp.where(first == (n == 0), mine, other)

    for n in range(2):
        here = slice(n * rows, (n + 1) * rows)
        w_qkv[here, :] = half(n, slice(0, rows), slice(0, 768))
        w_out[here, :] = half(n, slice(0, rows), slice(768, 1024))
        w_up[here, :] = half(n, slice(0, rows), slice(1024, 2048))
        for g in range(4):
            at = (4 * n + g) * rows
            w_down[at : at + rows, :] = half(n, slice(0, rows), slice(2048 + 256 * g, 2304 + 256 * g))
        line = half(n, slice(rows, rows + 16), slice(0, 1536)).astype(F32)[0:1]
        up_shift[:, 512 * n : 512 * n + 512] = line[:, 0:512]
        for g in range(4):
            vec[4 * n + g : 4 * n + g + 1, :] = line[:, 512 + 256 * g : 768 + 256 * g]
    shift[...] = jnp.concatenate([vec[0:1, :], jnp.zeros((1, 256), F32), vec[1:2, :]], axis=1)
    w_kt[...] = w_qkv[:, 256:512].astype(F32).T.astype(LOW)
    w_vt[...] = w_qkv[:, 512:768].astype(F32).T.astype(LOW)
    shift_vt[...] = jnp.broadcast_to(vec[1:2, :], (HALF, 256)).T


def unpack_weights(shard, own, got):
    shape = jax.ShapeDtypeStruct
    return pl.pallas_call(
        unpack_kernel,
        out_shape=(
            shape((256, 768), LOW), shape((256, 256), LOW), shape((256, 1024), LOW), shape((1024, 256), LOW),
            shape((256, 256), LOW), shape((256, 256), LOW), shape((1, 1024), F32), shape((8, 256), F32),
            shape((1, 768), F32), shape((256, HALF), F32),
        ),
        in_specs=[smem(), vmem(), vmem()],
        out_specs=[vmem()] * 10,
        compiler_params=pltpu.CompilerParams(vmem_limit_bytes=16 * 1024 * 1024),
        name="unpack_weights",
    )(shard, own, got)


def trade(pieces):
    count = lax.axis_size("dp")
    held = [pieces[0]]
    for n in (1, 2, 3):
        pairs = [(d * 2 + s, (d ^ (n % 2)) * 2 + (s ^ (n // 2))) for d in range(count) for s in range(2)]
        held.append(lax.ppermute(pieces[n], ("dp", "shard"), pairs))
    return held


def total(pieces):
    return sum(piece.astype(F32) for piece in pieces)


def sum_rest(part, data_index):
    count = lax.axis_size("dp")
    groups = count // 4
    half = part.shape[0] // 2
    bit = (data_index // 2) % 2
    flip = [(d, d ^ 2) for d in range(count)]
    keep = lax.dynamic_slice_in_dim(part, bit * half, half, 0)
    give = lax.dynamic_slice_in_dim(part, (1 - bit) * half, half, 0)
    part = keep + lax.ppermute(give.astype(LOW), "dp", flip).astype(F32)
    at = data_index // 4
    small = half // groups
    hops = [[(d, (d + 4 * k) % count) for d in range(count)] for k in range(1, groups)]

    def piece(k):
        return lax.dynamic_slice_in_dim(part, lax.rem(at + k, groups) * small, small, 0)

    mine = piece(0)
    got = [lax.ppermute(piece(k + 1).astype(LOW), "dp", hop) for k, hop in enumerate(hops)]
    for one in got:
        mine = mine + one.astype(F32)
    mine = mine.astype(LOW)
    near = jnp.stack([mine] + [lax.ppermute(mine, "dp", hop) for hop in hops])
    core = [(d, d ^ 1) for d in range(count)]
    across = lax.ppermute(near, "dp", flip)
    near_core, across_core = lax.ppermute(near, "dp", core), lax.ppermute(across, "dp", core)
    return jnp.stack([near, across, near_core, across_core]).astype(F32)


def adam_update(grad, state, decay):
    correct_one = 1.0 - FIRST_BETA**STEP
    correct_two = 1.0 - SECOND_BETA**STEP
    first_new = FIRST_BETA * state[1] + (1.0 - FIRST_BETA) * grad
    second_new = SECOND_BETA * state[2] + (1.0 - SECOND_BETA) * grad * grad
    direction = first_new / correct_one / (jnp.sqrt(second_new / correct_two) + ADAM_EPSILON)
    master_new = state[0] - LEARNING_RATE * (direction + decay * state[0])
    return (master_new, first_new, second_new)


def update_kernel(
    where, parts, s_qkv, s_out, s_up, s_down, s_bias, s_vec,
    g_qkv, g_out, g_up, g_down, g_bias, g_vec, o_master, o_first, o_second, grads, flat, sems,
):
    groups, small = parts.shape[1:3]
    index = where[0]
    for core in range(2):
        for side in range(2):
            base = ((index % 2) ^ core) * 64 + (((index // 2) % 2) ^ side) * 32
            for k in range(groups):
                at = base + lax.rem(index // 4 + groups - k, groups) * small
                grads[pl.ds(pl.multiple_of(at, small), small), :] = parts[2 * core + side, k]
    outs = [flat.at[n] for n in range(3)]

    def place(base, grad, state, decay):
        rows, columns = grad.shape
        wide = columns // HALF
        for out, value in zip(outs, adam_update(grad, state, decay)):
            for c in range(wide):
                at = pl.ds(base + c, rows, stride=wide) if wide > 1 else pl.ds(base, rows)
                out[at, :] = value[:, c * HALF : (c + 1) * HALF]

    qkv, outer, up = grads[:, 2304:3072], grads[:, 1024:1280], grads[:, 0:1024]
    g_qkv[...] = qkv
    g_out[...] = outer
    g_up[...] = up
    place(0, qkv, s_qkv, WEIGHT_DECAY)
    place(768, outer, s_out, WEIGHT_DECAY)
    place(1024, up, s_up, WEIGHT_DECAY)
    for n in range(4):
        rows = slice(128 * n, 128 * n + 128)
        down = grads[:, 1280 + 256 * n : 1536 + 256 * n]
        g_down[rows, :] = down
        place(2048 + 256 * n, down, s_down[:, rows, :], WEIGHT_DECAY)
    extra = grads[0:16, 3072:3200]
    g_bias[...] = extra[0:4]
    place(3072, extra[0:4], s_bias, 0.0)
    vec = jnp.concatenate(
        [jnp.concatenate([extra[4 + 2 * n : 5 + 2 * n], extra[5 + 2 * n : 6 + 2 * n]], axis=1) for n in range(4)], axis=0
    )
    g_vec[...] = vec
    place(3076, vec, s_vec, 0.0)
    copies = [
        pltpu.make_async_copy(flat.at[n], there.reshape(flat.shape[1:]), sems.at[n])
        for n, there in enumerate((o_master, o_first, o_second))
    ]
    for copy in copies:
        copy.start()
    for copy in copies:
        copy.wait()


def update(data_index, parts, states):
    shape = lambda *dims: jax.ShapeDtypeStruct(dims, F32)
    s_qkv, s_out, s_up, s_down, s_bias, s_vec = states
    flat = shape(1, 3084 * HALF)
    *grads, master, first, second = pl.pallas_call(
        update_kernel,
        out_shape=(
            shape(128, 768), shape(128, 256), shape(128, 1024), shape(512, 256), shape(4, HALF), shape(4, 256),
            flat, flat, flat,
        ),
        in_specs=[smem()] + [vmem()] * 7,
        out_specs=[vmem()] * 6 + [pl.BlockSpec(memory_space=pl.ANY)] * 3,
        scratch_shapes=[
            pltpu.VMEM((128, 3200), F32), pltpu.VMEM((3, 3084, HALF), F32), pltpu.SemaphoreType.DMA((3,)),
        ],
        compiler_params=pltpu.CompilerParams(vmem_limit_bytes=VMEM_LIMIT),
        cost_estimate=pl.CostEstimate(flops=10_000_000, bytes_accessed=14_000_000, transcendentals=400_000),
        name="update",
    )(data_index.reshape(1), parts, s_qkv, s_out, s_up, s_down, s_bias.reshape(3, 4, HALF), s_vec)
    grads[4] = grads[4].reshape(-1)
    return tuple(grads) + (master, first, second)


def on_device(
    hidden, cotangent, assign, live_blocks, tail_live, random_blocks, w_qkv, w_out, w_up, w_down, up_bias, vectors,
    state_qkv, state_out, state_up, state_down, state_ubias, state_vec,
):
    shard_count = lax.axis_size("shard")
    shard_index = lax.axis_index("shard")
    data_index = lax.axis_index("dp")
    row_seqs, rows_here, width = hidden.shape
    length = row_seqs * rows_here
    shard = shard_index.reshape(1)

    def to_slot(rows):
        return lax.all_to_all(rows, "dp", split_axis=0, concat_axis=0, tiled=True).reshape(length, width)

    sent = reorder(shard, assign, hidden, False)
    x = to_slot(sent)
    pack = pack_weights((w_qkv, w_out, w_up, w_down, up_bias, vectors), sent)
    got = lax.ppermute(pack, "shard", [(0, 1), (1, 0)])
    w_qkv, w_out, w_up, w_down, w_kt, w_vt, up_shift, vec, shift, shift_vt = unpack_weights(shard, pack, got)
    slot = assign[data_index * shard_count + shard_index]
    own = shard_index * row_seqs + slot
    scal = jnp.stack([live_blocks[own], 2 * shard_index + data_index % 2])
    table = bias_table(lax.dynamic_index_in_dim(tail_live, own, 0, keepdims=False))
    drawn = random_blocks.reshape(-1)
    ready = (w_qkv, scal, table, drawn)
    cot = to_slot(reorder(shard, assign, cotangent, False, ready))
    q, k, v, kt, ctx, lse = forward_attention(scal, drawn, table, x, w_qkv, w_kt, w_vt, shift, shift_vt)
    out, *kept = ahead(scal, table, x, ctx, w_out, w_up, w_down, up_shift, vec)

    def from_slot(rows):
        return lax.all_to_all(
            rows.reshape(row_seqs, rows_here, width), "dp", split_axis=0, concat_axis=0, tiled=True
        )

    back_out = from_slot(out)
    gz1, gctx, delta, *early = behind(scal, table, cot, ctx, *kept, w_out, w_up, w_down, vec)
    early = trade(early)
    gin, *late = backward_attention(scal, drawn, table, q, k, v, kt, gctx, lse, delta, gz1, x, w_qkv)
    gin, *late = hold((gin, *late), (back_out, *early[1:]))
    back_gin = from_slot(gin)

    def sum_all(early, late, back_out):
        early, late = total(early), total(trade(late))
        sums = jnp.concatenate([early[:, :2304], late[:, :768], early[:, 2304:] + late[:, 768:]], axis=1)
        return sum_rest(sums, data_index), reorder(shard, assign, back_out, True)

    made = jax.eval_shape(sum_all, early, late, back_out)
    parts, layer_out = lax.cond(
        live_blocks[0] > 0,
        sum_all,
        lambda *unused: jax.tree.map(lambda one: jnp.zeros(one.shape, one.dtype), made),
        early, late, back_out,
    )
    updated = update(data_index, parts, (state_qkv, state_out, state_up, state_down, state_ubias, state_vec))
    input_grad = reorder(shard, assign, back_gin, True)
    return (layer_out, input_grad) + updated


def solution(mesh):
    placed = (
        P("shard", "dp", None), P("shard", "dp", None), P(), P(), P(), P(("dp", "shard"), None, None, None),
        P("shard", None), P("shard", None), P("shard", None), P("shard", None), P("shard"), P("shard", None),
        P(None, "shard", None), P(None, "shard", None), P(None, "shard", None), P(None, "shard", None),
        P(None, "shard"), P(None, "shard", None),
    )
    return jax.shard_map(
        on_device,
        mesh=mesh,
        in_specs=placed,
        out_specs=(
            P("shard", "dp", None), P("shard", "dp", None), P("shard", None), P("shard", None), P("shard", None),
            P("shard", None), P("shard"), P("shard", None), P("shard", None), P("shard", None), P("shard", None),
        ),
        check_vma=False,
    )
```

```python
import functools

import jax
import jax.numpy as jnp
from jax import lax
from jax.experimental import pallas as pl
from jax.experimental.pallas import tpu as pltpu
from jax.sharding import PartitionSpec as P

STEP = 1
QUERY_SCALE = 0.125
NORM_EPSILON = 1e-12
LEARNING_RATE = 0.02
WEIGHT_DECAY = 0.01
ADAM_EPSILON = 1e-08
FIRST_BETA = 0.5
SECOND_BETA = 0.5
MASK_VALUE = -1e30
NORMAL_PEAK = 0.3989422804014327

LOW = jnp.bfloat16
F32 = jnp.float32
VMEM_LIMIT = 60 * 1024 * 1024

BLOCK = 64
HALF = 128
GROUP = 31
AHEAD_ROWS = 1024
BEHIND_ROWS = 512
BACK = 10


def dot_nn(a, b):
    return lax.dot_general(a, b, (((1,), (0,)), ((), ())), preferred_element_type=F32)


def dot_nt(a, b):
    return lax.dot_general(a, b, (((1,), (1,)), ((), ())), preferred_element_type=F32)


def dot_tn(a, b):
    return lax.dot_general(a, b, (((0,), (0,)), ((), ())), preferred_element_type=F32)


def first_half(rows):
    return lax.broadcasted_iota(jnp.int32, (rows, HALF), 1) < BLOCK


def spread_heads(rows, picks):
    return jnp.concatenate([rows, rows, rows, rows], axis=0) * picks


def pick_heads(wide):
    low = first_half(BLOCK)
    left = jnp.where(low, wide[0:64, 0:HALF], wide[64:128, 0:HALF])
    right = jnp.where(low, wide[128:192, HALF:], wide[192:256, HALF:])
    return jnp.concatenate([left, right], axis=1)


def head_picks():
    row = lax.broadcasted_iota(jnp.int32, (256, 256), 0) // BLOCK
    col = lax.broadcasted_iota(jnp.int32, (256, 256), 1) // BLOCK
    return jnp.where(row == col, 1.0, 0.0).astype(LOW)


def gather_slot(ref, chosen, tile):
    a, b = chosen[2 * tile], chosen[2 * tile + 1]
    cols = pl.ds(tile * HALF, HALF)
    left = ref[pl.ds(pl.multiple_of(a * BLOCK, BLOCK), BLOCK), cols]
    right = ref[pl.ds(pl.multiple_of(b * BLOCK, BLOCK), BLOCK), cols]
    return jnp.where(first_half(BLOCK), left, right)


def turn_pairs(ref, turned):
    pairs = turned.shape[0] // 2

    def one(j, _):
        pair = ref[:, pl.ds(pl.multiple_of(j * HALF, HALF), HALF)]
        turned[j] = pair
        turned[pairs + j] = jnp.concatenate([pair[:, BLOCK:], pair[:, :BLOCK]], axis=1)
        return 0

    lax.fori_loop(0, pairs, one, 0, unroll=8)


def pick_turned(wide):
    low = first_half(BLOCK)
    left, right = wide[0:HALF, 0:HALF].T, wide[HALF:, HALF:].T
    return jnp.concatenate(
        [jnp.where(low, part[0:BLOCK], part[BLOCK:]) for part in (left, right)], axis=1
    )


class Unit:
    def __init__(self, i, live, drawn, blocks):
        last = live - 1

        def state(b):
            return (b >= last).astype(jnp.int32) + (b > last).astype(jnp.int32)

        after = jnp.minimum(i + 1, blocks - 1)
        self.near = [i - 1, i, after]
        self.near_state = [
            jnp.where(i >= 3, state(i - 1), 2),
            state(i),
            jnp.where(i + 1 < blocks, state(after), 2),
        ]
        self.fixed_state = [state(0 * i), state(0 * i + 1)]
        self.chosen = [
            [drawn[(h * blocks + i) * 3 + s] for h in range(4)] for s in range(3)
        ]
        self.chosen_state = [[state(b) for b in row] for row in self.chosen]

    def bias(self, table, slots):
        rows = []
        for n in slots:
            if n < 5:
                one = table[(self.fixed_state + self.near_state)[n]]
                rows.append(jnp.concatenate([one, one], axis=1))
            else:
                st = self.chosen_state[n - 5]
                low = first_half(BLOCK)
                rows.append(
                    jnp.concatenate(
                        [
                            jnp.where(low, table[st[0]], table[st[1]]),
                            jnp.where(low, table[st[2]], table[st[3]]),
                        ],
                        axis=1,
                    )
                )
        return jnp.concatenate(rows, axis=0)


def chunk_bias(table, live, first, count):
    last = live - 1
    rows = []
    for n in range(count):
        b = first + n
        st = (b >= last).astype(jnp.int32) + (b > last).astype(jnp.int32)
        one = table[st]
        rows.append(jnp.concatenate([one, one], axis=1))
    return jnp.concatenate(rows, axis=0)


def slot_rows(unit, ref):
    near = [ref[pl.ds(pl.multiple_of(b * BLOCK, BLOCK), BLOCK), :] for b in unit.near]
    rand = [jnp.concatenate([gather_slot(ref, unit.chosen[s], t) for t in range(2)], axis=1) for s in range(3)]
    return jnp.concatenate([ref[0:128, :]] + near + rand, axis=0)


def slot_turned(unit, first, turned):
    low = lax.broadcasted_iota(jnp.int32, (BLOCK, HALF), 1) < BLOCK
    every = [[b] * 4 for b in unit.near] + unit.chosen
    pairs = turned.shape[0] // 2
    tiles = [first]
    for n in range(3):
        parts = []
        for h in range(4):
            rows = pl.ds(h * BLOCK, BLOCK)
            a, b = every[2 * n][h], every[2 * n + 1][h]
            left = turned[(a & 1) * pairs + (a >> 1), rows, :]
            right = turned[(1 - (b & 1)) * pairs + (b >> 1), rows, :]
            parts.append(jnp.where(low, left, right))
        tiles.append(jnp.concatenate(parts, axis=0))
    return jnp.concatenate(tiles, axis=1)


def forward_kernel(
    scal, drawn, table, x, w, w_kt, w_vt, shift, shift_vt,
    q_o, k_o, v_o, kt_o, ctx_o, lse_o, picks, q_v, k_v, v_v, kt_v, vt, turned, sg, og, sems,
):
    length = x.shape[0]
    blocks = length // BLOCK
    live = scal[0]
    picks[...] = head_picks()

    def project(c, _):
        rows = pl.ds(pl.multiple_of(c * 512, 512), 512)
        xc = x[rows, :]
        out = (dot_nn(xc, w[...]) + shift[...]).astype(LOW)
        q_v[rows, :] = out[:, 0:256]
        k_v[rows, :] = out[:, 256:512]
        v_v[rows, :] = out[:, 512:768]
        kt_v[:, rows] = dot_nt(w_kt[...], xc).astype(LOW)
        vt[:, rows] = (dot_nt(w_vt[...], xc) + shift_vt[:, 0:1]).astype(LOW)
        return 0

    lax.fori_loop(0, length // 512, project, 0, unroll=2)
    copies = [
        pltpu.make_async_copy(here, there, sems.at[n])
        for n, (here, there) in enumerate(((q_v, q_o), (k_v, k_o), (v_v, v_o), (kt_v, kt_o)))
    ]
    for copy in copies:
        copy.start()
    turn_pairs(vt, turned)

    def group(j, _):
        idx = [2 + GROUP * j + u for u in range(GROUP)]
        units = [Unit(i, live, drawn, blocks) for i in idx]
        rows = [pl.ds(pl.multiple_of(i * BLOCK, BLOCK), BLOCK) for i in idx]
        bd = [spread_heads(q_v[r, :] * jnp.asarray(QUERY_SCALE, LOW), picks[...]) for r in rows]
        every = range(GROUP)
        s = [dot_nt(slot_rows(units[u], k_v), bd[u]) + units[u].bias(table, range(8)) for u in every]
        m = [jnp.max(s[u], axis=0, keepdims=True) for u in every]
        e = [jnp.exp(s[u] - m[u]) for u in every]
        total = [jnp.sum(e[u], axis=0, keepdims=True) for u in every]
        o = [
            dot_nn(slot_turned(units[u], vt[:, 0:128], turned), e[u].astype(LOW)) * (1.0 / total[u]) for u in every
        ]
        for u in every:
            ctx_o[rows[u], :] = pick_turned(o[u]).astype(LOW)
            lse_o[pl.ds(idx[u], 1), :] = m[u] + jnp.log(total[u])
        return 0

    lax.fori_loop(0, (blocks - 2) // GROUP, group, 0)

    bds = [
        spread_heads(q_v[g * 64 : g * 64 + 64, :] * jnp.asarray(QUERY_SCALE, LOW), picks[...]) for g in range(2)
    ]

    def score(c, peaks):
        rows = pl.ds(pl.multiple_of(c * 512, 512), 512)
        bias = chunk_bias(table, live, c * 8, 8)
        out = []
        for g in range(2):
            s = dot_nt(k_v[rows, :], bds[g]) + bias
            sg[g, rows, :] = s
            out.append(jnp.maximum(peaks[g], jnp.max(s, axis=0, keepdims=True)))
        return tuple(out)

    peaks = lax.fori_loop(0, length // 512, score, (jnp.full((1, 256), MASK_VALUE, F32),) * 2, unroll=2)

    og[...] = jnp.zeros_like(og)

    def mix(c, totals):
        rows = pl.ds(pl.multiple_of(c * 512, 512), 512)
        out = []
        for g in range(2):
            e = jnp.exp(sg[g, rows, :] - peaks[g])
            out.append(totals[g] + jnp.sum(e, axis=0, keepdims=True))
            og[g] += dot_nn(vt[:, rows], e.astype(LOW))
        return tuple(out)

    totals = lax.fori_loop(0, length // 512, mix, (jnp.zeros((1, 256), F32),) * 2, unroll=2)
    for g in range(2):
        ctx_o[g * 64 : g * 64 + 64, :] = pick_turned(og[g] * (1.0 / totals[g])).astype(LOW)
        lse_o[g : g + 1, :] = peaks[g] + jnp.log(totals[g])
    for copy in copies:
        copy.wait()


def vmem():
    return pl.BlockSpec(memory_space=pltpu.VMEM)


def smem():
    return pl.BlockSpec(memory_space=pltpu.SMEM)


def forward_attention(scal, drawn, table, x, w, w_kt, w_vt, shift, shift_vt):
    length = x.shape[0]
    blocks = length // BLOCK
    rows = jax.ShapeDtypeStruct((length, 256), LOW)
    return pl.pallas_call(
        forward_kernel,
        out_shape=(
            rows, rows, rows, jax.ShapeDtypeStruct((256, length), LOW), rows, jax.ShapeDtypeStruct((blocks, 256), F32),
        ),
        in_specs=[smem(), smem()] + [vmem()] * 7,
        out_specs=[pl.BlockSpec(memory_space=pl.ANY)] * 4 + [vmem()] * 2,
        scratch_shapes=[
            pltpu.VMEM((256, 256), LOW),
            pltpu.VMEM((length, 256), LOW),
            pltpu.VMEM((length, 256), LOW),
            pltpu.VMEM((length, 256), LOW),
            pltpu.VMEM((256, length), LOW),
            pltpu.VMEM((256, length), LOW),
            pltpu.VMEM((blocks, 256, HALF), LOW),
            pltpu.VMEM((2, length, 256), F32),
            pltpu.VMEM((2, 256, 256), F32),
            pltpu.SemaphoreType.DMA((4,)),
        ],
        compiler_params=pltpu.CompilerParams(vmem_limit_bytes=VMEM_LIMIT),
        cost_estimate=pl.CostEstimate(flops=16_000_000_000, bytes_accessed=12_000_000, transcendentals=10_000_000),
        name="attend_forward",
    )(scal, drawn, table, x, w, w_kt, w_vt, shift, shift_vt)


def normalize(summed):
    center = summed - jnp.mean(summed, axis=-1, keepdims=True)
    return (*scaled(center), center)


def scaled(center):
    factor = lax.rsqrt(jnp.mean(center * center, axis=-1, keepdims=True) + NORM_EPSILON)
    return (center * factor, factor)


def normalize_back(grad_normed, normed, factor):
    return factor * (
        grad_normed
        - jnp.mean(grad_normed, axis=-1, keepdims=True)
        - normed * jnp.mean(grad_normed * normed, axis=-1, keepdims=True)
    )


ROOT_HALF = 0.7071067811865476


def gelu_weight(v):
    return 0.5 * (1.0 + lax.erf(v * ROOT_HALF))


def open_rows(table, scal, rows):
    last = scal[0] - 1
    marks = []
    for n in range(rows // BLOCK):
        b = pl.program_id(0) * (rows // BLOCK) + n
        one = table[(b >= last).astype(jnp.int32) + (b > last).astype(jnp.int32)]
        marks.append(jnp.concatenate([one, one], axis=1))
    return jnp.concatenate(marks, axis=0) == 0.0


def ahead_kernel(scal, table, x, ctx, w_out, w_up, w_down, up_shift, vec, out_o, one_o, two_o, act, slope_o):
    rows = x.shape[0]

    def row(n):
        return vec[n : n + 1, :]

    attended = dot_nn(ctx[...], w_out[...]) + row(2)
    normed_one, _, center = normalize(x[...].astype(F32) + attended)
    one_o[...] = center.astype(LOW)
    first_out = normed_one * row(3) + row(4)
    first_low = first_out.astype(LOW)
    for c in range(0, 1024, 256):
        pre = dot_nn(first_low, w_up[:, c : c + 256]) + up_shift[:, c : c + 256]
        weight = gelu_weight(pre)
        act[:, c : c + 256] = (pre * weight).astype(LOW)
        slope_o[:, c : c + 256] = (weight + pre * (NORMAL_PEAK * jnp.exp(-0.5 * pre * pre))).astype(LOW)
    branch = dot_nn(act[...], w_down[...]) + row(5)
    normed_two, _, center = normalize(first_out + branch)
    two_o[...] = center.astype(LOW)
    out_o[...] = jnp.where(open_rows(table, scal, rows), normed_two * row(6) + row(7), 0.0).astype(LOW)


def ahead(scal, table, x, ctx, w_out, w_up, w_down, up_shift, vec):
    length = x.shape[0]
    rows = AHEAD_ROWS

    def wide(columns):
        return pl.BlockSpec((rows, columns), lambda i, s: (i, 0))

    def whole(*shape):
        return pl.BlockSpec(shape, lambda i, s: (0,) * len(shape))

    shape = jax.ShapeDtypeStruct
    return pl.pallas_call(
        ahead_kernel,
        grid_spec=pltpu.PrefetchScalarGridSpec(
            num_scalar_prefetch=1,
            grid=(length // rows,),
            in_specs=[
                whole(3, 64, 128), wide(256), wide(256), whole(256, 256), whole(256, 1024), whole(1024, 256),
                whole(1, 1024), whole(8, 256),
            ],
            out_specs=[wide(256), wide(256), wide(256), wide(1024), wide(1024)],
        ),
        out_shape=(
            shape((length, 256), LOW), shape((length, 256), LOW), shape((length, 256), LOW),
            shape((length, 1024), LOW), shape((length, 1024), LOW),
        ),
        compiler_params=pltpu.CompilerParams(vmem_limit_bytes=VMEM_LIMIT),
        cost_estimate=pl.CostEstimate(flops=5_000_000_000, bytes_accessed=34_000_000, transcendentals=10_000_000),
        name="ahead",
    )(scal, table, x, ctx, w_out, w_up, w_down, up_shift, vec)


def behind_kernel(
    scal, table, cot, ctx, one, two, act, slope, w_out, w_up, w_down, vec,
    gz1_o, gctx_o, delta_o, pack0, pack1, pack2, pack3, gdown_o, gup_o, gout_o, gub_o, gvec_o, back,
):
    step = pl.program_id(0)
    rows = cot.shape[0]

    @pl.when(step == 0)
    def _():
        for ref in (gdown_o, gup_o, gout_o, gub_o, gvec_o):
            ref[...] = jnp.zeros_like(ref)

    def row(n):
        return vec[n : n + 1, :]

    normed_one, factor_one = scaled(one[...].astype(F32))
    normed_two, factor_two = scaled(two[...].astype(F32))
    first_low = (normed_one * row(3) + row(4)).astype(LOW)
    grad_y = jnp.where(open_rows(table, scal, rows), cot[...].astype(F32), 0.0)
    grad_z2 = normalize_back(grad_y * row(6), normed_two, factor_two)
    grad_branch = grad_z2.astype(LOW)
    for c in range(0, 1024, 256):
        grad_act = dot_nt(grad_branch, w_down[c : c + 256, :])
        grad_pre = (grad_act * slope[:, c : c + 256].astype(F32)).astype(LOW)
        back[:, c : c + 256] = grad_pre
        gub_o[:, c : c + 256] += jnp.sum(grad_pre.astype(F32), axis=0, keepdims=True)
    gdown_o[...] += dot_tn(act[...], grad_branch)
    grad_first = grad_z2 + dot_nt(back[...], w_up[...])
    gup_o[...] += dot_tn(first_low, back[...])
    grad_z1 = normalize_back(grad_first * row(3), normed_one, factor_one)
    gz1_o[...] = grad_z1
    grad_attended = grad_z1.astype(LOW)
    ctx_v = ctx[...]
    gout_o[...] += dot_tn(ctx_v, grad_attended)
    grad_context = dot_nt(grad_attended, w_out[...]).astype(LOW)
    gctx_o[...] = grad_context

    def add(n, values):
        gvec_o[n : n + 1, :] += jnp.sum(values, axis=0, keepdims=True)

    add(2, grad_attended.astype(F32))
    add(3, grad_first * normed_one)
    add(4, grad_first)
    add(5, grad_branch.astype(F32))
    add(6, grad_y * normed_two)
    add(7, grad_y)
    both = ctx_v.astype(F32) * grad_context.astype(F32)
    upper = both.astype(LOW)
    lower = (both - upper.astype(F32)).astype(LOW)
    group = lax.broadcasted_iota(jnp.int32, (8, 256), 1) // BLOCK
    ones = jnp.where(group == lax.broadcasted_iota(jnp.int32, (8, 256), 0), 1.0, 0.0).astype(LOW)
    sums = dot_nt(ones, upper) + dot_nt(ones, lower)
    for n in range(rows // BLOCK):
        part = sums[0:4, n * BLOCK : (n + 1) * BLOCK]
        delta_o[n : n + 1, :] = jnp.concatenate([part[h : h + 1, :] for h in range(4)], axis=1)

    @pl.when(step == pl.num_programs(0) - 1)
    def _():
        for r, pack in enumerate((pack0, pack1, pack2, pack3)):
            piece = scal[1] ^ r
            shard, core = piece // 2, piece % 2
            here = pl.ds(pl.multiple_of(piece * 64, 64), 64)
            pack[:, 0:1024] = gup_o[here, :].astype(LOW)
            pack[:, 1024:1280] = gout_o[here, :].astype(LOW)
            for g in range(4):
                at = pl.ds(pl.multiple_of(shard * 512 + g * 128 + core * 64, 64), 64)
                pack[:, 1280 + 256 * g : 1536 + 256 * g] = gdown_o[at, :].astype(LOW)
            lines = [gub_o[:, pl.ds(pl.multiple_of(shard * 512 + 128 * n, 128), 128)] for n in range(4)]
            first = shard == 0
            for n in range(4):
                line = jnp.where(first, gvec_o[n : n + 1, :], gvec_o[4 + n : 5 + n, :])
                lines += [line[:, 0:128], line[:, 128:256]]
            put_extra(pack, 2304, lines, core)


def put_extra(pack, at, lines, core):
    some = jnp.concatenate(lines + [jnp.zeros((16 - len(lines), HALF), F32)], axis=0)
    pack[0:16, at : at + HALF] = jnp.where(core == 0, some, 0.0).astype(LOW)
    pack[16:64, at : at + HALF] = jnp.zeros((48, HALF), LOW)


def behind(scal, table, cot, ctx, one, two, act, slope, w_out, w_up, w_down, vec):
    length = cot.shape[0]
    rows = BEHIND_ROWS

    def wide(columns):
        return pl.BlockSpec((rows, columns), lambda i, s: (i, 0))

    def whole(*shape):
        return pl.BlockSpec(shape, lambda i, s: (0,) * len(shape))

    shape = jax.ShapeDtypeStruct
    return pl.pallas_call(
        behind_kernel,
        grid_spec=pltpu.PrefetchScalarGridSpec(
            num_scalar_prefetch=1,
            grid=(length // rows,),
            in_specs=[
                whole(3, 64, 128), wide(256), wide(256), wide(256), wide(256), wide(1024), wide(1024),
                whole(256, 256), whole(256, 1024), whole(1024, 256), whole(8, 256),
            ],
            out_specs=[
                wide(256), wide(256), pl.BlockSpec((rows // BLOCK, 256), lambda i, s: (i, 0)),
                whole(64, 2432), whole(64, 2432), whole(64, 2432), whole(64, 2432),
            ],
            scratch_shapes=[
                pltpu.VMEM((1024, 256), F32), pltpu.VMEM((256, 1024), F32), pltpu.VMEM((256, 256), F32),
                pltpu.VMEM((1, 1024), F32), pltpu.VMEM((8, 256), F32), pltpu.VMEM((rows, 1024), LOW),
            ],
        ),
        out_shape=(
            shape((length, 256), F32), shape((length, 256), LOW), shape((length // BLOCK, 256), F32),
        ) + (shape((64, 2432), LOW),) * 4,
        compiler_params=pltpu.CompilerParams(vmem_limit_bytes=VMEM_LIMIT),
        cost_estimate=pl.CostEstimate(flops=10_000_000_000, bytes_accessed=40_000_000, transcendentals=0),
        name="behind",
    )(scal, table, cot, ctx, one, two, act, slope, w_out, w_up, w_down, vec)


def backward_kernel(
    scal, drawn, table, q, k, v, kt, gctx, lse, delta, gz1, x, w,
    gin_o, pack0, pack1, pack2, pack3, picks, turned, dqg, dq, dk, dv, gw_o, gz1_v, x_v, gin_v, sems,
):
    length = x.shape[0]
    blocks = length // BLOCK
    live = scal[0]
    picks[...] = head_picks()
    dk[...] = jnp.zeros_like(dk)
    dv[...] = jnp.zeros_like(dv)
    loads = [pltpu.make_async_copy(gz1, gz1_v, sems.at[0]), pltpu.make_async_copy(x, x_v, sems.at[1])]
    for load in loads:
        load.start()
    turn_pairs(kt, turned)

    def spread(i):
        rows = pl.ds(pl.multiple_of(i * BLOCK, BLOCK), BLOCK)
        bdq = spread_heads(q[rows, :] * jnp.asarray(QUERY_SCALE, LOW), picks[...])
        bdo = spread_heads(gctx[rows, :], picks[...])
        return rows, bdq, bdo

    def group(idx):
        units = [Unit(i, live, drawn, blocks) for i in idx]
        spreads = [spread(i) for i in idx]
        low = first_half(BLOCK)
        s, g, p, ds, dvs, dks, dqs = {}, {}, {}, {}, {}, {}, {}
        count = len(idx)
        for t in range(count + 1):
            u = t - 0
            if 0 <= u < count:
                s[u] = dot_nt(slot_rows(units[u], k), spreads[u][1])
            u = t - 0
            if 0 <= u < count:
                g[u] = dot_nt(slot_rows(units[u], v), spreads[u][2])
            u = t - 0
            if 0 <= u < count:
                e = jnp.exp(s[u] + units[u].bias(table, range(8)) - lse[pl.ds(idx[u], 1), :])
                ds[u] = (e * (g[u] - delta[pl.ds(idx[u], 1), :])).astype(LOW)
                p[u] = e.astype(LOW)
            u = t - 0
            if 0 <= u < count:
                dvs[u] = dot_nn(p[u], spreads[u][2])
                dks[u] = dot_nn(ds[u], spreads[u][1])
                dqs[u] = dot_nn(slot_turned(units[u], kt[:, 0:128], turned), ds[u])
            u = t - 1
            if 0 <= u < count:
                for acc, terms_ in ((dk, dks[u]), (dv, dvs[u])):
                    acc[0:128, :] += terms_[0:128, :]
                    for n in range(2, 8):
                        one = terms_[n * 64 : n * 64 + 64, :]
                        if n < 5:
                            at = pl.ds(pl.multiple_of(units[u].near[n - 2] * BLOCK, BLOCK), BLOCK)
                            acc[at, :] += one
                        else:
                            for h in range(4):
                                t_ = h // 2
                                at = pl.ds(pl.multiple_of(units[u].chosen[n - 5][h] * BLOCK, BLOCK), BLOCK)
                                cols = pl.ds(t_ * HALF, HALF)
                                mine = low if h % 2 == 0 else jnp.logical_not(low)
                                acc[at, cols] += jnp.where(mine, one[:, t_ * HALF : t_ * HALF + HALF], 0.0)
                dq[spreads[u][0], :] = (pick_turned(dqs[u]) * QUERY_SCALE).astype(LOW)

    def several(j, _):
        group([2 + BACK * j + u for u in range(BACK)])
        return 0

    lax.fori_loop(0, (blocks - 2) // BACK, several, 0)
    if (blocks - 2) % BACK:
        group([live * 0 + i for i in range(blocks - (blocks - 2) % BACK, blocks)])

    spreads = [spread(g)[1:] for g in range(2)]
    dqg[...] = jnp.zeros_like(dqg)

    def chunk(c, _):
        at = pl.ds(pl.multiple_of(c * 512, 512), 512)
        bias = chunk_bias(table, live, c * 8, 8)
        kh, vh, th = k[at, :], v[at, :], kt[:, at]
        two = range(2)
        s = [dot_nt(kh, spreads[g][0]) for g in two]
        t = [dot_nt(vh, spreads[g][1]) for g in two]
        p = [jnp.exp(s[g] + bias - lse[g : g + 1, :]) for g in two]
        ds = [(p[g] * (t[g] - delta[g : g + 1, :])).astype(LOW) for g in two]
        dvs = [dot_nn(p[g].astype(LOW), spreads[g][1]) for g in two]
        dks = [dot_nn(ds[g], spreads[g][0]) for g in two]
        for g in two:
            dqg[g] += dot_nn(th, ds[g])
        dv[at, :] += dvs[0] + dvs[1]
        dk[at, :] += dks[0] + dks[1]
        return 0

    lax.fori_loop(0, length // 512, chunk, 0, unroll=2)
    for g in range(2):
        dq[g * 64 : g * 64 + 64, :] = (pick_turned(dqg[g]) * QUERY_SCALE).astype(LOW)

    gw_o[...] = jnp.zeros_like(gw_o)
    for load in loads:
        load.wait()

    def finish(c, shifts):
        rows = pl.ds(pl.multiple_of(c * 512, 512), 512)
        dqkv = jnp.concatenate([dq[rows, :], dk[rows, :].astype(LOW), dv[rows, :].astype(LOW)], axis=1)
        gin_v[rows, :] = (gz1_v[rows, :] + dot_nt(dqkv, w[...])).astype(LOW)
        gw_o[...] += dot_tn(x_v[rows, :], dqkv)
        return shifts + jnp.sum(dqkv.astype(F32), axis=0, keepdims=True)

    shifts = lax.fori_loop(0, length // 512, finish, jnp.zeros((1, 768), F32))
    store = pltpu.make_async_copy(gin_v, gin_o, sems.at[2])
    store.start()
    for r, pack in enumerate((pack0, pack1, pack2, pack3)):
        piece = scal[1] ^ r
        core = piece % 2
        pack[:, 0:768] = gw_o[pl.ds(pl.multiple_of(piece * 64, 64), 64), :].astype(LOW)
        mine = jnp.where(piece // 2 == 0, shifts, 0.0)
        lines = [jnp.zeros((4, HALF), F32)] + [mine[:, a : a + HALF] for a in (0, 128, 512, 640)]
        lines += [jnp.zeros((8, HALF), F32)]
        pack[:, 768:896] = jnp.zeros((64, HALF), LOW)
        pack[0:16, 768:896] = jnp.where(core == 0, jnp.concatenate(lines, axis=0), 0.0).astype(LOW)
    store.wait()


def backward_attention(scal, drawn, table, q, k, v, kt, gctx, lse, delta, gz1, x, w):
    length = x.shape[0]
    shape = jax.ShapeDtypeStruct
    return pl.pallas_call(
        backward_kernel,
        out_shape=(shape((length, 256), LOW),) + (shape((64, 896), LOW),) * 4,
        in_specs=[smem(), smem()] + [vmem()] * 8 + [pl.BlockSpec(memory_space=pl.ANY)] * 2 + [vmem()],
        out_specs=[pl.BlockSpec(memory_space=pl.ANY)] + [vmem()] * 4,
        scratch_shapes=[
            pltpu.VMEM((256, 256), LOW),
            pltpu.VMEM((length // BLOCK, 256, HALF), LOW),
            pltpu.VMEM((2, 256, 256), F32),
            pltpu.VMEM((length, 256), LOW),
            pltpu.VMEM((length, 256), F32),
            pltpu.VMEM((length, 256), F32),
            pltpu.VMEM((256, 768), F32),
            pltpu.VMEM((length, 256), F32),
            pltpu.VMEM((length, 256), LOW),
            pltpu.VMEM((length, 256), LOW),
            pltpu.SemaphoreType.DMA((3,)),
        ],
        compiler_params=pltpu.CompilerParams(vmem_limit_bytes=VMEM_LIMIT),
        cost_estimate=pl.CostEstimate(flops=40_000_000_000, bytes_accessed=20_000_000, transcendentals=10_000_000),
        name="attend_backward",
    )(scal, drawn, table, q, k, v, kt, gctx, lse, delta, gz1, x, w)


def bias_table(tail):
    column = jnp.stack([jnp.zeros_like(tail, F32), jnp.where(tail == 1, 0.0, MASK_VALUE), jnp.full(tail.shape, MASK_VALUE, F32)])
    return jnp.broadcast_to(column[:, :, None], (3, BLOCK, HALF))


def reorder_kernel(scatter, where, assign, src, *rest):
    *_, dst, held, arrived, left = rest
    count = src.shape[0]
    shards = assign.shape[0] // count
    loads, stores = [], []
    for j in range(count):
        one = assign[shards * j + where[0]]
        loads.append(pltpu.make_async_copy(src.at[j if scatter else one], held.at[j], arrived.at[j]))
        stores.append(pltpu.make_async_copy(held.at[j], dst.at[one if scatter else j], left.at[j]))
        loads[-1].start()
    for load, store in zip(loads, stores):
        load.wait()
        store.start()
    for store in stores:
        store.wait()


def reorder(shard, assign, src, scatter, after=()):
    return pl.pallas_call(
        functools.partial(reorder_kernel, scatter),
        out_shape=jax.ShapeDtypeStruct(src.shape, src.dtype),
        in_specs=[smem(), smem(), pl.BlockSpec(memory_space=pltpu.HBM)]
        + [pl.BlockSpec(memory_space=pltpu.HBM)] * len(after),
        out_specs=pl.BlockSpec(memory_space=pltpu.HBM),
        scratch_shapes=[
            pltpu.VMEM(src.shape, src.dtype),
            pltpu.SemaphoreType.DMA((src.shape[0],)),
            pltpu.SemaphoreType.DMA((src.shape[0],)),
        ],
        compiler_params=pltpu.CompilerParams(vmem_limit_bytes=VMEM_LIMIT),
        cost_estimate=pl.CostEstimate(flops=0, bytes_accessed=4 * src.size, transcendentals=0),
        name="reorder",
    )(shard, assign, src, *after)


def hold(values, after):
    count = len(values)
    anywhere = pl.BlockSpec(memory_space=pltpu.HBM)
    return pl.pallas_call(
        lambda *refs: None,
        out_shape=tuple(jax.ShapeDtypeStruct(v.shape, v.dtype) for v in values),
        in_specs=[anywhere] * (count + len(after)),
        out_specs=(anywhere,) * count,
        input_output_aliases={n: n for n in range(count)},
        name="hold",
    )(*values, *after)


def pack_kernel(w_qkv, w_out, w_up, w_down, up_bias, vectors, after, out):
    rows = w_qkv.shape[0]
    out[0:rows, 0:768] = w_qkv[...]
    out[0:rows, 768:1024] = w_out[...]
    out[0:rows, 1024:2048] = w_up[...]
    for n in range(4):
        out[0:rows, 2048 + 256 * n : 2304 + 256 * n] = w_down[rows * n : rows * (n + 1), :]
    lines = [up_bias[...].astype(F32)] + [vectors[n : n + 1, :].astype(F32) for n in range(4)]
    line = jnp.concatenate(lines + [jnp.zeros((1, 3072 - 1536), F32)], axis=1)
    out[rows : rows + 16, :] = jnp.broadcast_to(line, (16, 3072)).astype(LOW)


def pack_weights(parts, after):
    w_qkv, w_out, w_up, w_down, up_bias, vectors = parts
    return pl.pallas_call(
        pack_kernel,
        out_shape=jax.ShapeDtypeStruct((w_qkv.shape[0] + 16, 3072), LOW),
        in_specs=[vmem()] * 6 + [pl.BlockSpec(memory_space=pltpu.HBM)],
        out_specs=vmem(),
        compiler_params=pltpu.CompilerParams(vmem_limit_bytes=VMEM_LIMIT),
        name="pack_weights",
    )(w_qkv, w_out, w_up, w_down, up_bias.reshape(1, -1), vectors, after)


def unpack_kernel(shard, own, got, w_qkv, w_out, w_up, w_down, w_kt, w_vt, up_shift, vec, shift, shift_vt):
    rows = own.shape[0] - 16
    first = shard[0] == 0

    def half(n, at, cols):
        mine, other = own[at, cols], got[at, cols]
        return jnp.where(first == (n == 0), mine, other)

    for n in range(2):
        here = slice(n * rows, (n + 1) * rows)
        w_qkv[here, :] = half(n, slice(0, rows), slice(0, 768))
        w_out[here, :] = half(n, slice(0, rows), slice(768, 1024))
        w_up[here, :] = half(n, slice(0, rows), slice(1024, 2048))
        for g in range(4):
            at = (4 * n + g) * rows
            w_down[at : at + rows, :] = half(n, slice(0, rows), slice(2048 + 256 * g, 2304 + 256 * g))
        line = half(n, slice(rows, rows + 16), slice(0, 1536)).astype(F32)[0:1]
        up_shift[:, 512 * n : 512 * n + 512] = line[:, 0:512]
        for g in range(4):
            vec[4 * n + g : 4 * n + g + 1, :] = line[:, 512 + 256 * g : 768 + 256 * g]
    shift[...] = jnp.concatenate([vec[0:1, :], jnp.zeros((1, 256), F32), vec[1:2, :]], axis=1)
    w_kt[...] = w_qkv[:, 256:512].astype(F32).T.astype(LOW)
    w_vt[...] = w_qkv[:, 512:768].astype(F32).T.astype(LOW)
    shift_vt[...] = jnp.broadcast_to(vec[1:2, :], (HALF, 256)).T


def unpack_weights(shard, own, got):
    shape = jax.ShapeDtypeStruct
    return pl.pallas_call(
        unpack_kernel,
        out_shape=(
            shape((256, 768), LOW), shape((256, 256), LOW), shape((256, 1024), LOW), shape((1024, 256), LOW),
            shape((256, 256), LOW), shape((256, 256), LOW), shape((1, 1024), F32), shape((8, 256), F32),
            shape((1, 768), F32), shape((256, HALF), F32),
        ),
        in_specs=[smem(), vmem(), vmem()],
        out_specs=[vmem()] * 10,
        compiler_params=pltpu.CompilerParams(vmem_limit_bytes=VMEM_LIMIT),
        name="unpack_weights",
    )(shard, own, got)


def trade(pieces):
    count = lax.axis_size("dp")
    held = [pieces[0]]
    for n in (1, 2, 3):
        pairs = [(d * 2 + s, (d ^ (n % 2)) * 2 + (s ^ (n // 2))) for d in range(count) for s in range(2)]
        held.append(lax.ppermute(pieces[n], ("dp", "shard"), pairs))
    return held


def total(pieces):
    return sum(piece.astype(F32) for piece in pieces)


def sum_rest(part, data_index):
    count = lax.axis_size("dp")
    groups = count // 4
    half = part.shape[0] // 2
    bit = (data_index // 2) % 2
    flip = [(d, d ^ 2) for d in range(count)]
    keep = lax.dynamic_slice_in_dim(part, bit * half, half, 0)
    give = lax.dynamic_slice_in_dim(part, (1 - bit) * half, half, 0)
    part = keep + lax.ppermute(give.astype(LOW), "dp", flip).astype(F32)
    at = data_index // 4
    small = half // groups
    hops = [[(d, (d + 4 * k) % count) for d in range(count)] for k in range(1, groups)]

    def piece(k):
        return lax.dynamic_slice_in_dim(part, lax.rem(at + k, groups) * small, small, 0)

    mine = piece(0)
    got = [lax.ppermute(piece(k + 1).astype(LOW), "dp", hop) for k, hop in enumerate(hops)]
    for one in got:
        mine = mine + one.astype(F32)
    return mine.astype(LOW)


def spread_sums(mine):
    count = lax.axis_size("dp")
    flip = [(d, d ^ 2) for d in range(count)]
    hops = [[(d, (d + 4 * k) % count) for d in range(count)] for k in range(1, count // 4)]
    near = jnp.stack([mine] + [lax.ppermute(mine, "dp", hop) for hop in hops])
    core = [(d, d ^ 1) for d in range(count)]
    across = lax.ppermute(near, "dp", flip)
    return near, across, lax.ppermute(near, "dp", core), lax.ppermute(across, "dp", core)


def adam_update(grad, state, decay):
    correct_one = 1.0 - FIRST_BETA**STEP
    correct_two = 1.0 - SECOND_BETA**STEP
    first_new = FIRST_BETA * state[1] + (1.0 - FIRST_BETA) * grad
    second_new = SECOND_BETA * state[2] + (1.0 - SECOND_BETA) * grad * grad
    direction = first_new / correct_one / (jnp.sqrt(second_new / correct_two) + ADAM_EPSILON)
    master_new = state[0] - LEARNING_RATE * (direction + decay * state[0])
    return (master_new, first_new, second_new)


def update_kernel(
    where, near, across, near_core, across_core, s_qkv, s_out, s_up, s_down, s_bias, s_vec, done_out, done_grad,
    g_qkv, g_out, g_up, g_down, g_bias, g_vec, o_master, o_first, o_second, grads, flat, sems,
):
    groups, small = near.shape[:2]
    parts = (near, across, near_core, across_core)
    index = where[0]
    for core in range(2):
        for side in range(2):
            base = ((index % 2) ^ core) * 64 + (((index // 2) % 2) ^ side) * 32
            for k in range(groups):
                at = base + lax.rem(index // 4 + groups - k, groups) * small
                grads[pl.ds(pl.multiple_of(at, small), small), :] = parts[2 * core + side][k].astype(F32)
    outs = [flat.at[n] for n in range(3)]

    def place(base, grad, state, decay):
        rows, columns = grad.shape
        wide = columns // HALF
        for out, value in zip(outs, adam_update(grad, state, decay)):
            for c in range(wide):
                at = pl.ds(base + c, rows, stride=wide) if wide > 1 else pl.ds(base, rows)
                out[at, :] = value[:, c * HALF : (c + 1) * HALF]

    qkv, outer, up = grads[:, 2304:3072], grads[:, 1024:1280], grads[:, 0:1024]
    g_qkv[...] = qkv
    g_out[...] = outer
    g_up[...] = up
    place(0, qkv, s_qkv, WEIGHT_DECAY)
    place(768, outer, s_out, WEIGHT_DECAY)
    place(1024, up, s_up, WEIGHT_DECAY)
    for n in range(4):
        rows = slice(128 * n, 128 * n + 128)
        down = grads[:, 1280 + 256 * n : 1536 + 256 * n]
        g_down[rows, :] = down
        place(2048 + 256 * n, down, s_down[:, rows, :], WEIGHT_DECAY)
    extra = grads[0:16, 3072:3200]
    g_bias[...] = extra[0:4]
    place(3072, extra[0:4], s_bias, 0.0)
    vec = jnp.concatenate(
        [jnp.concatenate([extra[4 + 2 * n : 5 + 2 * n], extra[5 + 2 * n : 6 + 2 * n]], axis=1) for n in range(4)], axis=0
    )
    g_vec[...] = vec
    place(3076, vec, s_vec, 0.0)
    copies = [
        pltpu.make_async_copy(flat.at[n], there.reshape(flat.shape[1:]), sems.at[n])
        for n, there in enumerate((o_master, o_first, o_second))
    ]
    for copy in copies:
        copy.start()
    for copy in copies:
        copy.wait()


def update(data_index, parts, states, after):
    shape = lambda *dims: jax.ShapeDtypeStruct(dims, F32)
    s_qkv, s_out, s_up, s_down, s_bias, s_vec = states
    flat = shape(1, 3084 * HALF)
    *grads, master, first, second = pl.pallas_call(
        update_kernel,
        out_shape=(
            shape(128, 768), shape(128, 256), shape(128, 1024), shape(512, 256), shape(4, HALF), shape(4, 256),
            flat, flat, flat,
        ),
        in_specs=[smem()] + [vmem()] * 10 + [pl.BlockSpec(memory_space=pltpu.HBM)] * 2,
        out_specs=[vmem()] * 6 + [pl.BlockSpec(memory_space=pltpu.HBM)] * 3,
        scratch_shapes=[
            pltpu.VMEM((128, 3200), F32), pltpu.VMEM((3, 3084, HALF), F32), pltpu.SemaphoreType.DMA((3,)),
        ],
        compiler_params=pltpu.CompilerParams(vmem_limit_bytes=VMEM_LIMIT),
        cost_estimate=pl.CostEstimate(flops=10_000_000, bytes_accessed=14_000_000, transcendentals=400_000),
        name="update",
    )(data_index.reshape(1), *parts, s_qkv, s_out, s_up, s_down, s_bias.reshape(3, 4, HALF), s_vec, *after)
    grads[4] = grads[4].reshape(-1)
    return tuple(grads) + (master, first, second)


def on_device(
    hidden, cotangent, assign, live_blocks, tail_live, random_blocks, w_qkv, w_out, w_up, w_down, up_bias, vectors,
    state_qkv, state_out, state_up, state_down, state_ubias, state_vec,
):
    shard_count = lax.axis_size("shard")
    shard_index = lax.axis_index("shard")
    data_index = lax.axis_index("dp")
    row_seqs, rows_here, width = hidden.shape
    length = row_seqs * rows_here
    shard = shard_index.reshape(1)

    def to_slot(rows):
        return lax.all_to_all(rows, "dp", split_axis=0, concat_axis=0, tiled=True).reshape(length, width)

    sent = reorder(shard, assign, hidden, False)
    x = to_slot(sent)
    pack = pack_weights((w_qkv, w_out, w_up, w_down, up_bias, vectors), sent)
    got = lax.ppermute(pack, "shard", [(0, 1), (1, 0)])
    w_qkv, w_out, w_up, w_down, w_kt, w_vt, up_shift, vec, shift, shift_vt = unpack_weights(shard, pack, got)
    slot = assign[data_index * shard_count + shard_index]
    own = shard_index * row_seqs + slot
    scal = jnp.stack([live_blocks[own], 2 * shard_index + data_index % 2])
    table = bias_table(lax.dynamic_index_in_dim(tail_live, own, 0, keepdims=False))
    drawn = random_blocks.reshape(-1)
    ready = (w_qkv, scal, table, drawn)
    cot = to_slot(reorder(shard, assign, cotangent, False, ready))
    q, k, v, kt, ctx, lse = forward_attention(scal, drawn, table, x, w_qkv, w_kt, w_vt, shift, shift_vt)
    out, *kept = ahead(scal, table, x, ctx, w_out, w_up, w_down, up_shift, vec)

    def from_slot(rows):
        return lax.all_to_all(
            rows.reshape(row_seqs, rows_here, width), "dp", split_axis=0, concat_axis=0, tiled=True
        )

    back_out = from_slot(out)
    gz1, gctx, delta, *early = behind(scal, table, cot, ctx, *kept, w_out, w_up, w_down, vec)
    early = trade(early)
    gin, *late = backward_attention(scal, drawn, table, q, k, v, kt, gctx, lse, delta, gz1, x, w_qkv)
    gin, *late = hold((gin, *late), (back_out, *early[1:]))
    back_gin = from_slot(gin)

    def sum_all(early, late):
        early, late = total(early), total(trade(late))
        sums = jnp.concatenate([early[:, :2304], late[:, :768], early[:, 2304:] + late[:, 768:]], axis=1)
        return sum_rest(sums, data_index)

    made = jax.eval_shape(sum_all, early, late)
    mine = lax.cond(live_blocks[0] > 0, sum_all, lambda *unused: jnp.zeros(made.shape, made.dtype), early, late)
    parts = spread_sums(mine)
    layer_out = reorder(shard, assign, back_out, True, (mine,))
    input_grad = reorder(shard, assign, back_gin, True, (parts[0],))
    states = (state_qkv, state_out, state_up, state_down, state_ubias, state_vec)
    updated = update(data_index, parts, states, (layer_out, input_grad))
    return (layer_out, input_grad) + updated


def solution(mesh):
    placed = (
        P("shard", "dp", None), P("shard", "dp", None), P(), P(), P(), P(("dp", "shard"), None, None, None),
        P("shard", None), P("shard", None), P("shard", None), P("shard", None), P("shard"), P("shard", None),
        P(None, "shard", None), P(None, "shard", None), P(None, "shard", None), P(None, "shard", None),
        P(None, "shard"), P(None, "shard", None),
    )
    return jax.shard_map(
        on_device,
        mesh=mesh,
        in_specs=placed,
        out_specs=(
            P("shard", "dp", None), P("shard", "dp", None), P("shard", None), P("shard", None), P("shard", None),
            P("shard", None), P("shard"), P("shard", None), P("shard", None), P("shard", None), P("shard", None),
        ),
        check_vma=False,
    )
```

```python
import functools

import jax
import jax.numpy as jnp
from jax import lax
from jax.experimental import pallas as pl
from jax.experimental.pallas import tpu as pltpu
from jax.sharding import PartitionSpec as P

STEP = 1
QUERY_SCALE = 0.125
NORM_EPSILON = 1e-12
LEARNING_RATE = 0.02
WEIGHT_DECAY = 0.01
ADAM_EPSILON = 1e-08
FIRST_BETA = 0.5
SECOND_BETA = 0.5
MASK_VALUE = -1e30
NORMAL_PEAK = 0.3989422804014327

LOW = jnp.bfloat16
F32 = jnp.float32
VMEM_LIMIT = 60 * 1024 * 1024

BLOCK = 64
HALF = 128
GROUP = 31
AHEAD_ROWS = 1024
BEHIND_ROWS = 512
BACK = 10


def dot_nn(a, b):
    return lax.dot_general(a, b, (((1,), (0,)), ((), ())), preferred_element_type=F32)


def dot_nt(a, b):
    return lax.dot_general(a, b, (((1,), (1,)), ((), ())), preferred_element_type=F32)


def dot_tn(a, b):
    return lax.dot_general(a, b, (((0,), (0,)), ((), ())), preferred_element_type=F32)


def first_half(rows):
    return lax.broadcasted_iota(jnp.int32, (rows, HALF), 1) < BLOCK


def spread_heads(rows, picks):
    return jnp.concatenate([rows, rows, rows, rows], axis=0) * picks


def pick_heads(wide):
    low = first_half(BLOCK)
    left = jnp.where(low, wide[0:64, 0:HALF], wide[64:128, 0:HALF])
    right = jnp.where(low, wide[128:192, HALF:], wide[192:256, HALF:])
    return jnp.concatenate([left, right], axis=1)


def head_picks():
    row = lax.broadcasted_iota(jnp.int32, (256, 256), 0) // BLOCK
    col = lax.broadcasted_iota(jnp.int32, (256, 256), 1) // BLOCK
    return jnp.where(row == col, 1.0, 0.0).astype(LOW)


def gather_slot(ref, chosen, tile):
    a, b = chosen[2 * tile], chosen[2 * tile + 1]
    cols = pl.ds(tile * HALF, HALF)
    left = ref[pl.ds(pl.multiple_of(a * BLOCK, BLOCK), BLOCK), cols]
    right = ref[pl.ds(pl.multiple_of(b * BLOCK, BLOCK), BLOCK), cols]
    return jnp.where(first_half(BLOCK), left, right)


def turn_pairs(ref, turned):
    pairs = turned.shape[0] // 2

    def one(j, _):
        pair = ref[:, pl.ds(pl.multiple_of(j * HALF, HALF), HALF)]
        turned[j] = pair
        turned[pairs + j] = jnp.concatenate([pair[:, BLOCK:], pair[:, :BLOCK]], axis=1)
        return 0

    lax.fori_loop(0, pairs, one, 0, unroll=8)


def pick_turned(wide):
    low = first_half(BLOCK)
    left, right = wide[0:HALF, 0:HALF].T, wide[HALF:, HALF:].T
    return jnp.concatenate(
        [jnp.where(low, part[0:BLOCK], part[BLOCK:]) for part in (left, right)], axis=1
    )


class Unit:
    def __init__(self, i, live, drawn, blocks):
        last = live - 1

        def state(b):
            return (b >= last).astype(jnp.int32) + (b > last).astype(jnp.int32)

        after = jnp.minimum(i + 1, blocks - 1)
        self.near = [i - 1, i, after]
        self.near_state = [
            jnp.where(i >= 3, state(i - 1), 2),
            state(i),
            jnp.where(i + 1 < blocks, state(after), 2),
        ]
        self.fixed_state = [state(0 * i), state(0 * i + 1)]
        self.chosen = [
            [drawn[(h * blocks + i) * 3 + s] for h in range(4)] for s in range(3)
        ]
        self.chosen_state = [[state(b) for b in row] for row in self.chosen]

    def bias(self, table, slots):
        rows = []
        for n in slots:
            if n < 5:
                one = table[(self.fixed_state + self.near_state)[n]]
                rows.append(jnp.concatenate([one, one], axis=1))
            else:
                st = self.chosen_state[n - 5]
                low = first_half(BLOCK)
                rows.append(
                    jnp.concatenate(
                        [
                            jnp.where(low, table[st[0]], table[st[1]]),
                            jnp.where(low, table[st[2]], table[st[3]]),
                        ],
                        axis=1,
                    )
                )
        return jnp.concatenate(rows, axis=0)


def masked(scores, bias):
    return jnp.concatenate([scores[0:HALF], scores[HALF:] + bias], axis=0)


def chunk_bias(table, live, first, count):
    last = live - 1
    rows = []
    for n in range(count):
        b = first + n
        st = (b >= last).astype(jnp.int32) + (b > last).astype(jnp.int32)
        one = table[st]
        rows.append(jnp.concatenate([one, one], axis=1))
    return jnp.concatenate(rows, axis=0)


def slot_rows(unit, ref):
    near = [ref[pl.ds(pl.multiple_of(b * BLOCK, BLOCK), BLOCK), :] for b in unit.near]
    rand = [jnp.concatenate([gather_slot(ref, unit.chosen[s], t) for t in range(2)], axis=1) for s in range(3)]
    return jnp.concatenate([ref[0:128, :]] + near + rand, axis=0)


def slot_turned(unit, first, turned):
    low = lax.broadcasted_iota(jnp.int32, (BLOCK, HALF), 1) < BLOCK
    every = [[b] * 4 for b in unit.near] + unit.chosen
    pairs = turned.shape[0] // 2
    tiles = [first]
    for n in range(3):
        parts = []
        for h in range(4):
            rows = pl.ds(h * BLOCK, BLOCK)
            a, b = every[2 * n][h], every[2 * n + 1][h]
            left = turned[(a & 1) * pairs + (a >> 1), rows, :]
            right = turned[(1 - (b & 1)) * pairs + (b >> 1), rows, :]
            parts.append(jnp.where(low, left, right))
        tiles.append(jnp.concatenate(parts, axis=0))
    return jnp.concatenate(tiles, axis=1)


def forward_kernel(
    scal, drawn, table, x, w, w_kt, w_vt, shift, shift_vt,
    q_o, k_o, v_o, kt_o, ctx_o, lse_o, picks, q_v, k_v, v_v, kt_v, vt, turned, sg, og, sems,
):
    length = x.shape[0]
    blocks = length // BLOCK
    live = scal[0]
    picks[...] = head_picks()

    def project(c, _):
        rows = pl.ds(pl.multiple_of(c * 512, 512), 512)
        xc = x[rows, :]
        out = (dot_nn(xc, w[...]) + shift[...]).astype(LOW)
        q_v[rows, :] = out[:, 0:256]
        k_v[rows, :] = out[:, 256:512]
        v_v[rows, :] = out[:, 512:768]
        kt_v[:, rows] = dot_nt(w_kt[...], xc).astype(LOW)
        vt[:, rows] = (dot_nt(w_vt[...], xc) + shift_vt[:, 0:1]).astype(LOW)
        return 0

    lax.fori_loop(0, length // 512, project, 0, unroll=2)
    copies = [
        pltpu.make_async_copy(here, there, sems.at[n])
        for n, (here, there) in enumerate(((q_v, q_o), (k_v, k_o), (v_v, v_o), (kt_v, kt_o)))
    ]
    for copy in copies:
        copy.start()
    turn_pairs(vt, turned)

    def group(j, _):
        idx = [2 + GROUP * j + u for u in range(GROUP)]
        units = [Unit(i, live, drawn, blocks) for i in idx]
        rows = [pl.ds(pl.multiple_of(i * BLOCK, BLOCK), BLOCK) for i in idx]
        bd = [spread_heads(q_v[r, :] * jnp.asarray(QUERY_SCALE, LOW), picks[...]) for r in rows]
        every = range(GROUP)
        s = [masked(dot_nt(slot_rows(units[u], k_v), bd[u]), units[u].bias(table, range(2, 8))) for u in every]
        m = [jnp.max(s[u], axis=0, keepdims=True) for u in every]
        e = [jnp.exp(s[u] - m[u]) for u in every]
        total = [jnp.sum(e[u], axis=0, keepdims=True) for u in every]
        o = [
            dot_nn(slot_turned(units[u], vt[:, 0:128], turned), e[u].astype(LOW)) * (1.0 / total[u]) for u in every
        ]
        for u in every:
            ctx_o[rows[u], :] = pick_turned(o[u]).astype(LOW)
            lse_o[pl.ds(idx[u], 1), :] = m[u] + jnp.log(total[u])
        return 0

    lax.fori_loop(0, (blocks - 2) // GROUP, group, 0)

    bds = [
        spread_heads(q_v[g * 64 : g * 64 + 64, :] * jnp.asarray(QUERY_SCALE, LOW), picks[...]) for g in range(2)
    ]

    def score(c, peaks):
        rows = pl.ds(pl.multiple_of(c * 512, 512), 512)
        bias = chunk_bias(table, live, c * 8, 8)
        out = []
        for g in range(2):
            s = dot_nt(k_v[rows, :], bds[g]) + bias
            sg[g, rows, :] = s
            out.append(jnp.maximum(peaks[g], jnp.max(s, axis=0, keepdims=True)))
        return tuple(out)

    peaks = lax.fori_loop(0, length // 512, score, (jnp.full((1, 256), MASK_VALUE, F32),) * 2, unroll=2)

    og[...] = jnp.zeros_like(og)

    def mix(c, totals):
        rows = pl.ds(pl.multiple_of(c * 512, 512), 512)
        out = []
        for g in range(2):
            e = jnp.exp(sg[g, rows, :] - peaks[g])
            out.append(totals[g] + jnp.sum(e, axis=0, keepdims=True))
            og[g] += dot_nn(vt[:, rows], e.astype(LOW))
        return tuple(out)

    totals = lax.fori_loop(0, length // 512, mix, (jnp.zeros((1, 256), F32),) * 2, unroll=2)
    for g in range(2):
        ctx_o[g * 64 : g * 64 + 64, :] = pick_turned(og[g] * (1.0 / totals[g])).astype(LOW)
        lse_o[g : g + 1, :] = peaks[g] + jnp.log(totals[g])
    for copy in copies:
        copy.wait()


def vmem():
    return pl.BlockSpec(memory_space=pltpu.VMEM)


def smem():
    return pl.BlockSpec(memory_space=pltpu.SMEM)


def forward_attention(scal, drawn, table, x, w, w_kt, w_vt, shift, shift_vt):
    length = x.shape[0]
    blocks = length // BLOCK
    rows = jax.ShapeDtypeStruct((length, 256), LOW)
    return pl.pallas_call(
        forward_kernel,
        out_shape=(
            rows, rows, rows, jax.ShapeDtypeStruct((256, length), LOW), rows, jax.ShapeDtypeStruct((blocks, 256), F32),
        ),
        in_specs=[smem(), smem()] + [vmem()] * 7,
        out_specs=[pl.BlockSpec(memory_space=pl.ANY)] * 4 + [vmem()] * 2,
        scratch_shapes=[
            pltpu.VMEM((256, 256), LOW),
            pltpu.VMEM((length, 256), LOW),
            pltpu.VMEM((length, 256), LOW),
            pltpu.VMEM((length, 256), LOW),
            pltpu.VMEM((256, length), LOW),
            pltpu.VMEM((256, length), LOW),
            pltpu.VMEM((blocks, 256, HALF), LOW),
            pltpu.VMEM((2, length, 256), F32),
            pltpu.VMEM((2, 256, 256), F32),
            pltpu.SemaphoreType.DMA((4,)),
        ],
        compiler_params=pltpu.CompilerParams(vmem_limit_bytes=VMEM_LIMIT),
        cost_estimate=pl.CostEstimate(flops=16_000_000_000, bytes_accessed=12_000_000, transcendentals=10_000_000),
        name="attend_forward",
    )(scal, drawn, table, x, w, w_kt, w_vt, shift, shift_vt)


def normalize(summed):
    center = summed - jnp.mean(summed, axis=-1, keepdims=True)
    return (*scaled(center), center)


def scaled(center):
    factor = lax.rsqrt(jnp.mean(center * center, axis=-1, keepdims=True) + NORM_EPSILON)
    return (center * factor, factor)


def normalize_back(grad_normed, normed, factor):
    return factor * (
        grad_normed
        - jnp.mean(grad_normed, axis=-1, keepdims=True)
        - normed * jnp.mean(grad_normed * normed, axis=-1, keepdims=True)
    )


ROOT_HALF = 0.7071067811865476


def gelu_weight(v):
    return 0.5 * (1.0 + lax.erf(v * ROOT_HALF))


def open_rows(table, scal, rows):
    last = scal[0] - 1
    marks = []
    for n in range(rows // BLOCK):
        b = pl.program_id(0) * (rows // BLOCK) + n
        one = table[(b >= last).astype(jnp.int32) + (b > last).astype(jnp.int32)]
        marks.append(jnp.concatenate([one, one], axis=1))
    return jnp.concatenate(marks, axis=0) == 0.0


def ahead_kernel(scal, table, x, ctx, w_out, w_up, w_down, up_shift, vec, out_o, one_o, two_o, act, slope_o):
    rows = x.shape[0]

    def row(n):
        return vec[n : n + 1, :]

    attended = dot_nn(ctx[...], w_out[...]) + row(2)
    normed_one, _, center = normalize(x[...].astype(F32) + attended)
    one_o[...] = center.astype(LOW)
    first_out = normed_one * row(3) + row(4)
    first_low = first_out.astype(LOW)
    for c in range(0, 1024, 256):
        pre = dot_nn(first_low, w_up[:, c : c + 256]) + up_shift[:, c : c + 256]
        weight = gelu_weight(pre)
        act[:, c : c + 256] = (pre * weight).astype(LOW)
        slope_o[:, c : c + 256] = (weight + pre * (NORMAL_PEAK * jnp.exp(-0.5 * pre * pre))).astype(LOW)
    branch = dot_nn(act[...], w_down[...]) + row(5)
    normed_two, _, center = normalize(first_out + branch)
    two_o[...] = center.astype(LOW)
    out_o[...] = jnp.where(open_rows(table, scal, rows), normed_two * row(6) + row(7), 0.0).astype(LOW)


def ahead(scal, table, x, ctx, w_out, w_up, w_down, up_shift, vec):
    length = x.shape[0]
    rows = AHEAD_ROWS

    def wide(columns):
        return pl.BlockSpec((rows, columns), lambda i, s: (i, 0))

    def whole(*shape):
        return pl.BlockSpec(shape, lambda i, s: (0,) * len(shape))

    shape = jax.ShapeDtypeStruct
    return pl.pallas_call(
        ahead_kernel,
        grid_spec=pltpu.PrefetchScalarGridSpec(
            num_scalar_prefetch=1,
            grid=(length // rows,),
            in_specs=[
                whole(3, 64, 128), wide(256), wide(256), whole(256, 256), whole(256, 1024), whole(1024, 256),
                whole(1, 1024), whole(8, 256),
            ],
            out_specs=[wide(256), wide(256), wide(256), wide(1024), wide(1024)],
        ),
        out_shape=(
            shape((length, 256), LOW), shape((length, 256), LOW), shape((length, 256), LOW),
            shape((length, 1024), LOW), shape((length, 1024), LOW),
        ),
        compiler_params=pltpu.CompilerParams(vmem_limit_bytes=VMEM_LIMIT),
        cost_estimate=pl.CostEstimate(flops=5_000_000_000, bytes_accessed=34_000_000, transcendentals=10_000_000),
        name="ahead",
    )(scal, table, x, ctx, w_out, w_up, w_down, up_shift, vec)


def behind_kernel(
    scal, table, cot, ctx, one, two, act, slope, w_out, w_up, w_down, vec,
    gz1_o, gctx_o, delta_o, pack0, pack1, pack2, pack3, gdown_o, gup_o, gout_o, gub_o, gvec_o, back,
):
    step = pl.program_id(0)
    rows = cot.shape[0]

    @pl.when(step == 0)
    def _():
        for ref in (gdown_o, gup_o, gout_o, gub_o, gvec_o):
            ref[...] = jnp.zeros_like(ref)

    def row(n):
        return vec[n : n + 1, :]

    normed_one, factor_one = scaled(one[...].astype(F32))
    normed_two, factor_two = scaled(two[...].astype(F32))
    first_low = (normed_one * row(3) + row(4)).astype(LOW)
    grad_y = jnp.where(open_rows(table, scal, rows), cot[...].astype(F32), 0.0)
    grad_z2 = normalize_back(grad_y * row(6), normed_two, factor_two)
    grad_branch = grad_z2.astype(LOW)
    for c in range(0, 1024, 256):
        grad_act = dot_nt(grad_branch, w_down[c : c + 256, :])
        grad_pre = (grad_act * slope[:, c : c + 256].astype(F32)).astype(LOW)
        back[:, c : c + 256] = grad_pre
        gub_o[:, c : c + 256] += jnp.sum(grad_pre.astype(F32), axis=0, keepdims=True)
    gdown_o[...] += dot_tn(act[...], grad_branch)
    grad_first = grad_z2 + dot_nt(back[...], w_up[...])
    gup_o[...] += dot_tn(first_low, back[...])
    grad_z1 = normalize_back(grad_first * row(3), normed_one, factor_one)
    gz1_o[...] = grad_z1
    grad_attended = grad_z1.astype(LOW)
    ctx_v = ctx[...]
    gout_o[...] += dot_tn(ctx_v, grad_attended)
    grad_context = dot_nt(grad_attended, w_out[...]).astype(LOW)
    gctx_o[...] = grad_context

    def add(n, values):
        gvec_o[n : n + 1, :] += jnp.sum(values, axis=0, keepdims=True)

    add(2, grad_attended.astype(F32))
    add(3, grad_first * normed_one)
    add(4, grad_first)
    add(5, grad_branch.astype(F32))
    add(6, grad_y * normed_two)
    add(7, grad_y)
    both = ctx_v.astype(F32) * grad_context.astype(F32)
    upper = both.astype(LOW)
    lower = (both - upper.astype(F32)).astype(LOW)
    group = lax.broadcasted_iota(jnp.int32, (8, 256), 1) // BLOCK
    ones = jnp.where(group == lax.broadcasted_iota(jnp.int32, (8, 256), 0), 1.0, 0.0).astype(LOW)
    sums = dot_nt(ones, upper) + dot_nt(ones, lower)
    for n in range(rows // BLOCK):
        part = sums[0:4, n * BLOCK : (n + 1) * BLOCK]
        delta_o[n : n + 1, :] = jnp.concatenate([part[h : h + 1, :] for h in range(4)], axis=1)

    @pl.when(step == pl.num_programs(0) - 1)
    def _():
        for r, pack in enumerate((pack0, pack1, pack2, pack3)):
            piece = scal[1] ^ r
            shard, core = piece // 2, piece % 2
            here = pl.ds(pl.multiple_of(piece * 64, 64), 64)
            pack[:, 0:1024] = gup_o[here, :].astype(LOW)
            pack[:, 1024:1280] = gout_o[here, :].astype(LOW)
            for g in range(4):
                at = pl.ds(pl.multiple_of(shard * 512 + g * 128 + core * 64, 64), 64)
                pack[:, 1280 + 256 * g : 1536 + 256 * g] = gdown_o[at, :].astype(LOW)
            lines = [gub_o[:, pl.ds(pl.multiple_of(shard * 512 + 128 * n, 128), 128)] for n in range(4)]
            first = shard == 0
            for n in range(4):
                line = jnp.where(first, gvec_o[n : n + 1, :], gvec_o[4 + n : 5 + n, :])
                lines += [line[:, 0:128], line[:, 128:256]]
            put_extra(pack, 2304, lines, core)


def put_extra(pack, at, lines, core):
    some = jnp.concatenate(lines + [jnp.zeros((16 - len(lines), HALF), F32)], axis=0)
    pack[0:16, at : at + HALF] = jnp.where(core == 0, some, 0.0).astype(LOW)
    pack[16:64, at : at + HALF] = jnp.zeros((48, HALF), LOW)


def behind(scal, table, cot, ctx, one, two, act, slope, w_out, w_up, w_down, vec):
    length = cot.shape[0]
    rows = BEHIND_ROWS

    def wide(columns):
        return pl.BlockSpec((rows, columns), lambda i, s: (i, 0))

    def whole(*shape):
        return pl.BlockSpec(shape, lambda i, s: (0,) * len(shape))

    shape = jax.ShapeDtypeStruct
    return pl.pallas_call(
        behind_kernel,
        grid_spec=pltpu.PrefetchScalarGridSpec(
            num_scalar_prefetch=1,
            grid=(length // rows,),
            in_specs=[
                whole(3, 64, 128), wide(256), wide(256), wide(256), wide(256), wide(1024), wide(1024),
                whole(256, 256), whole(256, 1024), whole(1024, 256), whole(8, 256),
            ],
            out_specs=[
                wide(256), wide(256), pl.BlockSpec((rows // BLOCK, 256), lambda i, s: (i, 0)),
                whole(64, 2432), whole(64, 2432), whole(64, 2432), whole(64, 2432),
            ],
            scratch_shapes=[
                pltpu.VMEM((1024, 256), F32), pltpu.VMEM((256, 1024), F32), pltpu.VMEM((256, 256), F32),
                pltpu.VMEM((1, 1024), F32), pltpu.VMEM((8, 256), F32), pltpu.VMEM((rows, 1024), LOW),
            ],
        ),
        out_shape=(
            shape((length, 256), F32), shape((length, 256), LOW), shape((length // BLOCK, 256), F32),
        ) + (shape((64, 2432), LOW),) * 4,
        compiler_params=pltpu.CompilerParams(vmem_limit_bytes=VMEM_LIMIT),
        cost_estimate=pl.CostEstimate(flops=10_000_000_000, bytes_accessed=40_000_000, transcendentals=0),
        name="behind",
    )(scal, table, cot, ctx, one, two, act, slope, w_out, w_up, w_down, vec)


def backward_kernel(
    scal, drawn, table, q, k, v, kt, gctx, lse, delta, gz1, x, w,
    gin_o, pack0, pack1, pack2, pack3, picks, turned, dqg, dq, dk, dv, gw_o, gz1_v, x_v, gin_v, sems,
):
    length = x.shape[0]
    blocks = length // BLOCK
    live = scal[0]
    picks[...] = head_picks()
    dk[...] = jnp.zeros_like(dk)
    dv[...] = jnp.zeros_like(dv)
    loads = [pltpu.make_async_copy(gz1, gz1_v, sems.at[0]), pltpu.make_async_copy(x, x_v, sems.at[1])]
    for load in loads:
        load.start()
    turn_pairs(kt, turned)

    def spread(i):
        rows = pl.ds(pl.multiple_of(i * BLOCK, BLOCK), BLOCK)
        bdq = spread_heads(q[rows, :] * jnp.asarray(QUERY_SCALE, LOW), picks[...])
        bdo = spread_heads(gctx[rows, :], picks[...])
        return rows, bdq, bdo

    def group(idx):
        units = [Unit(i, live, drawn, blocks) for i in idx]
        spreads = [spread(i) for i in idx]
        low = first_half(BLOCK)
        s, g, p, ds, dvs, dks, dqs = {}, {}, {}, {}, {}, {}, {}
        count = len(idx)
        for t in range(count + 1):
            u = t - 0
            if 0 <= u < count:
                s[u] = dot_nt(slot_rows(units[u], k), spreads[u][1])
            u = t - 0
            if 0 <= u < count:
                g[u] = dot_nt(slot_rows(units[u], v), spreads[u][2])
            u = t - 0
            if 0 <= u < count:
                e = jnp.exp(masked(s[u], units[u].bias(table, range(2, 8))) - lse[pl.ds(idx[u], 1), :])
                ds[u] = (e * (g[u] - delta[pl.ds(idx[u], 1), :])).astype(LOW)
                p[u] = e.astype(LOW)
            u = t - 0
            if 0 <= u < count:
                dvs[u] = dot_nn(p[u], spreads[u][2])
                dks[u] = dot_nn(ds[u], spreads[u][1])
                dqs[u] = dot_nn(slot_turned(units[u], kt[:, 0:128], turned), ds[u])
            u = t - 1
            if 0 <= u < count:
                for acc, terms_ in ((dk, dks[u]), (dv, dvs[u])):
                    acc[0:128, :] += terms_[0:128, :]
                    for n in range(2, 8):
                        one = terms_[n * 64 : n * 64 + 64, :]
                        if n < 5:
                            at = pl.ds(pl.multiple_of(units[u].near[n - 2] * BLOCK, BLOCK), BLOCK)
                            acc[at, :] += one
                        else:
                            for h in range(4):
                                t_ = h // 2
                                at = pl.ds(pl.multiple_of(units[u].chosen[n - 5][h] * BLOCK, BLOCK), BLOCK)
                                cols = pl.ds(t_ * HALF, HALF)
                                mine = low if h % 2 == 0 else jnp.logical_not(low)
                                acc[at, cols] += jnp.where(mine, one[:, t_ * HALF : t_ * HALF + HALF], 0.0)
                dq[spreads[u][0], :] = (pick_turned(dqs[u]) * QUERY_SCALE).astype(LOW)

    def several(j, _):
        group([2 + BACK * j + u for u in range(BACK)])
        return 0

    lax.fori_loop(0, (blocks - 2) // BACK, several, 0)
    if (blocks - 2) % BACK:
        group([live * 0 + i for i in range(blocks - (blocks - 2) % BACK, blocks)])

    spreads = [spread(g)[1:] for g in range(2)]
    dqg[...] = jnp.zeros_like(dqg)

    def chunk(c, _):
        at = pl.ds(pl.multiple_of(c * 512, 512), 512)
        bias = chunk_bias(table, live, c * 8, 8)
        kh, vh, th = k[at, :], v[at, :], kt[:, at]
        two = range(2)
        s = [dot_nt(kh, spreads[g][0]) for g in two]
        t = [dot_nt(vh, spreads[g][1]) for g in two]
        p = [jnp.exp(s[g] + bias - lse[g : g + 1, :]) for g in two]
        ds = [(p[g] * (t[g] - delta[g : g + 1, :])).astype(LOW) for g in two]
        dvs = [dot_nn(p[g].astype(LOW), spreads[g][1]) for g in two]
        dks = [dot_nn(ds[g], spreads[g][0]) for g in two]
        for g in two:
            dqg[g] += dot_nn(th, ds[g])
        dv[at, :] += dvs[0] + dvs[1]
        dk[at, :] += dks[0] + dks[1]
        return 0

    lax.fori_loop(0, length // 512, chunk, 0, unroll=2)
    for g in range(2):
        dq[g * 64 : g * 64 + 64, :] = (pick_turned(dqg[g]) * QUERY_SCALE).astype(LOW)

    gw_o[...] = jnp.zeros_like(gw_o)
    for load in loads:
        load.wait()

    def finish(c, shifts):
        rows = pl.ds(pl.multiple_of(c * 512, 512), 512)
        dqkv = jnp.concatenate([dq[rows, :], dk[rows, :].astype(LOW), dv[rows, :].astype(LOW)], axis=1)
        gin_v[rows, :] = (gz1_v[rows, :] + dot_nt(dqkv, w[...])).astype(LOW)
        gw_o[...] += dot_tn(x_v[rows, :], dqkv)
        return shifts + jnp.sum(dqkv.astype(F32), axis=0, keepdims=True)

    shifts = lax.fori_loop(0, length // 512, finish, jnp.zeros((1, 768), F32), unroll=2)
    store = pltpu.make_async_copy(gin_v, gin_o, sems.at[2])
    store.start()
    for r, pack in enumerate((pack0, pack1, pack2, pack3)):
        piece = scal[1] ^ r
        core = piece % 2
        pack[:, 0:768] = gw_o[pl.ds(pl.multiple_of(piece * 64, 64), 64), :].astype(LOW)
        mine = jnp.where(piece // 2 == 0, shifts, 0.0)
        lines = [jnp.zeros((4, HALF), F32)] + [mine[:, a : a + HALF] for a in (0, 128, 512, 640)]
        lines += [jnp.zeros((8, HALF), F32)]
        pack[:, 768:896] = jnp.zeros((64, HALF), LOW)
        pack[0:16, 768:896] = jnp.where(core == 0, jnp.concatenate(lines, axis=0), 0.0).astype(LOW)
    store.wait()


def backward_attention(scal, drawn, table, q, k, v, kt, gctx, lse, delta, gz1, x, w):
    length = x.shape[0]
    shape = jax.ShapeDtypeStruct
    return pl.pallas_call(
        backward_kernel,
        out_shape=(shape((length, 256), LOW),) + (shape((64, 896), LOW),) * 4,
        in_specs=[smem(), smem()] + [vmem()] * 8 + [pl.BlockSpec(memory_space=pl.ANY)] * 2 + [vmem()],
        out_specs=[pl.BlockSpec(memory_space=pl.ANY)] + [vmem()] * 4,
        scratch_shapes=[
            pltpu.VMEM((256, 256), LOW),
            pltpu.VMEM((length // BLOCK, 256, HALF), LOW),
            pltpu.VMEM((2, 256, 256), F32),
            pltpu.VMEM((length, 256), LOW),
            pltpu.VMEM((length, 256), F32),
            pltpu.VMEM((length, 256), F32),
            pltpu.VMEM((256, 768), F32),
            pltpu.VMEM((length, 256), F32),
            pltpu.VMEM((length, 256), LOW),
            pltpu.VMEM((length, 256), LOW),
            pltpu.SemaphoreType.DMA((3,)),
        ],
        compiler_params=pltpu.CompilerParams(vmem_limit_bytes=VMEM_LIMIT),
        cost_estimate=pl.CostEstimate(flops=40_000_000_000, bytes_accessed=20_000_000, transcendentals=10_000_000),
        name="attend_backward",
    )(scal, drawn, table, q, k, v, kt, gctx, lse, delta, gz1, x, w)


def bias_table(tail):
    column = jnp.stack([jnp.zeros_like(tail, F32), jnp.where(tail == 1, 0.0, MASK_VALUE), jnp.full(tail.shape, MASK_VALUE, F32)])
    return jnp.broadcast_to(column[:, :, None], (3, BLOCK, HALF))


def reorder_kernel(scatter, where, assign, src, *rest):
    *_, dst, held, arrived, left = rest
    count = src.shape[0]
    shards = assign.shape[0] // count
    loads, stores = [], []
    for j in range(count):
        one = assign[shards * j + where[0]]
        loads.append(pltpu.make_async_copy(src.at[j if scatter else one], held.at[j], arrived.at[j]))
        stores.append(pltpu.make_async_copy(held.at[j], dst.at[one if scatter else j], left.at[j]))
        loads[-1].start()
    for load, store in zip(loads, stores):
        load.wait()
        store.start()
    for store in stores:
        store.wait()


def reorder(shard, assign, src, scatter, after=()):
    return pl.pallas_call(
        functools.partial(reorder_kernel, scatter),
        out_shape=jax.ShapeDtypeStruct(src.shape, src.dtype),
        in_specs=[smem(), smem(), pl.BlockSpec(memory_space=pltpu.HBM)]
        + [pl.BlockSpec(memory_space=pltpu.HBM)] * len(after),
        out_specs=pl.BlockSpec(memory_space=pltpu.HBM),
        scratch_shapes=[
            pltpu.VMEM(src.shape, src.dtype),
            pltpu.SemaphoreType.DMA((src.shape[0],)),
            pltpu.SemaphoreType.DMA((src.shape[0],)),
        ],
        compiler_params=pltpu.CompilerParams(vmem_limit_bytes=VMEM_LIMIT),
        cost_estimate=pl.CostEstimate(flops=0, bytes_accessed=4 * src.size, transcendentals=0),
        name="reorder",
    )(shard, assign, src, *after)


def hold(values, after):
    count = len(values)
    anywhere = pl.BlockSpec(memory_space=pltpu.HBM)
    return pl.pallas_call(
        lambda *refs: None,
        out_shape=tuple(jax.ShapeDtypeStruct(v.shape, v.dtype) for v in values),
        in_specs=[anywhere] * (count + len(after)),
        out_specs=(anywhere,) * count,
        input_output_aliases={n: n for n in range(count)},
        name="hold",
    )(*values, *after)


def pack_kernel(w_qkv, w_out, w_up, w_down, up_bias, vectors, after, out):
    rows = w_qkv.shape[0]
    out[0:rows, 0:768] = w_qkv[...]
    out[0:rows, 768:1024] = w_out[...]
    out[0:rows, 1024:2048] = w_up[...]
    for n in range(4):
        out[0:rows, 2048 + 256 * n : 2304 + 256 * n] = w_down[rows * n : rows * (n + 1), :]
    lines = [up_bias[...].astype(F32)] + [vectors[n : n + 1, :].astype(F32) for n in range(4)]
    line = jnp.concatenate(lines + [jnp.zeros((1, 3072 - 1536), F32)], axis=1)
    out[rows : rows + 16, :] = jnp.broadcast_to(line, (16, 3072)).astype(LOW)


def pack_weights(parts, after):
    w_qkv, w_out, w_up, w_down, up_bias, vectors = parts
    return pl.pallas_call(
        pack_kernel,
        out_shape=jax.ShapeDtypeStruct((w_qkv.shape[0] + 16, 3072), LOW),
        in_specs=[vmem()] * 6 + [pl.BlockSpec(memory_space=pltpu.HBM)],
        out_specs=vmem(),
        compiler_params=pltpu.CompilerParams(vmem_limit_bytes=VMEM_LIMIT),
        name="pack_weights",
    )(w_qkv, w_out, w_up, w_down, up_bias.reshape(1, -1), vectors, after)


def unpack_kernel(shard, own, got, w_qkv, w_out, w_up, w_down, w_kt, w_vt, up_shift, vec, shift, shift_vt):
    rows = own.shape[0] - 16
    first = shard[0] == 0

    def half(n, at, cols):
        mine, other = own[at, cols], got[at, cols]
        return jnp.where(first == (n == 0), mine, other)

    for n in range(2):
        here = slice(n * rows, (n + 1) * rows)
        w_qkv[here, :] = half(n, slice(0, rows), slice(0, 768))
        w_out[here, :] = half(n, slice(0, rows), slice(768, 1024))
        w_up[here, :] = half(n, slice(0, rows), slice(1024, 2048))
        for g in range(4):
            at = (4 * n + g) * rows
            w_down[at : at + rows, :] = half(n, slice(0, rows), slice(2048 + 256 * g, 2304 + 256 * g))
        line = half(n, slice(rows, rows + 16), slice(0, 1536)).astype(F32)[0:1]
        up_shift[:, 512 * n : 512 * n + 512] = line[:, 0:512]
        for g in range(4):
            vec[4 * n + g : 4 * n + g + 1, :] = line[:, 512 + 256 * g : 768 + 256 * g]
    shift[...] = jnp.concatenate([vec[0:1, :], jnp.zeros((1, 256), F32), vec[1:2, :]], axis=1)
    w_kt[...] = w_qkv[:, 256:512].astype(F32).T.astype(LOW)
    w_vt[...] = w_qkv[:, 512:768].astype(F32).T.astype(LOW)
    shift_vt[...] = jnp.broadcast_to(vec[1:2, :], (HALF, 256)).T


def unpack_weights(shard, own, got):
    shape = jax.ShapeDtypeStruct
    return pl.pallas_call(
        unpack_kernel,
        out_shape=(
            shape((256, 768), LOW), shape((256, 256), LOW), shape((256, 1024), LOW), shape((1024, 256), LOW),
            shape((256, 256), LOW), shape((256, 256), LOW), shape((1, 1024), F32), shape((8, 256), F32),
            shape((1, 768), F32), shape((256, HALF), F32),
        ),
        in_specs=[smem(), vmem(), vmem()],
        out_specs=[vmem()] * 10,
        compiler_params=pltpu.CompilerParams(vmem_limit_bytes=VMEM_LIMIT),
        name="unpack_weights",
    )(shard, own, got)


def trade(pieces):
    count = lax.axis_size("dp")
    held = [pieces[0]]
    for n in (1, 2, 3):
        pairs = [(d * 2 + s, (d ^ (n % 2)) * 2 + (s ^ (n // 2))) for d in range(count) for s in range(2)]
        held.append(lax.ppermute(pieces[n], ("dp", "shard"), pairs))
    return held


def total(pieces):
    return sum(piece.astype(F32) for piece in pieces)


def sum_rest(part, data_index, meanwhile):
    count = lax.axis_size("dp")
    groups = count // 4
    half = part.shape[0] // 2
    bit = (data_index // 2) % 2
    flip = [(d, d ^ 2) for d in range(count)]
    keep = lax.dynamic_slice_in_dim(part, bit * half, half, 0)
    give = lax.dynamic_slice_in_dim(part, (1 - bit) * half, half, 0)
    part = keep + lax.ppermute(give.astype(LOW), "dp", flip).astype(F32)
    at = data_index // 4
    small = half // groups
    hops = [[(d, (d + 4 * k) % count) for d in range(count)] for k in range(1, groups)]

    def piece(k):
        return lax.dynamic_slice_in_dim(part, lax.rem(at + k, groups) * small, small, 0)

    other = meanwhile(part)
    mine = hold((piece(0),), (other,))[0]
    got = [lax.ppermute(piece(k + 1).astype(LOW), "dp", hop) for k, hop in enumerate(hops)]
    for one in got:
        mine = mine + one.astype(F32)
    return mine.astype(LOW), other


def spread_sums(mine, meanwhile):
    count = lax.axis_size("dp")
    flip = [(d, d ^ 2) for d in range(count)]
    hops = [[(d, (d + 4 * k) % count) for d in range(count)] for k in range(1, count // 4)]
    near = jnp.stack([mine] + [lax.ppermute(mine, "dp", hop) for hop in hops])
    core = [(d, d ^ 1) for d in range(count)]
    other = meanwhile(near)
    across = hold((lax.ppermute(near, "dp", flip),), (other,))[0]
    return (near, across, lax.ppermute(near, "dp", core), lax.ppermute(across, "dp", core)), other


def adam_update(grad, state, decay):
    correct_one = 1.0 - FIRST_BETA**STEP
    correct_two = 1.0 - SECOND_BETA**STEP
    first_new = FIRST_BETA * state[1] + (1.0 - FIRST_BETA) * grad
    second_new = SECOND_BETA * state[2] + (1.0 - SECOND_BETA) * grad * grad
    direction = first_new / correct_one / (jnp.sqrt(second_new / correct_two) + ADAM_EPSILON)
    master_new = state[0] - LEARNING_RATE * (direction + decay * state[0])
    return (master_new, first_new, second_new)


def update_kernel(
    where, near, across, near_core, across_core, s_qkv, s_out, s_up, s_down, s_bias, s_vec,
    g_qkv, g_out, g_up, g_down, g_bias, g_vec, o_master, o_first, o_second, grads, flat, sems,
):
    groups, small = near.shape[:2]
    parts = (near, across, near_core, across_core)
    index = where[0]
    for core in range(2):
        for side in range(2):
            base = ((index % 2) ^ core) * 64 + (((index // 2) % 2) ^ side) * 32
            for k in range(groups):
                at = base + lax.rem(index // 4 + groups - k, groups) * small
                grads[pl.ds(pl.multiple_of(at, small), small), :] = parts[2 * core + side][k].astype(F32)
    copies = []

    def send(here, there):
        copies.append(pltpu.make_async_copy(here, there, sems.at[len(copies)]))
        copies[-1].start()

    send(grads.at[:, 2304:3072], g_qkv)
    send(grads.at[:, 1024:1280], g_out)
    send(grads.at[:, 0:1024], g_up)
    for n in range(4):
        send(grads.at[:, 1280 + 256 * n : 1536 + 256 * n], g_down.at[pl.ds(128 * n, 128), :])
    outs = (o_master, o_first, o_second)

    def place(base, grad, state, decay):
        rows, columns = grad.shape
        wide = columns // HALF
        for n, value in enumerate(adam_update(grad, state, decay)):
            for c in range(wide):
                at = pl.ds(base + c, rows, stride=wide) if wide > 1 else pl.ds(base, rows)
                flat[n, at, :] = value[:, c * HALF : (c + 1) * HALF]

    def ship(base, count):
        for n, there in enumerate(outs):
            send(flat.at[n, pl.ds(base, count), :], there.reshape(flat.shape[1:]).at[pl.ds(base, count), :])

    place(1024, grads[:, 0:1024], s_up, WEIGHT_DECAY)
    ship(1024, 1024)
    for n in range(4):
        rows = slice(128 * n, 128 * n + 128)
        place(2048 + 256 * n, grads[:, 1280 + 256 * n : 1536 + 256 * n], s_down[:, rows, :], WEIGHT_DECAY)
    ship(2048, 1024)
    place(0, grads[:, 2304:3072], s_qkv, WEIGHT_DECAY)
    ship(0, 768)
    place(768, grads[:, 1024:1280], s_out, WEIGHT_DECAY)
    ship(768, 256)
    extra = grads[0:16, 3072:3200]
    g_bias[...] = extra[0:4]
    bias = [
        jnp.concatenate([s_bias[n : n + 1, c * HALF : (c + 1) * HALF] for c in range(4)], axis=0) for n in range(3)
    ]
    place(3072, extra[0:4], bias, 0.0)
    vec = jnp.concatenate(
        [jnp.concatenate([extra[4 + 2 * n : 5 + 2 * n], extra[5 + 2 * n : 6 + 2 * n]], axis=1) for n in range(4)], axis=0
    )
    g_vec[...] = vec
    place(3076, vec, s_vec, 0.0)
    ship(3072, 12)
    for copy in copies:
        copy.wait()


def update(data_index, parts, states):
    shape = lambda *dims: jax.ShapeDtypeStruct(dims, F32)
    s_qkv, s_out, s_up, s_down, s_bias, s_vec = states
    flat = shape(1, 3084 * HALF)
    away = pl.BlockSpec(memory_space=pltpu.HBM)
    *grads, master, first, second = pl.pallas_call(
        update_kernel,
        out_shape=(
            shape(128, 768), shape(128, 256), shape(128, 1024), shape(512, 256), shape(4, HALF), shape(4, 256),
            flat, flat, flat,
        ),
        in_specs=[smem()] + [vmem()] * 10,
        out_specs=[away] * 4 + [vmem()] * 2 + [away] * 3,
        scratch_shapes=[
            pltpu.VMEM((128, 3200), F32), pltpu.VMEM((3, 3084, HALF), F32), pltpu.SemaphoreType.DMA((22,)),
        ],
        compiler_params=pltpu.CompilerParams(vmem_limit_bytes=VMEM_LIMIT),
        cost_estimate=pl.CostEstimate(flops=10_000_000, bytes_accessed=14_000_000, transcendentals=400_000),
        name="update",
    )(data_index.reshape(1), *parts, s_qkv, s_out, s_up, s_down, s_bias, s_vec)
    grads[4] = grads[4].reshape(-1)
    return tuple(grads) + (master, first, second)


def on_device(
    hidden, cotangent, assign, live_blocks, tail_live, random_blocks, w_qkv, w_out, w_up, w_down, up_bias, vectors,
    state_qkv, state_out, state_up, state_down, state_ubias, state_vec,
):
    shard_count = lax.axis_size("shard")
    shard_index = lax.axis_index("shard")
    data_index = lax.axis_index("dp")
    row_seqs, rows_here, width = hidden.shape
    length = row_seqs * rows_here
    shard = shard_index.reshape(1)

    def to_slot(rows):
        return lax.all_to_all(rows, "dp", split_axis=0, concat_axis=0, tiled=True).reshape(length, width)

    sent = reorder(shard, assign, hidden, False)
    x = to_slot(sent)
    pack = pack_weights((w_qkv, w_out, w_up, w_down, up_bias, vectors), sent)
    got = lax.ppermute(pack, "shard", [(0, 1), (1, 0)])
    w_qkv, w_out, w_up, w_down, w_kt, w_vt, up_shift, vec, shift, shift_vt = unpack_weights(shard, pack, got)
    slot = assign[data_index * shard_count + shard_index]
    own = shard_index * row_seqs + slot
    scal = jnp.stack([live_blocks[own], 2 * shard_index + data_index % 2])
    table = bias_table(lax.dynamic_index_in_dim(tail_live, own, 0, keepdims=False))
    drawn = random_blocks.reshape(-1)
    ready = (w_qkv, scal, table, drawn)
    cot = to_slot(reorder(shard, assign, cotangent, False, ready))
    q, k, v, kt, ctx, lse = forward_attention(scal, drawn, table, x, w_qkv, w_kt, w_vt, shift, shift_vt)
    out, *kept = ahead(scal, table, x, ctx, w_out, w_up, w_down, up_shift, vec)

    def from_slot(rows):
        return lax.all_to_all(
            rows.reshape(row_seqs, rows_here, width), "dp", split_axis=0, concat_axis=0, tiled=True
        )

    back_out = from_slot(out)
    gz1, gctx, delta, *early = behind(scal, table, cot, ctx, *kept, w_out, w_up, w_down, vec)
    early = trade(early)
    gin, *late = backward_attention(scal, drawn, table, q, k, v, kt, gctx, lse, delta, gz1, x, w_qkv)
    gin, *late = hold((gin, *late), (back_out, *early[1:]))
    back_gin = from_slot(gin)

    def sum_all(early, late, back_out):
        early, late = total(early), total(trade(late))
        sums = jnp.concatenate([early[:, :2304], late[:, :768], early[:, 2304:] + late[:, 768:]], axis=1)
        return sum_rest(sums, data_index, lambda part: reorder(shard, assign, back_out, True, (part,)))

    made = jax.eval_shape(sum_all, early, late, back_out)
    mine, layer_out = lax.cond(
        live_blocks[0] > 0,
        sum_all,
        lambda *unused: jax.tree.map(lambda one: jnp.zeros(one.shape, one.dtype), made),
        early, late, back_out,
    )
    parts, input_grad = spread_sums(mine, lambda near: reorder(shard, assign, back_gin, True, (near,)))
    states = (state_qkv, state_out, state_up, state_down, state_ubias, state_vec)
    updated = update(data_index, parts, states)
    return (layer_out, input_grad) + updated


def solution(mesh):
    placed = (
        P("shard", "dp", None), P("shard", "dp", None), P(), P(), P(), P(("dp", "shard"), None, None, None),
        P("shard", None), P("shard", None), P("shard", None), P("shard", None), P("shard"), P("shard", None),
        P(None, "shard", None), P(None, "shard", None), P(None, "shard", None), P(None, "shard", None),
        P(None, "shard"), P(None, "shard", None),
    )
    return jax.shard_map(
        on_device,
        mesh=mesh,
        in_specs=placed,
        out_specs=(
            P("shard", "dp", None), P("shard", "dp", None), P("shard", None), P("shard", None), P("shard", None),
            P("shard", None), P("shard"), P("shard", None), P("shard", None), P("shard", None), P("shard", None),
        ),
        check_vma=False,
    )
```

```python
import functools

import jax
import jax.numpy as jnp
from jax import lax
from jax.experimental import pallas as pl
from jax.experimental.pallas import tpu as pltpu
from jax.sharding import PartitionSpec as P

STEP = 1
QUERY_SCALE = 0.125
NORM_EPSILON = 1e-12
LEARNING_RATE = 0.02
WEIGHT_DECAY = 0.01
ADAM_EPSILON = 1e-08
FIRST_BETA = 0.5
SECOND_BETA = 0.5
MASK_VALUE = -1e30
NORMAL_PEAK = 0.3989422804014327

LOW = jnp.bfloat16
F32 = jnp.float32
VMEM_LIMIT = 60 * 1024 * 1024

BLOCK = 64
HALF = 128
GROUP = 31
AHEAD_ROWS = 1024
BEHIND_ROWS = 512
BACK = 20


def dot_nn(a, b):
    return lax.dot_general(a, b, (((1,), (0,)), ((), ())), preferred_element_type=F32)


def dot_nt(a, b):
    return lax.dot_general(a, b, (((1,), (1,)), ((), ())), preferred_element_type=F32)


def dot_tn(a, b):
    return lax.dot_general(a, b, (((0,), (0,)), ((), ())), preferred_element_type=F32)


def first_half(rows):
    return lax.broadcasted_iota(jnp.int32, (rows, HALF), 1) < BLOCK


def spread_heads(rows, picks):
    return jnp.concatenate([rows, rows, rows, rows], axis=0) * picks


def pick_heads(wide):
    low = first_half(BLOCK)
    left = jnp.where(low, wide[0:64, 0:HALF], wide[64:128, 0:HALF])
    right = jnp.where(low, wide[128:192, HALF:], wide[192:256, HALF:])
    return jnp.concatenate([left, right], axis=1)


def head_picks():
    row = lax.broadcasted_iota(jnp.int32, (256, 256), 0) // BLOCK
    col = lax.broadcasted_iota(jnp.int32, (256, 256), 1) // BLOCK
    return jnp.where(row == col, 1.0, 0.0).astype(LOW)


def gather_slot(ref, chosen, tile):
    a, b = chosen[2 * tile], chosen[2 * tile + 1]
    cols = pl.ds(tile * HALF, HALF)
    left = ref[pl.ds(pl.multiple_of(a * BLOCK, BLOCK), BLOCK), cols]
    right = ref[pl.ds(pl.multiple_of(b * BLOCK, BLOCK), BLOCK), cols]
    return jnp.where(first_half(BLOCK), left, right)


def turn_pairs(ref, turned):
    pairs = turned.shape[0] // 2

    def one(j, _):
        pair = ref[:, pl.ds(pl.multiple_of(j * HALF, HALF), HALF)]
        turned[j] = pair
        turned[pairs + j] = jnp.concatenate([pair[:, BLOCK:], pair[:, :BLOCK]], axis=1)
        return 0

    lax.fori_loop(0, pairs, one, 0, unroll=8)


def pick_turned(wide):
    low = first_half(BLOCK)
    left, right = wide[0:HALF, 0:HALF].T, wide[HALF:, HALF:].T
    return jnp.concatenate(
        [jnp.where(low, part[0:BLOCK], part[BLOCK:]) for part in (left, right)], axis=1
    )


class Unit:
    def __init__(self, i, live, drawn, blocks):
        last = live - 1

        def state(b):
            return (b >= last).astype(jnp.int32) + (b > last).astype(jnp.int32)

        after = jnp.minimum(i + 1, blocks - 1)
        self.near = [i - 1, i, after]
        self.near_state = [
            jnp.where(i >= 3, state(i - 1), 2),
            state(i),
            jnp.where(i + 1 < blocks, state(after), 2),
        ]
        self.fixed_state = [state(0 * i), state(0 * i + 1)]
        self.chosen = [
            [drawn[(h * blocks + i) * 3 + s] for h in range(4)] for s in range(3)
        ]
        self.chosen_state = [[state(b) for b in row] for row in self.chosen]

    def bias(self, table, slots):
        rows = []
        for n in slots:
            if n < 5:
                one = table[(self.fixed_state + self.near_state)[n]]
                rows.append(jnp.concatenate([one, one], axis=1))
            else:
                st = self.chosen_state[n - 5]
                low = first_half(BLOCK)
                rows.append(
                    jnp.concatenate(
                        [
                            jnp.where(low, table[st[0]], table[st[1]]),
                            jnp.where(low, table[st[2]], table[st[3]]),
                        ],
                        axis=1,
                    )
                )
        return jnp.concatenate(rows, axis=0)


def masked(scores, bias):
    return jnp.concatenate([scores[0:HALF], scores[HALF:] + bias], axis=0)


def chunk_bias(table, live, first, count):
    last = live - 1
    rows = []
    for n in range(count):
        b = first + n
        st = (b >= last).astype(jnp.int32) + (b > last).astype(jnp.int32)
        one = table[st]
        rows.append(jnp.concatenate([one, one], axis=1))
    return jnp.concatenate(rows, axis=0)


def slot_rows(unit, ref):
    near = [ref[pl.ds(pl.multiple_of(b * BLOCK, BLOCK), BLOCK), :] for b in unit.near]
    rand = [jnp.concatenate([gather_slot(ref, unit.chosen[s], t) for t in range(2)], axis=1) for s in range(3)]
    return jnp.concatenate([ref[0:128, :]] + near + rand, axis=0)


def slot_turned(unit, first, turned):
    low = lax.broadcasted_iota(jnp.int32, (BLOCK, HALF), 1) < BLOCK
    every = [[b] * 4 for b in unit.near] + unit.chosen
    pairs = turned.shape[0] // 2
    tiles = [first]
    for n in range(3):
        parts = []
        for h in range(4):
            rows = pl.ds(h * BLOCK, BLOCK)
            a, b = every[2 * n][h], every[2 * n + 1][h]
            left = turned[(a & 1) * pairs + (a >> 1), rows, :]
            right = turned[(1 - (b & 1)) * pairs + (b >> 1), rows, :]
            parts.append(jnp.where(low, left, right))
        tiles.append(jnp.concatenate(parts, axis=0))
    return jnp.concatenate(tiles, axis=1)


def forward_kernel(
    scal, drawn, table, x, w, w_kt, w_vt, shift, shift_vt,
    q_o, k_o, v_o, kt_o, ctx_o, lse_o, picks, q_v, k_v, v_v, kt_v, vt, turned, sg, og, sems,
):
    length = x.shape[0]
    blocks = length // BLOCK
    live = scal[0]
    picks[...] = head_picks()

    def project(c, _):
        rows = pl.ds(pl.multiple_of(c * 512, 512), 512)
        xc = x[rows, :]
        out = (dot_nn(xc, w[...]) + shift[...]).astype(LOW)
        q_v[rows, :] = out[:, 0:256]
        k_v[rows, :] = out[:, 256:512]
        v_v[rows, :] = out[:, 512:768]
        kt_v[:, rows] = dot_nt(w_kt[...], xc).astype(LOW)
        vt[:, rows] = (dot_nt(w_vt[...], xc) + shift_vt[:, 0:1]).astype(LOW)
        return 0

    lax.fori_loop(0, length // 512, project, 0, unroll=2)
    copies = [
        pltpu.make_async_copy(here, there, sems.at[n])
        for n, (here, there) in enumerate(((q_v, q_o), (k_v, k_o), (v_v, v_o), (kt_v, kt_o)))
    ]
    for copy in copies:
        copy.start()
    turn_pairs(vt, turned)

    def group(j, _):
        idx = [2 + GROUP * j + u for u in range(GROUP)]
        units = [Unit(i, live, drawn, blocks) for i in idx]
        rows = [pl.ds(pl.multiple_of(i * BLOCK, BLOCK), BLOCK) for i in idx]
        bd = [spread_heads(q_v[r, :] * jnp.asarray(QUERY_SCALE, LOW), picks[...]) for r in rows]
        every = range(GROUP)
        s = [masked(dot_nt(slot_rows(units[u], k_v), bd[u]), units[u].bias(table, range(2, 8))) for u in every]
        m = [jnp.max(s[u], axis=0, keepdims=True) for u in every]
        e = [jnp.exp(s[u] - m[u]) for u in every]
        total = [jnp.sum(e[u], axis=0, keepdims=True) for u in every]
        o = [
            dot_nn(slot_turned(units[u], vt[:, 0:128], turned), e[u].astype(LOW)) * (1.0 / total[u]) for u in every
        ]
        for u in every:
            ctx_o[rows[u], :] = pick_turned(o[u]).astype(LOW)
            lse_o[pl.ds(idx[u], 1), :] = m[u] + jnp.log(total[u])
        return 0

    lax.fori_loop(0, (blocks - 2) // GROUP, group, 0)

    bds = [
        spread_heads(q_v[g * 64 : g * 64 + 64, :] * jnp.asarray(QUERY_SCALE, LOW), picks[...]) for g in range(2)
    ]

    def score(c, peaks):
        rows = pl.ds(pl.multiple_of(c * 512, 512), 512)
        bias = chunk_bias(table, live, c * 8, 8)
        out = []
        for g in range(2):
            s = dot_nt(k_v[rows, :], bds[g]) + bias
            sg[g, rows, :] = s
            out.append(jnp.maximum(peaks[g], jnp.max(s, axis=0, keepdims=True)))
        return tuple(out)

    peaks = lax.fori_loop(0, length // 512, score, (jnp.full((1, 256), MASK_VALUE, F32),) * 2, unroll=2)

    og[...] = jnp.zeros_like(og)

    def mix(c, totals):
        rows = pl.ds(pl.multiple_of(c * 512, 512), 512)
        out = []
        for g in range(2):
            e = jnp.exp(sg[g, rows, :] - peaks[g])
            out.append(totals[g] + jnp.sum(e, axis=0, keepdims=True))
            og[g] += dot_nn(vt[:, rows], e.astype(LOW))
        return tuple(out)

    totals = lax.fori_loop(0, length // 512, mix, (jnp.zeros((1, 256), F32),) * 2, unroll=2)
    for g in range(2):
        ctx_o[g * 64 : g * 64 + 64, :] = pick_turned(og[g] * (1.0 / totals[g])).astype(LOW)
        lse_o[g : g + 1, :] = peaks[g] + jnp.log(totals[g])
    for copy in copies:
        copy.wait()


def vmem():
    return pl.BlockSpec(memory_space=pltpu.VMEM)


def smem():
    return pl.BlockSpec(memory_space=pltpu.SMEM)


def forward_attention(scal, drawn, table, x, w, w_kt, w_vt, shift, shift_vt):
    length = x.shape[0]
    blocks = length // BLOCK
    rows = jax.ShapeDtypeStruct((length, 256), LOW)
    return pl.pallas_call(
        forward_kernel,
        out_shape=(
            rows, rows, rows, jax.ShapeDtypeStruct((256, length), LOW), rows, jax.ShapeDtypeStruct((blocks, 256), F32),
        ),
        in_specs=[smem(), smem()] + [vmem()] * 7,
        out_specs=[pl.BlockSpec(memory_space=pl.ANY)] * 4 + [vmem()] * 2,
        scratch_shapes=[
            pltpu.VMEM((256, 256), LOW),
            pltpu.VMEM((length, 256), LOW),
            pltpu.VMEM((length, 256), LOW),
            pltpu.VMEM((length, 256), LOW),
            pltpu.VMEM((256, length), LOW),
            pltpu.VMEM((256, length), LOW),
            pltpu.VMEM((blocks, 256, HALF), LOW),
            pltpu.VMEM((2, length, 256), F32),
            pltpu.VMEM((2, 256, 256), F32),
            pltpu.SemaphoreType.DMA((4,)),
        ],
        compiler_params=pltpu.CompilerParams(vmem_limit_bytes=VMEM_LIMIT),
        cost_estimate=pl.CostEstimate(flops=16_000_000_000, bytes_accessed=12_000_000, transcendentals=10_000_000),
        name="attend_forward",
    )(scal, drawn, table, x, w, w_kt, w_vt, shift, shift_vt)


def normalize(summed):
    center = summed - jnp.mean(summed, axis=-1, keepdims=True)
    return (*scaled(center), center)


def scaled(center):
    factor = lax.rsqrt(jnp.mean(center * center, axis=-1, keepdims=True) + NORM_EPSILON)
    return (center * factor, factor)


def normalize_back(grad_normed, normed, factor):
    return factor * (
        grad_normed
        - jnp.mean(grad_normed, axis=-1, keepdims=True)
        - normed * jnp.mean(grad_normed * normed, axis=-1, keepdims=True)
    )


ROOT_HALF = 0.7071067811865476


def gelu_weight(v):
    return 0.5 * (1.0 + lax.erf(v * ROOT_HALF))


def open_rows(table, scal, rows):
    last = scal[0] - 1
    marks = []
    for n in range(rows // BLOCK):
        b = pl.program_id(0) * (rows // BLOCK) + n
        one = table[(b >= last).astype(jnp.int32) + (b > last).astype(jnp.int32)]
        marks.append(jnp.concatenate([one, one], axis=1))
    return jnp.concatenate(marks, axis=0) == 0.0


def ahead_kernel(scal, table, x, ctx, w_out, w_up, w_down, up_shift, vec, out_o, one_o, two_o, act, slope_o):
    rows = x.shape[0]

    def row(n):
        return vec[n : n + 1, :]

    attended = dot_nn(ctx[...], w_out[...]) + row(2)
    normed_one, _, center = normalize(x[...].astype(F32) + attended)
    one_o[...] = center.astype(LOW)
    first_out = normed_one * row(3) + row(4)
    first_low = first_out.astype(LOW)
    for c in range(0, 1024, 256):
        pre = dot_nn(first_low, w_up[:, c : c + 256]) + up_shift[:, c : c + 256]
        weight = gelu_weight(pre)
        act[:, c : c + 256] = (pre * weight).astype(LOW)
        slope_o[:, c : c + 256] = (weight + pre * (NORMAL_PEAK * jnp.exp(-0.5 * pre * pre))).astype(LOW)
    branch = dot_nn(act[...], w_down[...]) + row(5)
    normed_two, _, center = normalize(first_out + branch)
    two_o[...] = center.astype(LOW)
    out_o[...] = jnp.where(open_rows(table, scal, rows), normed_two * row(6) + row(7), 0.0).astype(LOW)


def ahead(scal, table, x, ctx, w_out, w_up, w_down, up_shift, vec):
    length = x.shape[0]
    rows = AHEAD_ROWS

    def wide(columns):
        return pl.BlockSpec((rows, columns), lambda i, s: (i, 0))

    def whole(*shape):
        return pl.BlockSpec(shape, lambda i, s: (0,) * len(shape))

    shape = jax.ShapeDtypeStruct
    return pl.pallas_call(
        ahead_kernel,
        grid_spec=pltpu.PrefetchScalarGridSpec(
            num_scalar_prefetch=1,
            grid=(length // rows,),
            in_specs=[
                whole(3, 64, 128), wide(256), wide(256), whole(256, 256), whole(256, 1024), whole(1024, 256),
                whole(1, 1024), whole(8, 256),
            ],
            out_specs=[wide(256), wide(256), wide(256), wide(1024), wide(1024)],
        ),
        out_shape=(
            shape((length, 256), LOW), shape((length, 256), LOW), shape((length, 256), LOW),
            shape((length, 1024), LOW), shape((length, 1024), LOW),
        ),
        compiler_params=pltpu.CompilerParams(vmem_limit_bytes=VMEM_LIMIT),
        cost_estimate=pl.CostEstimate(flops=5_000_000_000, bytes_accessed=34_000_000, transcendentals=10_000_000),
        name="ahead",
    )(scal, table, x, ctx, w_out, w_up, w_down, up_shift, vec)


def behind_kernel(
    scal, table, cot, ctx, one, two, act, slope, w_out, w_up, w_down, vec,
    gz1_o, gctx_o, delta_o, pack0, pack1, pack2, pack3, gdown_o, gup_o, gout_o, gub_o, gvec_o, back,
):
    step = pl.program_id(0)
    rows = cot.shape[0]

    @pl.when(step == 0)
    def _():
        for ref in (gdown_o, gup_o, gout_o, gub_o, gvec_o):
            ref[...] = jnp.zeros_like(ref)

    def row(n):
        return vec[n : n + 1, :]

    normed_one, factor_one = scaled(one[...].astype(F32))
    normed_two, factor_two = scaled(two[...].astype(F32))
    first_low = (normed_one * row(3) + row(4)).astype(LOW)
    grad_y = jnp.where(open_rows(table, scal, rows), cot[...].astype(F32), 0.0)
    grad_z2 = normalize_back(grad_y * row(6), normed_two, factor_two)
    grad_branch = grad_z2.astype(LOW)
    for c in range(0, 1024, 256):
        grad_act = dot_nt(grad_branch, w_down[c : c + 256, :])
        grad_pre = (grad_act * slope[:, c : c + 256].astype(F32)).astype(LOW)
        back[:, c : c + 256] = grad_pre
        gub_o[:, c : c + 256] += jnp.sum(grad_pre.astype(F32), axis=0, keepdims=True)
    gdown_o[...] += dot_tn(act[...], grad_branch)
    grad_first = grad_z2 + dot_nt(back[...], w_up[...])
    gup_o[...] += dot_tn(first_low, back[...])
    grad_z1 = normalize_back(grad_first * row(3), normed_one, factor_one)
    grad_attended = grad_z1.astype(LOW)
    gz1_o[...] = grad_attended
    ctx_v = ctx[...]
    gout_o[...] += dot_tn(ctx_v, grad_attended)
    grad_context = dot_nt(grad_attended, w_out[...]).astype(LOW)
    gctx_o[...] = grad_context

    def add(n, values):
        gvec_o[n : n + 1, :] += jnp.sum(values, axis=0, keepdims=True)

    add(2, grad_attended.astype(F32))
    add(3, grad_first * normed_one)
    add(4, grad_first)
    add(5, grad_branch.astype(F32))
    add(6, grad_y * normed_two)
    add(7, grad_y)
    both = ctx_v.astype(F32) * grad_context.astype(F32)
    upper = both.astype(LOW)
    lower = (both - upper.astype(F32)).astype(LOW)
    group = lax.broadcasted_iota(jnp.int32, (8, 256), 1) // BLOCK
    ones = jnp.where(group == lax.broadcasted_iota(jnp.int32, (8, 256), 0), 1.0, 0.0).astype(LOW)
    sums = dot_nt(ones, upper) + dot_nt(ones, lower)
    for n in range(rows // BLOCK):
        part = sums[0:4, n * BLOCK : (n + 1) * BLOCK]
        delta_o[n : n + 1, :] = jnp.concatenate([part[h : h + 1, :] for h in range(4)], axis=1)

    @pl.when(step == pl.num_programs(0) - 1)
    def _():
        for r, pack in enumerate((pack0, pack1, pack2, pack3)):
            piece = scal[1] ^ r
            shard, core = piece // 2, piece % 2
            here = pl.ds(pl.multiple_of(piece * 64, 64), 64)
            pack[:, 0:1024] = gup_o[here, :].astype(LOW)
            pack[:, 1024:1280] = gout_o[here, :].astype(LOW)
            for g in range(4):
                at = pl.ds(pl.multiple_of(shard * 512 + g * 128 + core * 64, 64), 64)
                pack[:, 1280 + 256 * g : 1536 + 256 * g] = gdown_o[at, :].astype(LOW)
            lines = [gub_o[:, pl.ds(pl.multiple_of(shard * 512 + 128 * n, 128), 128)] for n in range(4)]
            first = shard == 0
            for n in range(4):
                line = jnp.where(first, gvec_o[n : n + 1, :], gvec_o[4 + n : 5 + n, :])
                lines += [line[:, 0:128], line[:, 128:256]]
            put_extra(pack, 2304, lines, core)


def put_extra(pack, at, lines, core):
    some = jnp.concatenate(lines + [jnp.zeros((16 - len(lines), HALF), F32)], axis=0)
    pack[0:16, at : at + HALF] = jnp.where(core == 0, some, 0.0).astype(LOW)
    pack[16:64, at : at + HALF] = jnp.zeros((48, HALF), LOW)


def behind(scal, table, cot, ctx, one, two, act, slope, w_out, w_up, w_down, vec):
    length = cot.shape[0]
    rows = BEHIND_ROWS

    def wide(columns):
        return pl.BlockSpec((rows, columns), lambda i, s: (i, 0))

    def whole(*shape):
        return pl.BlockSpec(shape, lambda i, s: (0,) * len(shape))

    shape = jax.ShapeDtypeStruct
    return pl.pallas_call(
        behind_kernel,
        grid_spec=pltpu.PrefetchScalarGridSpec(
            num_scalar_prefetch=1,
            grid=(length // rows,),
            in_specs=[
                whole(3, 64, 128), wide(256), wide(256), wide(256), wide(256), wide(1024), wide(1024),
                whole(256, 256), whole(256, 1024), whole(1024, 256), whole(8, 256),
            ],
            out_specs=[
                wide(256), wide(256), pl.BlockSpec((rows // BLOCK, 256), lambda i, s: (i, 0)),
                whole(64, 2432), whole(64, 2432), whole(64, 2432), whole(64, 2432),
            ],
            scratch_shapes=[
                pltpu.VMEM((1024, 256), F32), pltpu.VMEM((256, 1024), F32), pltpu.VMEM((256, 256), F32),
                pltpu.VMEM((1, 1024), F32), pltpu.VMEM((8, 256), F32), pltpu.VMEM((rows, 1024), LOW),
            ],
        ),
        out_shape=(
            shape((length, 256), LOW), shape((length, 256), LOW), shape((length // BLOCK, 256), F32),
        ) + (shape((64, 2432), LOW),) * 4,
        compiler_params=pltpu.CompilerParams(vmem_limit_bytes=VMEM_LIMIT),
        cost_estimate=pl.CostEstimate(flops=10_000_000_000, bytes_accessed=40_000_000, transcendentals=0),
        name="behind",
    )(scal, table, cot, ctx, one, two, act, slope, w_out, w_up, w_down, vec)


def backward_kernel(
    scal, drawn, table, q, k, v, kt, gctx, lse, delta, gz1, x, w,
    gin_o, pack0, pack1, pack2, pack3, picks, turned, dqg, dq, dk, dv, gw_o, gz1_v, x_v, gin_v, sems,
):
    length = x.shape[0]
    blocks = length // BLOCK
    live = scal[0]
    picks[...] = head_picks()
    dk[...] = jnp.zeros_like(dk)
    dv[...] = jnp.zeros_like(dv)
    loads = [pltpu.make_async_copy(gz1, gz1_v, sems.at[0]), pltpu.make_async_copy(x, x_v, sems.at[1])]
    for load in loads:
        load.start()
    turn_pairs(kt, turned)

    def spread(i):
        rows = pl.ds(pl.multiple_of(i * BLOCK, BLOCK), BLOCK)
        bdq = spread_heads(q[rows, :] * jnp.asarray(QUERY_SCALE, LOW), picks[...])
        bdo = spread_heads(gctx[rows, :], picks[...])
        return rows, bdq, bdo

    def group(idx):
        units = [Unit(i, live, drawn, blocks) for i in idx]
        spreads = [spread(i) for i in idx]
        low = first_half(BLOCK)
        s, g, p, ds, dvs, dks, dqs = {}, {}, {}, {}, {}, {}, {}
        count = len(idx)
        for t in range(count + 1):
            u = t - 0
            if 0 <= u < count:
                s[u] = dot_nt(slot_rows(units[u], k), spreads[u][1])
            u = t - 0
            if 0 <= u < count:
                g[u] = dot_nt(slot_rows(units[u], v), spreads[u][2])
            u = t - 0
            if 0 <= u < count:
                e = jnp.exp(masked(s[u], units[u].bias(table, range(2, 8))) - lse[pl.ds(idx[u], 1), :])
                ds[u] = (e * (g[u] - delta[pl.ds(idx[u], 1), :])).astype(LOW)
                p[u] = e.astype(LOW)
            u = t - 0
            if 0 <= u < count:
                dvs[u] = dot_nn(p[u], spreads[u][2])
                dks[u] = dot_nn(ds[u], spreads[u][1])
                dqs[u] = dot_nn(slot_turned(units[u], kt[:, 0:128], turned), ds[u])
            u = t - 1
            if 0 <= u < count:
                for acc, terms_ in ((dk, dks[u]), (dv, dvs[u])):
                    acc[0:128, :] += terms_[0:128, :]
                    for n in range(2, 8):
                        one = terms_[n * 64 : n * 64 + 64, :]
                        if n < 5:
                            at = pl.ds(pl.multiple_of(units[u].near[n - 2] * BLOCK, BLOCK), BLOCK)
                            acc[at, :] += one
                        else:
                            for h in range(4):
                                t_ = h // 2
                                at = pl.ds(pl.multiple_of(units[u].chosen[n - 5][h] * BLOCK, BLOCK), BLOCK)
                                cols = pl.ds(t_ * HALF, HALF)
                                mine = low if h % 2 == 0 else jnp.logical_not(low)
                                acc[at, cols] += jnp.where(mine, one[:, t_ * HALF : t_ * HALF + HALF], 0.0)
                dq[spreads[u][0], :] = (pick_turned(dqs[u]) * QUERY_SCALE).astype(LOW)

    def several(j, _):
        group([2 + BACK * j + u for u in range(BACK)])
        return 0

    lax.fori_loop(0, (blocks - 2) // BACK, several, 0)
    if (blocks - 2) % BACK:
        group([live * 0 + i for i in range(blocks - (blocks - 2) % BACK, blocks)])

    spreads = [spread(g)[1:] for g in range(2)]
    dqg[...] = jnp.zeros_like(dqg)

    def chunk(c, _):
        at = pl.ds(pl.multiple_of(c * 512, 512), 512)
        bias = chunk_bias(table, live, c * 8, 8)
        kh, vh, th = k[at, :], v[at, :], kt[:, at]
        two = range(2)
        s = [dot_nt(kh, spreads[g][0]) for g in two]
        t = [dot_nt(vh, spreads[g][1]) for g in two]
        p = [jnp.exp(s[g] + bias - lse[g : g + 1, :]) for g in two]
        ds = [(p[g] * (t[g] - delta[g : g + 1, :])).astype(LOW) for g in two]
        dvs = [dot_nn(p[g].astype(LOW), spreads[g][1]) for g in two]
        dks = [dot_nn(ds[g], spreads[g][0]) for g in two]
        for g in two:
            dqg[g] += dot_nn(th, ds[g])
        dv[at, :] += dvs[0] + dvs[1]
        dk[at, :] += dks[0] + dks[1]
        return 0

    lax.fori_loop(0, length // 512, chunk, 0, unroll=2)
    for g in range(2):
        dq[g * 64 : g * 64 + 64, :] = (pick_turned(dqg[g]) * QUERY_SCALE).astype(LOW)

    gw_o[...] = jnp.zeros_like(gw_o)
    for load in loads:
        load.wait()

    def finish(c, shifts):
        rows = pl.ds(pl.multiple_of(c * 512, 512), 512)
        dqkv = jnp.concatenate([dq[rows, :], dk[rows, :].astype(LOW), dv[rows, :].astype(LOW)], axis=1)
        gin_v[rows, :] = (gz1_v[rows, :].astype(F32) + dot_nt(dqkv, w[...])).astype(LOW)
        gw_o[...] += dot_tn(x_v[rows, :], dqkv)
        return shifts + jnp.sum(dqkv.astype(F32), axis=0, keepdims=True)

    shifts = lax.fori_loop(0, length // 512, finish, jnp.zeros((1, 768), F32), unroll=2)
    store = pltpu.make_async_copy(gin_v, gin_o, sems.at[2])
    store.start()
    for r, pack in enumerate((pack0, pack1, pack2, pack3)):
        piece = scal[1] ^ r
        core = piece % 2
        pack[:, 0:768] = gw_o[pl.ds(pl.multiple_of(piece * 64, 64), 64), :].astype(LOW)
        mine = jnp.where(piece // 2 == 0, shifts, 0.0)
        lines = [jnp.zeros((4, HALF), F32)] + [mine[:, a : a + HALF] for a in (0, 128, 512, 640)]
        lines += [jnp.zeros((8, HALF), F32)]
        pack[:, 768:896] = jnp.zeros((64, HALF), LOW)
        pack[0:16, 768:896] = jnp.where(core == 0, jnp.concatenate(lines, axis=0), 0.0).astype(LOW)
    store.wait()


def backward_attention(scal, drawn, table, q, k, v, kt, gctx, lse, delta, gz1, x, w):
    length = x.shape[0]
    shape = jax.ShapeDtypeStruct
    return pl.pallas_call(
        backward_kernel,
        out_shape=(shape((length, 256), LOW),) + (shape((64, 896), LOW),) * 4,
        in_specs=[smem(), smem()] + [vmem()] * 8 + [pl.BlockSpec(memory_space=pl.ANY)] * 2 + [vmem()],
        out_specs=[pl.BlockSpec(memory_space=pl.ANY)] + [vmem()] * 4,
        scratch_shapes=[
            pltpu.VMEM((256, 256), LOW),
            pltpu.VMEM((length // BLOCK, 256, HALF), LOW),
            pltpu.VMEM((2, 256, 256), F32),
            pltpu.VMEM((length, 256), LOW),
            pltpu.VMEM((length, 256), F32),
            pltpu.VMEM((length, 256), F32),
            pltpu.VMEM((256, 768), F32),
            pltpu.VMEM((length, 256), LOW),
            pltpu.VMEM((length, 256), LOW),
            pltpu.VMEM((length, 256), LOW),
            pltpu.SemaphoreType.DMA((3,)),
        ],
        compiler_params=pltpu.CompilerParams(vmem_limit_bytes=VMEM_LIMIT),
        cost_estimate=pl.CostEstimate(flops=40_000_000_000, bytes_accessed=20_000_000, transcendentals=10_000_000),
        name="attend_backward",
    )(scal, drawn, table, q, k, v, kt, gctx, lse, delta, gz1, x, w)


def bias_table(tail):
    column = jnp.stack([jnp.zeros_like(tail, F32), jnp.where(tail == 1, 0.0, MASK_VALUE), jnp.full(tail.shape, MASK_VALUE, F32)])
    return jnp.broadcast_to(column[:, :, None], (3, BLOCK, HALF))


def reorder_kernel(scatter, where, assign, src, *rest):
    *_, dst, held, arrived, left = rest
    count = src.shape[0]
    shards = assign.shape[0] // count
    loads, stores = [], []
    for j in range(count):
        one = assign[shards * j + where[0]]
        loads.append(pltpu.make_async_copy(src.at[j if scatter else one], held.at[j], arrived.at[j]))
        stores.append(pltpu.make_async_copy(held.at[j], dst.at[one if scatter else j], left.at[j]))
        loads[-1].start()
    for load, store in zip(loads, stores):
        load.wait()
        store.start()
    for store in stores:
        store.wait()


def reorder(shard, assign, src, scatter, after=()):
    return pl.pallas_call(
        functools.partial(reorder_kernel, scatter),
        out_shape=jax.ShapeDtypeStruct(src.shape, src.dtype),
        in_specs=[smem(), smem(), pl.BlockSpec(memory_space=pltpu.HBM)]
        + [pl.BlockSpec(memory_space=pltpu.HBM)] * len(after),
        out_specs=pl.BlockSpec(memory_space=pltpu.HBM),
        scratch_shapes=[
            pltpu.VMEM(src.shape, src.dtype),
            pltpu.SemaphoreType.DMA((src.shape[0],)),
            pltpu.SemaphoreType.DMA((src.shape[0],)),
        ],
        compiler_params=pltpu.CompilerParams(vmem_limit_bytes=VMEM_LIMIT),
        cost_estimate=pl.CostEstimate(flops=0, bytes_accessed=4 * src.size, transcendentals=0),
        name="reorder",
    )(shard, assign, src, *after)


def hold(values, after):
    count = len(values)
    anywhere = pl.BlockSpec(memory_space=pltpu.HBM)
    return pl.pallas_call(
        lambda *refs: None,
        out_shape=tuple(jax.ShapeDtypeStruct(v.shape, v.dtype) for v in values),
        in_specs=[anywhere] * (count + len(after)),
        out_specs=(anywhere,) * count,
        input_output_aliases={n: n for n in range(count)},
        name="hold",
    )(*values, *after)


def pack_kernel(w_qkv, w_out, w_up, w_down, up_bias, vectors, after, out):
    rows = w_qkv.shape[0]
    out[0:rows, 0:768] = w_qkv[...]
    out[0:rows, 768:1024] = w_out[...]
    out[0:rows, 1024:2048] = w_up[...]
    for n in range(4):
        out[0:rows, 2048 + 256 * n : 2304 + 256 * n] = w_down[rows * n : rows * (n + 1), :]
    lines = [up_bias[...].astype(F32)] + [vectors[n : n + 1, :].astype(F32) for n in range(4)]
    line = jnp.concatenate(lines + [jnp.zeros((1, 3072 - 1536), F32)], axis=1)
    out[rows : rows + 16, :] = jnp.broadcast_to(line, (16, 3072)).astype(LOW)


def pack_weights(parts, after):
    w_qkv, w_out, w_up, w_down, up_bias, vectors = parts
    return pl.pallas_call(
        pack_kernel,
        out_shape=jax.ShapeDtypeStruct((w_qkv.shape[0] + 16, 3072), LOW),
        in_specs=[vmem()] * 6 + [pl.BlockSpec(memory_space=pltpu.HBM)],
        out_specs=vmem(),
        compiler_params=pltpu.CompilerParams(vmem_limit_bytes=VMEM_LIMIT),
        name="pack_weights",
    )(w_qkv, w_out, w_up, w_down, up_bias.reshape(1, -1), vectors, after)


def unpack_kernel(shard, own, got, w_qkv, w_out, w_up, w_down, w_kt, w_vt, up_shift, vec, shift, shift_vt):
    rows = own.shape[0] - 16
    first = shard[0] == 0

    def half(n, at, cols):
        mine, other = own[at, cols], got[at, cols]
        return jnp.where(first == (n == 0), mine, other)

    for n in range(2):
        here = slice(n * rows, (n + 1) * rows)
        w_qkv[here, :] = half(n, slice(0, rows), slice(0, 768))
        w_out[here, :] = half(n, slice(0, rows), slice(768, 1024))
        w_up[here, :] = half(n, slice(0, rows), slice(1024, 2048))
        for g in range(4):
            at = (4 * n + g) * rows
            w_down[at : at + rows, :] = half(n, slice(0, rows), slice(2048 + 256 * g, 2304 + 256 * g))
        line = half(n, slice(rows, rows + 16), slice(0, 1536)).astype(F32)[0:1]
        up_shift[:, 512 * n : 512 * n + 512] = line[:, 0:512]
        for g in range(4):
            vec[4 * n + g : 4 * n + g + 1, :] = line[:, 512 + 256 * g : 768 + 256 * g]
    shift[...] = jnp.concatenate([vec[0:1, :], jnp.zeros((1, 256), F32), vec[1:2, :]], axis=1)
    w_kt[...] = w_qkv[:, 256:512].astype(F32).T.astype(LOW)
    w_vt[...] = w_qkv[:, 512:768].astype(F32).T.astype(LOW)
    shift_vt[...] = jnp.broadcast_to(vec[1:2, :], (HALF, 256)).T


def unpack_weights(shard, own, got):
    shape = jax.ShapeDtypeStruct
    return pl.pallas_call(
        unpack_kernel,
        out_shape=(
            shape((256, 768), LOW), shape((256, 256), LOW), shape((256, 1024), LOW), shape((1024, 256), LOW),
            shape((256, 256), LOW), shape((256, 256), LOW), shape((1, 1024), F32), shape((8, 256), F32),
            shape((1, 768), F32), shape((256, HALF), F32),
        ),
        in_specs=[smem(), vmem(), vmem()],
        out_specs=[vmem()] * 10,
        compiler_params=pltpu.CompilerParams(vmem_limit_bytes=VMEM_LIMIT),
        name="unpack_weights",
    )(shard, own, got)


def trade(pieces):
    count = lax.axis_size("dp")
    held = [pieces[0]]
    for n in (1, 2, 3):
        pairs = [(d * 2 + s, (d ^ (n % 2)) * 2 + (s ^ (n // 2))) for d in range(count) for s in range(2)]
        held.append(lax.ppermute(pieces[n], ("dp", "shard"), pairs))
    return held


def total(pieces):
    return sum(piece.astype(F32) for piece in pieces)


def sum_rest(part, data_index, meanwhile):
    count = lax.axis_size("dp")
    groups = count // 4
    half = part.shape[0] // 2
    bit = (data_index // 2) % 2
    flip = [(d, d ^ 2) for d in range(count)]
    keep = lax.dynamic_slice_in_dim(part, bit * half, half, 0)
    give = lax.dynamic_slice_in_dim(part, (1 - bit) * half, half, 0)
    part = keep + lax.ppermute(give.astype(LOW), "dp", flip).astype(F32)
    at = data_index // 4
    small = half // groups
    hops = [[(d, (d + 4 * k) % count) for d in range(count)] for k in range(1, groups)]

    def piece(k):
        return lax.dynamic_slice_in_dim(part, lax.rem(at + k, groups) * small, small, 0)

    other = meanwhile(part)
    mine = hold((piece(0),), (other,))[0]
    got = [lax.ppermute(piece(k + 1).astype(LOW), "dp", hop) for k, hop in enumerate(hops)]
    for one in got:
        mine = mine + one.astype(F32)
    return mine.astype(LOW), other


def spread_sums(mine, meanwhile):
    count = lax.axis_size("dp")
    flip = [(d, d ^ 2) for d in range(count)]
    hops = [[(d, (d + 4 * k) % count) for d in range(count)] for k in range(1, count // 4)]
    near = jnp.stack([mine] + [lax.ppermute(mine, "dp", hop) for hop in hops])
    core = [(d, d ^ 1) for d in range(count)]
    other = meanwhile(near)
    across = hold((lax.ppermute(near, "dp", flip),), (other,))[0]
    return (near, across, lax.ppermute(near, "dp", core), lax.ppermute(across, "dp", core)), other


def adam_update(grad, state, decay):
    correct_one = 1.0 - FIRST_BETA**STEP
    correct_two = 1.0 - SECOND_BETA**STEP
    first_new = FIRST_BETA * state[1] + (1.0 - FIRST_BETA) * grad
    second_new = SECOND_BETA * state[2] + (1.0 - SECOND_BETA) * grad * grad
    direction = first_new / correct_one / (jnp.sqrt(second_new / correct_two) + ADAM_EPSILON)
    master_new = state[0] - LEARNING_RATE * (direction + decay * state[0])
    return (master_new, first_new, second_new)


def update_kernel(
    where, near, across, near_core, across_core, s_qkv, s_out, s_up, s_down, s_bias, s_vec,
    g_qkv, g_out, g_up, g_down, g_bias, g_vec, o_master, o_first, o_second, grads, flat, sems,
):
    groups, small = near.shape[:2]
    parts = (near, across, near_core, across_core)
    index = where[0]
    for core in range(2):
        for side in range(2):
            base = ((index % 2) ^ core) * 64 + (((index // 2) % 2) ^ side) * 32
            for k in range(groups):
                at = base + lax.rem(index // 4 + groups - k, groups) * small
                grads[pl.ds(pl.multiple_of(at, small), small), :] = parts[2 * core + side][k].astype(F32)
    copies = []

    def send(here, there):
        copies.append(pltpu.make_async_copy(here, there, sems.at[len(copies)]))
        copies[-1].start()

    send(grads.at[:, 2304:3072], g_qkv)
    send(grads.at[:, 1024:1280], g_out)
    send(grads.at[:, 0:1024], g_up)
    for n in range(4):
        send(grads.at[:, 1280 + 256 * n : 1536 + 256 * n], g_down.at[pl.ds(128 * n, 128), :])
    outs = (o_master, o_first, o_second)

    def place(base, grad, state, decay):
        rows, columns = grad.shape
        wide = columns // HALF
        for n, value in enumerate(adam_update(grad, state, decay)):
            for c in range(wide):
                at = pl.ds(base + c, rows, stride=wide) if wide > 1 else pl.ds(base, rows)
                flat[n, at, :] = value[:, c * HALF : (c + 1) * HALF]

    def ship(base, count):
        for n, there in enumerate(outs):
            send(flat.at[n, pl.ds(base, count), :], there.reshape(flat.shape[1:]).at[pl.ds(base, count), :])

    place(1024, grads[:, 0:1024], s_up, WEIGHT_DECAY)
    ship(1024, 1024)
    for n in range(4):
        rows = slice(128 * n, 128 * n + 128)
        place(2048 + 256 * n, grads[:, 1280 + 256 * n : 1536 + 256 * n], s_down[:, rows, :], WEIGHT_DECAY)
    ship(2048, 1024)
    place(0, grads[:, 2304:3072], s_qkv, WEIGHT_DECAY)
    ship(0, 768)
    place(768, grads[:, 1024:1280], s_out, WEIGHT_DECAY)
    ship(768, 256)
    extra = grads[0:16, 3072:3200]
    g_bias[...] = extra[0:4]
    bias = [
        jnp.concatenate([s_bias[n : n + 1, c * HALF : (c + 1) * HALF] for c in range(4)], axis=0) for n in range(3)
    ]
    place(3072, extra[0:4], bias, 0.0)
    vec = jnp.concatenate(
        [jnp.concatenate([extra[4 + 2 * n : 5 + 2 * n], extra[5 + 2 * n : 6 + 2 * n]], axis=1) for n in range(4)], axis=0
    )
    g_vec[...] = vec
    place(3076, vec, s_vec, 0.0)
    ship(3072, 12)
    for copy in copies:
        copy.wait()


def update(data_index, parts, states):
    shape = lambda *dims: jax.ShapeDtypeStruct(dims, F32)
    s_qkv, s_out, s_up, s_down, s_bias, s_vec = states
    flat = shape(1, 3084 * HALF)
    away = pl.BlockSpec(memory_space=pltpu.HBM)
    *grads, master, first, second = pl.pallas_call(
        update_kernel,
        out_shape=(
            shape(128, 768), shape(128, 256), shape(128, 1024), shape(512, 256), shape(4, HALF), shape(4, 256),
            flat, flat, flat,
        ),
        in_specs=[smem()] + [vmem()] * 10,
        out_specs=[away] * 4 + [vmem()] * 2 + [away] * 3,
        scratch_shapes=[
            pltpu.VMEM((128, 3200), F32), pltpu.VMEM((3, 3084, HALF), F32), pltpu.SemaphoreType.DMA((22,)),
        ],
        compiler_params=pltpu.CompilerParams(vmem_limit_bytes=VMEM_LIMIT),
        cost_estimate=pl.CostEstimate(flops=10_000_000, bytes_accessed=14_000_000, transcendentals=400_000),
        name="update",
    )(data_index.reshape(1), *parts, s_qkv, s_out, s_up, s_down, s_bias, s_vec)
    grads[4] = grads[4].reshape(-1)
    return tuple(grads) + (master, first, second)


def on_device(
    hidden, cotangent, assign, live_blocks, tail_live, random_blocks, w_qkv, w_out, w_up, w_down, up_bias, vectors,
    state_qkv, state_out, state_up, state_down, state_ubias, state_vec,
):
    shard_count = lax.axis_size("shard")
    shard_index = lax.axis_index("shard")
    data_index = lax.axis_index("dp")
    row_seqs, rows_here, width = hidden.shape
    length = row_seqs * rows_here
    shard = shard_index.reshape(1)

    def to_slot(rows):
        return lax.all_to_all(rows, "dp", split_axis=0, concat_axis=0, tiled=True).reshape(length, width)

    sent = reorder(shard, assign, hidden, False)
    x = to_slot(sent)
    pack = pack_weights((w_qkv, w_out, w_up, w_down, up_bias, vectors), sent)
    got = lax.ppermute(pack, "shard", [(0, 1), (1, 0)])
    w_qkv, w_out, w_up, w_down, w_kt, w_vt, up_shift, vec, shift, shift_vt = unpack_weights(shard, pack, got)
    slot = assign[data_index * shard_count + shard_index]
    own = shard_index * row_seqs + slot
    scal = jnp.stack([live_blocks[own], 2 * shard_index + data_index % 2])
    table = bias_table(lax.dynamic_index_in_dim(tail_live, own, 0, keepdims=False))
    drawn = random_blocks.reshape(-1)
    ready = (w_qkv, scal, table, drawn)
    cot = to_slot(reorder(shard, assign, cotangent, False, ready))
    q, k, v, kt, ctx, lse = forward_attention(scal, drawn, table, x, w_qkv, w_kt, w_vt, shift, shift_vt)
    out, *kept = ahead(scal, table, x, ctx, w_out, w_up, w_down, up_shift, vec)

    def from_slot(rows):
        return lax.all_to_all(
            rows.reshape(row_seqs, rows_here, width), "dp", split_axis=0, concat_axis=0, tiled=True
        )

    back_out = from_slot(out)
    gz1, gctx, delta, *early = behind(scal, table, cot, ctx, *kept, w_out, w_up, w_down, vec)
    early = trade(early)
    gin, *late = backward_attention(scal, drawn, table, q, k, v, kt, gctx, lse, delta, gz1, x, w_qkv)
    gin, *late = hold((gin, *late), (back_out, *early[1:]))
    back_gin = from_slot(gin)

    def sum_all(early, late, back_out):
        early, late = total(early), total(trade(late))
        sums = jnp.concatenate([early[:, :2304], late[:, :768], early[:, 2304:] + late[:, 768:]], axis=1)
        return sum_rest(sums, data_index, lambda part: reorder(shard, assign, back_out, True, (part,)))

    made = jax.eval_shape(sum_all, early, late, back_out)
    mine, layer_out = lax.cond(
        live_blocks[0] > 0,
        sum_all,
        lambda *unused: jax.tree.map(lambda one: jnp.zeros(one.shape, one.dtype), made),
        early, late, back_out,
    )
    parts, input_grad = spread_sums(mine, lambda near: reorder(shard, assign, back_gin, True, (near,)))
    states = (state_qkv, state_out, state_up, state_down, state_ubias, state_vec)
    updated = update(data_index, parts, states)
    return (layer_out, input_grad) + updated


def solution(mesh):
    placed = (
        P("shard", "dp", None), P("shard", "dp", None), P(), P(), P(), P(("dp", "shard"), None, None, None),
        P("shard", None), P("shard", None), P("shard", None), P("shard", None), P("shard"), P("shard", None),
        P(None, "shard", None), P(None, "shard", None), P(None, "shard", None), P(None, "shard", None),
        P(None, "shard"), P(None, "shard", None),
    )
    return jax.shard_map(
        on_device,
        mesh=mesh,
        in_specs=placed,
        out_specs=(
            P("shard", "dp", None), P("shard", "dp", None), P("shard", None), P("shard", None), P("shard", None),
            P("shard", None), P("shard"), P("shard", None), P("shard", None), P("shard", None), P("shard", None),
        ),
        check_vma=False,
    )
```
